128 devices in a mesh: batch: 8 (over y, core), seq: 16 (over x, z).
Axes of the slice: x: 4, y: 4, z: 4, core: 2. Of those that a mesh axis runs over, the one named last changes fastest.
Arguments:
- feats: bfloat16 [16, 1024, 512], P('batch', 'seq'), may hold values from -6 to 6
- lengths: int32 [16], P('batch'), may hold values from 256 to 1024, as said below
- skip_flag: int32 [8], P('batch'), may hold values from 0 to 1, as said below
- cotangent: bfloat16 [16, 1024, 768], P('batch', 'seq'), may hold values from -6 to 6
- input_gain: bfloat16 [512], replicated, may hold values from 0.5 to 1.5
- input_shift: bfloat16 [512], replicated, may hold values from -3 to 3
- proj_weight: bfloat16 [512, 768], replicated, may hold values from -0.25 to 0.25
- proj_bias: bfloat16 [768], replicated, may hold values from -3 to 3
- conv_weight: bfloat16 [768, 48, 128], replicated, may hold values from -0.078125 to 0.078125
- conv_bias: bfloat16 [768], replicated, may hold values from -3 to 3
- encoder_gain: bfloat16 [768], replicated, may hold values from 0.5 to 1.5
- encoder_shift: bfloat16 [768], replicated, may hold values from -3 to 3
- qkv_weight: bfloat16 [768, 2304], replicated, may hold values from -0.21875 to 0.21875
- query_bias: bfloat16 [768], replicated, may hold values from -3 to 3
- value_bias: bfloat16 [768], replicated, may hold values from -3 to 3
- output_weight: bfloat16 [768, 768], replicated, may hold values from -3.5 to 3.5
- output_bias: bfloat16 [768], replicated, may hold values from -3 to 3
- middle_gain: bfloat16 [768], replicated, may hold values from 0.5 to 1.5
- middle_shift: bfloat16 [768], replicated, may hold values from -3 to 3
- inner_weight: bfloat16 [768, 3072], replicated, may hold values from -0.21875 to 0.21875
- inner_bias: bfloat16 [3072], replicated, may hold values from -3 to 3
- outer_weight: bfloat16 [3072, 768], replicated, may hold values from -0.109375 to 0.109375
- outer_bias: bfloat16 [768], replicated, may hold values from -3 to 3
- final_gain: bfloat16 [768], replicated, may hold values from 0.5 to 1.5
- final_shift: bfloat16 [768], replicated, may hold values from -3 to 3
Outputs:
- activations: bfloat16 [16, 1024, 768], P('batch', 'seq')
- grad_feats: float32 [16, 1024, 512], P('batch', 'seq')
- grad_input_gain: float32 [512], P(('batch', 'seq'))
- grad_input_shift: float32 [512], P(('batch', 'seq'))
- grad_proj_weight: float32 [512, 768], P(('batch', 'seq'))
- grad_proj_bias: float32 [768], P(('batch', 'seq'))
- grad_conv_weight: float32 [768, 48, 128], P(('batch', 'seq'))
- grad_conv_bias: float32 [768], P(('batch', 'seq'))
- grad_encoder_gain: float32 [768], P(('batch', 'seq'))
- grad_encoder_shift: float32 [768], P(('batch', 'seq'))
- grad_qkv_weight: float32 [768, 2304], P(('batch', 'seq'))
- grad_query_bias: float32 [768], P(('batch', 'seq'))
- grad_value_bias: float32 [768], P(('batch', 'seq'))
- grad_output_weight: float32 [768, 768], P(('batch', 'seq'))
- grad_output_bias: float32 [768], P(('batch', 'seq'))
- grad_middle_gain: float32 [768], P(('batch', 'seq'))
- grad_middle_shift: float32 [768], P(('batch', 'seq'))
- grad_inner_weight: float32 [768, 3072], P(('batch', 'seq'))
- grad_inner_bias: float32 [3072], P(('batch', 'seq'))
- grad_outer_weight: float32 [3072, 768], P(('batch', 'seq'))
- grad_outer_bias: float32 [768], P(('batch', 'seq'))
- grad_final_gain: float32 [768], P(('batch', 'seq'))
- grad_final_shift: float32 [768], P(('batch', 'seq'))
The draws below stay inside these ranges and needn't reach their ends.
Inputs may be any that keep to these rules, and one draw needn't show every extreme that they name: `lengths`: in each bucket of 2 utterances one, chosen by the seed, has all 1024 frames. `skip_flag`: at least one bucket keeps the feed-forward branch and at least one drops it.
All inputs are finite; a program needn't handle non-finite values.
Results may differ from the reference program's by a relative error of at most 0.0208.
Values may be sent and summed in bfloat16 or wider, within the bound.
No kernel may reach another device: no remote copies, remote signals or barrier semaphores. Data moves between devices by JAX's collectives and lax.ppermute only.
A program may use at most 704 MiB of HBM per device.

```python
import jax
import jax.numpy as jnp
from jax import lax

D = 768
HEADS = 12
HEAD_DIM = 64
FF = 3072
C_IN = 512
GROUPS = 16
KW = 128
UTT_DEV = 2
FRAMES = 1024
UTTS = 16


def draw_lengths(key, part):
    key = jax.random.fold_in(key, 11)
    pick_key, length_key = jax.random.split(key)
    buckets = UTTS // UTT_DEV
    chosen = jax.random.randint(pick_key, (buckets,), 0, UTT_DEV)
    short_lengths = jax.random.randint(length_key, (buckets, UTT_DEV), FRAMES // 4, FRAMES + 1)
    slot_index = jnp.arange(UTT_DEV)[None, :]
    return jnp.where(slot_index == chosen[:, None], FRAMES, short_lengths).reshape(UTTS).astype(jnp.int32)


def draw_skip_flag(key, part):
    key = jax.random.fold_in(key, 23)
    flag_key, order_key = jax.random.split(key)
    buckets = UTTS // UTT_DEV
    flags = jax.random.randint(flag_key, (buckets,), 0, 2)
    order = jax.random.permutation(order_key, jnp.arange(buckets, dtype=jnp.int32))
    flags = jnp.where(order == 0, 0, flags)
    flags = jnp.where(order == 1, 1, flags)
    return flags.astype(jnp.int32)


def shard_levels(rng, dims, shards, smallest, largest):
    gain = 1.0
    for dim, shards_of in shards:
        steps = jax.random.uniform(jax.random.fold_in(jax.random.fold_in(rng, 6), dim), (shards_of,), jnp.float32, smallest / len(shards), largest / len(shards))
        gain = gain * jnp.repeat(jnp.exp(steps), dims[dim] // shards_of).reshape((-1,) + (1,) * (len(dims) - 1 - dim))
    return gain


def gaussian(key, extent, width, most, cuts=(), held_as=jnp.bfloat16):
    drawn = width * jax.random.normal(key, extent, jnp.float32)
    if cuts:
        drawn = drawn * shard_levels(key, extent, cuts, -0.22, 0.18)
    return jnp.clip(drawn, -most, most).astype(held_as)


def setup_inputs(seed: int = 0) -> dict:
    streams_of = jax.random.split(jax.random.key(seed), 26)
    feats = gaussian(streams_of[0], (UTTS, FRAMES, C_IN), 1.0, 6.0, ((0, 8), (1, 16)))
    lengths = draw_lengths(jax.random.fold_in(streams_of[25], 71), 0)
    skip_flag = draw_skip_flag(jax.random.fold_in(streams_of[25], 71), 0)
    cotangent = gaussian(streams_of[3], (UTTS, FRAMES, D), 1.0, 6.0, ((0, 8), (1, 16)))
    input_gain = jnp.clip(1.0 + 0.1 * jax.random.normal(streams_of[4], (C_IN,), jnp.float32), 0.5, 1.5).astype(jnp.bfloat16)
    input_shift = gaussian(streams_of[5], (C_IN,), 0.5, 3.0)
    proj_weight = gaussian(streams_of[6], (C_IN, D), C_IN ** -0.5, 0.25)
    proj_bias = gaussian(streams_of[7], (D,), 0.5, 3.0)
    conv_weight = gaussian(streams_of[8], (D, D // GROUPS, KW), (D // GROUPS * KW) ** -0.5, 0.078125)
    conv_bias = gaussian(streams_of[9], (D,), 0.5, 3.0)
    encoder_gain = jnp.clip(1.0 + 0.1 * jax.random.normal(streams_of[10], (D,), jnp.float32), 0.5, 1.5).astype(jnp.bfloat16)
    encoder_shift = gaussian(streams_of[11], (D,), 0.5, 3.0)
    qkv_weight = gaussian(streams_of[12], (D, 3 * D), D ** -0.5, 0.21875)
    query_bias = gaussian(streams_of[13], (D,), 0.5, 3.0)
    value_bias = gaussian(streams_of[14], (D,), 0.5, 3.0)
    output_weight = gaussian(streams_of[15], (D, D), (max(D // 256, 1)) ** -0.5, 3.5)
    output_bias = gaussian(streams_of[16], (D,), 0.5, 3.0)
    middle_gain = jnp.clip(1.0 + 0.1 * jax.random.normal(streams_of[17], (D,), jnp.float32), 0.5, 1.5).astype(jnp.bfloat16)
    middle_shift = gaussian(streams_of[18], (D,), 0.5, 3.0)
    inner_weight = gaussian(streams_of[19], (D, FF), D ** -0.5, 0.21875)
    inner_bias = gaussian(streams_of[20], (FF,), 0.5, 3.0)
    outer_weight = gaussian(streams_of[21], (FF, D), FF ** -0.5, 0.109375)
    outer_bias = gaussian(streams_of[22], (D,), 0.5, 3.0)
    final_gain = jnp.clip(1.0 + 0.1 * jax.random.normal(streams_of[23], (D,), jnp.float32), 0.5, 1.5).astype(jnp.bfloat16)
    final_shift = gaussian(streams_of[24], (D,), 0.5, 3.0)
    return dict(feats=feats, lengths=lengths, skip_flag=skip_flag, cotangent=cotangent, input_gain=input_gain, input_shift=input_shift, proj_weight=proj_weight, proj_bias=proj_bias, conv_weight=conv_weight, conv_bias=conv_bias, encoder_gain=encoder_gain, encoder_shift=encoder_shift, qkv_weight=qkv_weight, query_bias=query_bias, value_bias=value_bias, output_weight=output_weight, output_bias=output_bias, middle_gain=middle_gain, middle_shift=middle_shift, inner_weight=inner_weight, inner_bias=inner_bias, outer_weight=outer_weight, outer_bias=outer_bias, final_gain=final_gain, final_shift=final_shift)


@jax.custom_vjp
def low(v):
    return lax.optimization_barrier(v.astype(jnp.bfloat16)).astype(jnp.float32)

@jax.custom_vjp
def low_back(v):
    return v

def low_keep(v):
    return (low(v), None)

def low_pass(kept, grad):
    return (grad,)

def back_keep(v):
    return (v, None)

def back_low(kept, grad):
    return (low(grad),)
low.defvjp(low_keep, low_pass)
low_back.defvjp(back_keep, back_low)
norm_eps = 1e-05
head_scale = 0.125
neg_fill = -1e+30

def layer_norm(values, scale_vec, shift_vec):
    center = values - lax.optimization_barrier(jnp.mean(values, axis=-1, keepdims=True))
    spread = lax.optimization_barrier(jnp.mean(center * center, axis=-1, keepdims=True))
    return center * lax.rsqrt(spread + norm_eps) * scale_vec + shift_vec

def mat(left, right):
    return jnp.dot(left, right, precision=lax.Precision.HIGHEST, preferred_element_type=jnp.float32)

def gelu_exact(values):
    return jax.nn.gelu(values, approximate=False)

def group_forward(params, block_in, block_len, keep_scale):
    input_gain, input_shift, proj_weight, proj_bias, conv_weight, conv_bias, encoder_gain, encoder_shift, qkv_weight, query_bias, value_bias, output_weight, output_bias, middle_gain, middle_shift, inner_weight, inner_bias, outer_weight, outer_bias, final_gain, final_shift = params
    utts_here = block_in.shape[0]
    row_count = utts_here * FRAMES
    frame_index = jnp.arange(FRAMES, dtype=jnp.int32)
    live_grid = frame_index[None, :] < block_len[:, None]
    live_rows = live_grid.astype(jnp.float32).reshape(row_count, 1)
    normed = layer_norm(block_in.reshape(row_count, C_IN), input_gain, input_shift)
    projected = low_back(mat(low(normed), proj_weight) + proj_bias)
    masked = projected * live_rows
    conv_in = low(masked).reshape(utts_here, FRAMES, D)
    conv_out = lax.conv_general_dilated(conv_in, conv_weight, (1,), ((KW // 2, KW // 2),), dimension_numbers=('NWC', 'OIW', 'NWC'), feature_group_count=GROUPS, precision=lax.Precision.HIGHEST)
    conv_pre = low_back(conv_out[:, :FRAMES, :].reshape(row_count, D) + conv_bias)
    summed = masked + gelu_exact(conv_pre)
    hidden = layer_norm(summed, encoder_gain, encoder_shift)
    qkv_bias = jnp.concatenate([query_bias, jnp.zeros((D,), jnp.float32), value_bias])
    qkv = low(low_back(mat(low(hidden), qkv_weight) + qkv_bias))
    query_heads = qkv[:, :D].reshape(utts_here, FRAMES, HEADS, HEAD_DIM)
    key_heads = qkv[:, D:2 * D].reshape(utts_here, FRAMES, HEADS, HEAD_DIM)
    value_heads = qkv[:, 2 * D:].reshape(utts_here, FRAMES, HEADS, HEAD_DIM)
    raw = low_back(jnp.einsum('uqhd,ukhd->uhqk', query_heads, key_heads, precision=lax.Precision.HIGHEST))
    scores = jnp.where(live_grid[:, None, None, :], raw * head_scale, neg_fill)
    attn_probs = jax.nn.softmax(scores, axis=-1)
    attended = jnp.einsum('uhqk,ukhd->uqhd', low(attn_probs), value_heads, precision=lax.Precision.HIGHEST).reshape(row_count, D)
    attended = low(low_back(attended))
    attn_out = low_back(mat(attended, output_weight) + output_bias)
    middle_in = hidden + attn_out
    middle = layer_norm(middle_in, middle_gain, middle_shift)
    inner_pre = low_back(mat(low(middle), inner_weight) + inner_bias)
    inner_act = low(gelu_exact(inner_pre))
    outer_out = low_back(mat(inner_act, outer_weight) + outer_bias)
    final_in = middle + keep_scale * outer_out
    return layer_norm(final_in, final_gain, final_shift).reshape(utts_here, FRAMES, D)

def reference(feats, lengths, skip_flag, cotangent, input_gain, input_shift, proj_weight, proj_bias, conv_weight, conv_bias, encoder_gain, encoder_shift, qkv_weight, query_bias, value_bias, output_weight, output_bias, middle_gain, middle_shift, inner_weight, inner_bias, outer_weight, outer_bias, final_gain, final_shift):
    params = tuple((item.astype(jnp.float32) for item in (input_gain, input_shift, proj_weight, proj_bias, conv_weight, conv_bias, encoder_gain, encoder_shift, qkv_weight, query_bias, value_bias, output_weight, output_bias, middle_gain, middle_shift, inner_weight, inner_bias, outer_weight, outer_bias, final_gain, final_shift)))
    buckets = UTTS // UTT_DEV
    keep_scales = (1 - skip_flag.astype(jnp.int32)).astype(jnp.float32)
    inputs = feats.astype(jnp.float32)
    bucket_lengths = lengths.astype(jnp.int32).reshape(buckets, UTT_DEV)

    def forward(inputs, params):

        def step(carry, triple):
            block_in, block_len, keep_scale = triple
            return (carry, group_forward(params, block_in, block_len, keep_scale))
        _, outputs = lax.scan(jax.checkpoint(step), jnp.float32(0.0), (inputs.reshape(buckets, UTT_DEV, FRAMES, C_IN), bucket_lengths, keep_scales))
        return outputs.reshape(UTTS, FRAMES, D)
    result, pull = jax.vjp(forward, inputs, params)
    grad_in, grads = pull(cotangent.astype(jnp.float32))
    return (result.astype(jnp.bfloat16), grad_in, grads[0], grads[1], grads[2], grads[3], grads[4], grads[5], grads[6], grads[7], grads[8], grads[9], grads[10], grads[11], grads[12], grads[13], grads[14], grads[15], grads[16], grads[17], grads[18], grads[19], grads[20])
```

```python
import functools

import jax
import jax.numpy as jnp
from jax import lax
from jax.experimental import pallas as pl
from jax.experimental.pallas import tpu as pltpu
from jax.sharding import PartitionSpec as P

f32 = jnp.float32
bf16 = jnp.bfloat16
i32 = jnp.int32

norm_eps = 1e-05
head_scale = 0.125
neg_fill = -1e30

D = 768
C_IN = 512
FF = 3072
GROUPS = 16
GW = 48
KW = 128
SUPER = 16
TAP_BLOCKS = 9
ROWS = 128
SEQ = 16
PAIRS = 6
VMEM = 60 * 1024 * 1024
TRANSPOSE_SCRATCH = pltpu.VMEM((D, 128), f32)

(
    R_IN_G, R_IN_S, R_PROJ_B, R_CONV_B, R_ENC_G, R_ENC_S, R_Q_B, R_V_B, R_OUT_B, R_MID_G, R_MID_S, R_INNER_B,
    _r12, _r13, _r14, R_OUTER_B, R_FIN_G, R_FIN_S,
) = range(18)


def nn(a, b):
    return lax.dot_general(a, b, (((1,), (0,)), ((), ())), preferred_element_type=f32)


def nt(a, b):
    return lax.dot_general(a, b, (((1,), (1,)), ((), ())), preferred_element_type=f32)


def tn(a, b):
    return lax.dot_general(a, b, (((0,), (0,)), ((), ())), preferred_element_type=f32)


def iota(shape, dim):
    return lax.broadcasted_iota(i32, shape, dim)


def int_div(x, c):
    return ((x.astype(f32) + 0.5) * (1.0 / c)).astype(i32)


def stats(x):
    c = x - jnp.mean(x, axis=-1, keepdims=True)
    r = lax.rsqrt(jnp.mean(c * c, axis=-1, keepdims=True) + norm_eps)
    return c * r, r


def norm_back(xhat, r, gain, g):
    e = g * gain
    dx = r * (e - jnp.mean(e, axis=-1, keepdims=True) - xhat * jnp.mean(e * xhat, axis=-1, keepdims=True))
    return dx, jnp.sum(g * xhat, axis=0, keepdims=True), jnp.sum(g, axis=0, keepdims=True)


def cdf(x):
    return 0.5 * (1.0 + lax.erf(x * 0.7071067811865476))


def gelu(x):
    return x * cdf(x)


def gelu_slope(x):
    return cdf(x) + x * (0.3989422804014327 * jnp.exp(-0.5 * x * x))


def col_sum(x):
    return jnp.sum(x.astype(f32), axis=0, keepdims=True)


def vec(vecs_ref, row, width=D):
    return vecs_ref[row : row + 1, :width]


def swap_blocks(xs):
    ys = [pltpu.roll(x, f * GW, 1) if f else x for f, x in enumerate(xs)]
    lane = iota((8, 128), 1)
    outs = []
    for g in range(GROUPS):
        tiles = []
        for v in range(D // 128):
            lo, hi = (128 * v) // GW, (128 * v + 127) // GW
            tile = ys[(lo - g) % 16][:, v * 128 : (v + 1) * 128]
            for q in range(lo + 1, hi + 1):
                tile = jnp.where(lane >= q * GW - 128 * v, ys[(q - g) % 16][:, v * 128 : (v + 1) * 128], tile)
            tiles.append(tile)
        w = jnp.concatenate(tiles, axis=1)
        outs.append(pltpu.roll(w, D - g * GW, 1) if g else w)
    return outs


LANE_TILES = D // 128


def rows_to_groups(x, scratch, out_ref):
    for v in range(LANE_TILES):
        scratch[v * ROWS : (v + 1) * ROWS, :] = x[:, v * 128 : (v + 1) * 128]
    outs = swap_blocks(
        [
            jnp.concatenate([scratch[pl.ds(v * ROWS + f, 8, stride=SUPER), :] for v in range(LANE_TILES)], axis=1)
            for f in range(SUPER)
        ]
    )
    for g in range(0, GROUPS, 2):
        out_ref[g * 8 : g * 8 + 16, :] = jnp.concatenate(outs[g : g + 2], axis=0).astype(out_ref.dtype)


def groups_to_rows(in_ref, scratch):
    xs = []
    for g in range(0, GROUPS, 2):
        both = in_ref[g * 8 : g * 8 + 16, :].astype(f32)
        xs += [both[:8], both[8:]]
    for f, x in enumerate(swap_blocks(xs)):
        for v in range(LANE_TILES):
            scratch[pl.ds(v * ROWS + f, 8, stride=SUPER), :] = x[:, v * 128 : (v + 1) * 128]
    return jnp.concatenate([scratch[v * ROWS : (v + 1) * ROWS, :] for v in range(LANE_TILES)], axis=1)


def call(body, out_shapes, *args, scratch=(), smem=(), grid=None, in_specs=None, out_specs=None, flops=0, name=None):
    specs = [
        pl.BlockSpec(memory_space=pltpu.SMEM) if i in smem else pl.BlockSpec(memory_space=pltpu.VMEM)
        for i in range(len(args))
    ]
    bytes_accessed = sum(a.size * a.dtype.itemsize for a in args) + sum(
        s.size * s.dtype.itemsize for s in out_shapes
    )
    kwargs = dict(grid=grid) if grid else {}
    return pl.pallas_call(
        body,
        out_shape=out_shapes,
        in_specs=in_specs or specs,
        out_specs=out_specs or [pl.BlockSpec(memory_space=pltpu.VMEM)] * len(out_shapes),
        scratch_shapes=list(scratch),
        compiler_params=pltpu.CompilerParams(vmem_limit_bytes=VMEM),
        cost_estimate=pl.CostEstimate(flops=flops, bytes_accessed=bytes_accessed, transcendentals=0),
        name=name,
        **kwargs,
    )(*args)


def shape(dims, dtype):
    return jax.ShapeDtypeStruct(dims, dtype)


def live_rows(info):
    row = iota((ROWS, 1), 0)
    frame = (row & 63) + info[2] * 64
    length = jnp.where(row < 64, info[0], info[1])
    return (frame < length).astype(f32)


def project_kernel(info, feats, vecs, weight, normed_out, masked_out, send_out, scratch):
    xhat, _ = stats(feats[...].astype(f32))
    normed = (xhat * vec(vecs, R_IN_G, C_IN) + vec(vecs, R_IN_S, C_IN)).astype(bf16)
    normed_out[...] = normed
    masked = (nn(normed, weight[...]) + vec(vecs, R_PROJ_B)) * live_rows(info)
    masked_out[...] = masked
    rows_to_groups(masked, scratch, send_out)


def toeplitz_kernel(taps, out):
    flat = jnp.concatenate([taps[...].astype(f32), jnp.zeros((GW, D), f32)], axis=1)
    for f in range(SUPER):
        rolled = pltpu.roll(flat, f * GW, 1) if f else flat
        out[f * GW : (f + 1) * GW, :] = rolled.astype(bf16)


def shift_matrix(delta):
    r, c = iota((ROWS, ROWS), 0), iota((ROWS, ROWS), 1)
    frame_r = (r >> 3) * 4 + (r & 3)
    frame_c = (c >> 3) * 4 + (c & 3)
    return ((frame_c == frame_r + delta) & ((r & 4) == (c & 4))).astype(f32).astype(bf16)


def conv_kernel(x, w, out, acc):
    i = pl.program_id(0)

    @pl.when(i == 0)
    def _():
        acc[...] = jnp.zeros_like(acc)

    acc[...] += nt(nn(shift_matrix(i - 4), x[...]).astype(bf16), w[...])

    @pl.when(i == TAP_BLOCKS - 1)
    def _():
        out[...] = acc[...].astype(out.dtype)


def conv_back_kernel(g, w, out, acc):
    i = pl.program_id(0)

    @pl.when(i == 0)
    def _():
        acc[...] = jnp.zeros_like(acc)

    acc[...] += nn(nn(shift_matrix(4 - i), g[...]).astype(bf16), w[...])

    @pl.when(i == TAP_BLOCKS - 1)
    def _():
        out[...] = acc[...].astype(out.dtype)


def conv_weight_kernel(g, x, out, acc, spread):
    i = pl.program_id(0)

    @pl.when(i == 0)
    def _():
        acc[...] = jnp.zeros_like(acc)

    window = nn(shift_matrix(i - 4), x[...]).astype(bf16)
    product = tn(g[...], window)
    lane = iota((GW, D), 1)
    same = product[:GW]
    before = jnp.zeros((GW, D), f32)
    for f in range(1, SUPER):
        rolled = pltpu.roll(product[f * GW : (f + 1) * GW], D - f * GW, 1)
        keep = lane < D - f * GW
        same += jnp.where(keep, rolled, 0.0)
        before += jnp.where(keep, 0.0, rolled)
    acc[i] += same

    @pl.when(i > 0)
    def _():
        acc[i - 1] += before

    @pl.when(i == TAP_BLOCKS - 1)
    def _():
        for v in range(LANE_TILES):
            for j in range(TAP_BLOCKS - 1):
                spread[pl.ds(j, GW, stride=TAP_BLOCKS - 1), :] = acc[j, :, v * 128 : (v + 1) * 128]
            out[:, v * 128 : (v + 1) * 128] = spread[...]


def qkv_kernel(conv, masked, vecs, weight, pre_out, hidden_out, send_out, scratch):
    pre = groups_to_rows(conv, scratch) + vec(vecs, R_CONV_B)
    pre_out[...] = pre
    xhat, _ = stats(masked[...] + gelu(pre))
    hidden = xhat * vec(vecs, R_ENC_G) + vec(vecs, R_ENC_S)
    hidden_out[...] = hidden
    hidden_b = hidden.astype(bf16)
    zero = jnp.zeros((1, D), f32)
    for slot, (block, bias) in enumerate(((1, zero), (2, vec(vecs, R_V_B)), (0, vec(vecs, R_Q_B)))):
        part = (nn(hidden_b, weight[:, block * D : (block + 1) * D]) + bias).astype(bf16)
        for u in range(2):
            for pair in range(PAIRS):
                send_out[u * PAIRS + pair, slot * 64 : (slot + 1) * 64, :] = part[
                    u * 64 : (u + 1) * 64, pair * 128 : (pair + 1) * 128
                ]
    send_out[2 * PAIRS :] = jnp.zeros((SEQ - 2 * PAIRS, 192, 128), bf16)


Q_BLOCK = 256


def attend_kernel(info, qkv, out, log_out):
    keys = qkv[:, 0:64, :].reshape(1024, 128)
    values = qkv[:, 64:128, :].reshape(1024, 128)
    left = iota((Q_BLOCK, 128), 1) < 64
    key_live = iota((Q_BLOCK, 1024), 1) < info[5]
    per = Q_BLOCK // 64

    def step(n, carry):
        query = qkv[pl.ds(n * per, per), 128:192, :].reshape(Q_BLOCK, 128)
        parts, logs = [], []
        for head in range(2):
            own = left if head == 0 else ~left
            scores = nt(jnp.where(own, query, jnp.zeros_like(query)), keys)
            scores = jnp.where(key_live, scores * head_scale, neg_fill)
            top = jnp.max(scores, axis=-1, keepdims=True)
            e = jnp.exp(scores - top)
            total = jnp.sum(e, axis=-1, keepdims=True)
            probs = (e * (1.0 / total)).astype(bf16)
            parts.append(nn(probs, values))
            logs.append(top + jnp.log(total))
        rows = pl.ds(pl.multiple_of(n * Q_BLOCK, Q_BLOCK), Q_BLOCK)
        out[rows, :] = jnp.where(left, parts[0], parts[1]).astype(bf16)
        log_out[rows, :] = jnp.where(left, logs[0], logs[1])
        return carry

    lax.fori_loop(0, 1024 // Q_BLOCK, step, 0)


def attend_back_kernel(info, qkv, grad, logs, out, dk, dv):
    keys = qkv[:, 0:64, :].reshape(1024, 128)
    values = qkv[:, 64:128, :].reshape(1024, 128)
    left = iota((Q_BLOCK, 128), 1) < 64
    key_live = iota((Q_BLOCK, 1024), 1) < info[5]
    per = Q_BLOCK // 64
    dk[...] = jnp.zeros_like(dk)
    dv[...] = jnp.zeros_like(dv)

    def step(n, carry):
        query = qkv[pl.ds(n * per, per), 128:192, :].reshape(Q_BLOCK, 128)
        rows = pl.ds(pl.multiple_of(n * Q_BLOCK, Q_BLOCK), Q_BLOCK)
        go = grad[rows, :]
        parts = []
        for head in range(2):
            own = left if head == 0 else ~left
            q_h = jnp.where(own, query, jnp.zeros_like(query))
            g_h = jnp.where(own, go, jnp.zeros_like(go))
            scores = jnp.where(key_live, nt(q_h, keys) * head_scale, neg_fill)
            probs = jnp.exp(scores - logs[rows, head * 64 : head * 64 + 1])
            grad_probs = nt(g_h, values)
            delta = jnp.sum(probs * grad_probs, axis=-1, keepdims=True)
            grad_scores = (head_scale * probs * (grad_probs - delta)).astype(bf16)
            parts.append(nn(grad_scores, keys))
            dk[...] += tn(grad_scores, q_h)
            dv[...] += tn(probs.astype(bf16), g_h)
        grad_query = jnp.where(left, parts[0], parts[1]).astype(bf16)
        out[pl.ds(n * per, per), 0:64, :] = grad_query.reshape(per, 64, 128)
        return carry

    lax.fori_loop(0, 1024 // Q_BLOCK, step, 0)
    out[:, 64:128, :] = dk[...].astype(bf16).reshape(SEQ, 64, 128)
    out[:, 128:192, :] = dv[...].astype(bf16).reshape(SEQ, 64, 128)


def owner_order(core):
    src, dst = iota((D, 1024), 0), iota((D, 1024), 1)
    half = dst >> 9
    s = (dst >> 5) & 15
    y = (dst >> 3) & 3
    j = dst & 7
    which = jnp.where(half == 0, core, 1 - core)
    col = (2 * y + which) * 96 + s * 6 + j
    return ((src == col) & (j < 6)).astype(f32).astype(bf16)


S_MID, S_GI, S_INNER, S_GO, S_ATT, S_GA, S_END = 0, 512, 3584, 5120, 5888, 6400, 7168


def middle_kernel(
    info, recv, hidden, vecs, cot, out_w, inner_w, outer_w,
    act_out, grad_att_out, gmi_out, send_out, own_out, small_out,
    act, slope,
):
    core = info[3]
    keep = info[4].astype(f32)
    att = jnp.concatenate(
        [jnp.concatenate([recv[u * PAIRS + p] for p in range(PAIRS)], axis=1) for u in range(2)], axis=0
    )
    middle_in = hidden[...] + nn(att, out_w[...]) + vec(vecs, R_OUT_B)
    xm, rm = stats(middle_in)
    middle = xm * vec(vecs, R_MID_G) + vec(vecs, R_MID_S)
    middle_b = middle.astype(bf16)
    outer = jnp.zeros((ROWS, D), f32)
    for q in range(4):
        cols = slice(q * D, (q + 1) * D)
        pre = nn(middle_b, inner_w[:, cols]) + vec(vecs, R_INNER_B + q)
        c = cdf(pre)
        inner_b = (pre * c).astype(bf16)
        act[:, cols] = inner_b
        slope[:, cols] = c + pre * (0.3989422804014327 * jnp.exp(-0.5 * pre * pre))
        outer += nn(inner_b, outer_w[cols, :])
    final_in = middle + keep * (outer + vec(vecs, R_OUTER_B))
    xf, rf = stats(final_in)
    act_out[...] = (xf * vec(vecs, R_FIN_G) + vec(vecs, R_FIN_S)).astype(bf16)
    gfi, fin_g, fin_s = norm_back(xf, rf, vec(vecs, R_FIN_G), cot[...].astype(f32))
    grad_outer = (keep * gfi).astype(bf16)
    grad_middle = gfi
    for q in range(4):
        cols = slice(q * D, (q + 1) * D)
        grad_inner = (slope[:, cols] * nt(grad_outer, outer_w[cols, :])).astype(bf16)
        send_out[:, S_GI + q * D : S_GI + (q + 1) * D] = grad_inner
        small_out[3 + q : 4 + q, :] = col_sum(grad_inner)
        grad_middle += nt(grad_inner, inner_w[:, cols])
    gmi, mid_g, mid_s = norm_back(xm, rm, vec(vecs, R_MID_G), grad_middle)
    gmi_out[...] = gmi
    grad_attn = gmi.astype(bf16)
    grad_att = nt(grad_attn, out_w[...]).astype(bf16)
    for u in range(2):
        for p in range(PAIRS):
            grad_att_out[u * PAIRS + p] = grad_att[u * 64 : (u + 1) * 64, p * 128 : (p + 1) * 128]
    grad_att_out[2 * PAIRS :] = jnp.zeros((SEQ - 2 * PAIRS, 64, 128), bf16)
    for row, value in ((0, fin_g), (1, fin_s), (2, col_sum(grad_outer)), (7, mid_g), (8, mid_s), (9, col_sum(grad_attn))):
        small_out[row : row + 1, :] = value
    small_out[10:16, :] = jnp.zeros((6, D), f32)
    order = owner_order(core)
    mid = nn(middle_b, order).astype(bf16)
    att_p = nn(att, order).astype(bf16)
    own_out[:, 0:512] = mid[:, :512]
    own_out[:, 2048:2560] = att_p[:, :512]
    send_out[:, S_MID : S_MID + 512] = mid[:, 512:]
    send_out[:, S_ATT : S_ATT + 512] = att_p[:, 512:]
    send_out[:, S_GO : S_GO + D] = grad_outer
    send_out[:, S_GA : S_GA + D] = grad_attn
    first = core == 0
    for y in range(4):
        even = act[:, 2 * y * 384 : (2 * y + 1) * 384]
        odd = act[:, (2 * y + 1) * 384 : (2 * y + 2) * 384]
        own_out[:, 512 + y * 384 : 512 + (y + 1) * 384] = jnp.where(first, even, odd)
        send_out[:, S_INNER + y * 384 : S_INNER + (y + 1) * 384] = jnp.where(first, odd, even)


def dense_grads_kernel(own, sent, got, out):
    def right(start, width):
        return jnp.concatenate([sent[:, start : start + width], got[:, start : start + width]], axis=0)

    def left(start, theirs, width):
        return jnp.concatenate([own[:, start : start + width], got[:, theirs : theirs + width]], axis=0)

    mid = left(0, S_MID, 512)
    for half in range(2):
        res = [tn(mid, right(S_GI + (2 * half + k) * D, D)) for k in range(2)]
        for n in range(64):
            pair = jnp.concatenate([r[n * 8 : n * 8 + 8] for r in res], axis=0)
            out[n * 64 + half * 16 : n * 64 + half * 16 + 16, :] = pair.astype(bf16)
    outer = tn(left(512, S_INNER, 1536), right(S_GO, D))
    output = tn(left(2048, S_ATT, 512), right(S_GA, D))
    for s in range(16):
        for y in range(4):
            n = s * 4 + y
            both = jnp.concatenate(
                [outer[y * 384 + s * 24 : y * 384 + s * 24 + 24], output[n * 8 : n * 8 + 8]], axis=0
            )
            out[n * 64 + 32 : n * 64 + 64, :] = both.astype(bf16)


def qkv_back_kernel(
    info, recv, gmi, pre_in, masked, vecs, weight, summed_out, conv_out, send_out, own_out, small_out, scratch
):
    pre = pre_in[...]
    xhat, r = stats(masked[...] + gelu(pre))
    hidden_b = (xhat * vec(vecs, R_ENC_G) + vec(vecs, R_ENC_S)).astype(bf16)
    grad_hidden = gmi[...]
    sums = []
    for slot in range(3):
        part = jnp.concatenate(
            [
                jnp.concatenate([recv[u * PAIRS + p, slot * 64 : (slot + 1) * 64, :] for p in range(PAIRS)], axis=1)
                for u in range(2)
            ],
            axis=0,
        )
        send_out[:, 512 + slot * D : 512 + (slot + 1) * D] = part
        sums.append(col_sum(part))
        grad_hidden += nt(part, weight[:, slot * D : (slot + 1) * D])
    grad_summed, enc_g, enc_s = norm_back(xhat, r, vec(vecs, R_ENC_G), grad_hidden)
    summed_out[...] = grad_summed
    grad_conv = (gelu_slope(pre) * grad_summed).astype(bf16).astype(f32)
    rows_to_groups(grad_conv, scratch, conv_out)
    for row, value in enumerate((enc_g, enc_s, sums[0], sums[2], jnp.sum(grad_conv, axis=0, keepdims=True))):
        small_out[row : row + 1, :] = value
    small_out[5:8, :] = jnp.zeros((3, D), f32)
    hid = nn(hidden_b, owner_order(info[3])).astype(bf16)
    own_out[...] = hid[:, :512]
    send_out[:, :512] = hid[:, 512:]


def qkv_grad_kernel(own, sent, got, out):
    left = jnp.concatenate([own[...], got[:, :512]], axis=0)
    res = [
        tn(left, jnp.concatenate([x[:, 512 + q * D : 512 + (q + 1) * D] for x in (sent, got)], axis=0))
        for q in range(3)
    ]
    for n in range(0, 64, 2):
        rows = [r[m * 8 : m * 8 + 8] for m in (n, n + 1) for r in res]
        out[n * 24 : n * 24 + 48, :] = jnp.concatenate(rows, axis=0).astype(bf16)


def feats_back_kernel(
    info, conv, summed, feats, vecs, weight, small_a, small_b, feats_out, tail_out, rows, spread
):
    grad_proj = ((summed[...] + groups_to_rows(conv, rows)) * live_rows(info)).astype(bf16)
    xhat, r = stats(feats[...].astype(f32))
    normed = (xhat * vec(vecs, R_IN_G, C_IN) + vec(vecs, R_IN_S, C_IN)).astype(bf16)
    grad_feats, in_g, in_s = norm_back(xhat, r, vec(vecs, R_IN_G, C_IN), nt(grad_proj, weight[...]))
    feats_out[...] = grad_feats
    proj = tn(normed, grad_proj)
    upper = iota((8, 384), 0) < 4
    for n in range(0, 128, 2):
        a, b = proj[n * 4 : n * 4 + 8, :384], proj[n * 4 : n * 4 + 8, 384:]
        both = jnp.concatenate(
            [jnp.where(upper, a, pltpu.roll(b, 4, 0)), jnp.where(upper, pltpu.roll(a, 4, 0), b)], axis=0
        )
        tail_out[n * 8 : n * 8 + 16, :384] = both.astype(bf16)
    a = lambda k: small_a[k : k + 1, :]
    b = lambda k: small_b[k : k + 1, :]
    vectors = [col_sum(grad_proj), b(4), b(0), b(1), b(2), b(3), a(9), a(7), a(8), a(2), a(0), a(1)]
    lane = iota((8, D), 1)
    sub = iota((8, D), 0)
    slot6 = lane - 6 * int_div(lane, 6)
    main = jnp.concatenate([jnp.where(slot6 == sub, v, 0.0) for v in vectors] + [jnp.zeros((32, D), f32)], axis=0)
    lane24, sub24 = iota((24, D), 1), iota((24, D), 0)
    slot24 = lane24 - 24 * int_div(lane24, 24)
    inner = [
        jnp.concatenate(
            [jnp.zeros((96, D), f32), jnp.where(slot24 == sub24, a(3 + k), 0.0), jnp.zeros((8, D), f32)], axis=0
        )
        for k in range(4)
    ]
    lane4, sub4 = iota((8, C_IN), 1) & 3, iota((8, C_IN), 0)
    last = jnp.concatenate(
        [
            jnp.zeros((120, C_IN), f32),
            jnp.where(lane4 == sub4, in_g, 0.0) + jnp.where(lane4 == sub4 - 4, in_s, 0.0),
        ],
        axis=0,
    )
    own = iota((128, D), 0)
    col = iota((128, D), 1)
    pick6 = (int_div(col, 6) == own).astype(f32).astype(bf16)
    pick24 = [(int_div(col, 24) + 32 * k == own).astype(f32).astype(bf16) for k in range(4)]
    pick4 = ((iota((128, C_IN), 1) >> 2) == iota((128, C_IN), 0)).astype(f32).astype(bf16)
    spread[...] = jnp.zeros_like(spread)
    terms = [(pick6, main)] + list(zip(pick24, inner)) + [(pick4, last)]
    high = [(p, m.astype(bf16)) for p, m in terms]
    low = [(p, (m - h.astype(f32)).astype(bf16)) for (p, m), (_, h) in zip(terms, high)]
    for k, part in enumerate((high, low)):
        spread[pl.ds(k, 128, stride=8), :] = functools.reduce(lambda x, y: x + y, [nt(p, m) for p, m in part])
    tail_out[:, 384:] = spread[...].astype(bf16)


def to_peers(x, axis, groups=None):
    return lax.all_to_all(x, axis, 0, 0, tiled=True, axis_index_groups=groups)


Y_GROUPS = [[0, 2, 4, 6], [1, 3, 5, 7]]


def local(
    feats, lengths, skip_flag, cotangent, input_gain, input_shift, proj_weight, proj_bias, conv_weight, conv_bias,
    encoder_gain, encoder_shift, qkv_weight, query_bias, value_bias, output_weight, output_bias, middle_gain,
    middle_shift, inner_weight, inner_bias, outer_weight, outer_bias, final_gain, final_shift,
):
    seq = lax.axis_index("seq")
    core = lax.axis_index("batch") % 2
    pad = jnp.zeros((D - C_IN,), bf16)
    vecs = (
        jnp.concatenate(
            [
                input_gain, pad, input_shift, pad, proj_bias, conv_bias, encoder_gain, encoder_shift, query_bias,
                value_bias, output_bias, middle_gain, middle_shift, inner_bias, outer_bias, final_gain, final_shift,
            ]
        )
        .astype(f32)
        .reshape(18, D)
    )
    attend_len = jnp.where(seq < PAIRS, lengths[0], lengths[1])
    info = jnp.stack([lengths[0], lengths[1], seq, core, 1 - skip_flag[0], attend_len]).astype(i32)
    rows_in = feats.reshape(ROWS, C_IN)
    cot = cotangent.reshape(ROWS, D)

    normed, masked, conv_send = call(
        project_kernel,
        [shape((ROWS, C_IN), bf16), shape((ROWS, D), f32), shape((ROWS, D), bf16)],
        info, rows_in, vecs, proj_weight, smem=(0,), flops=2 * ROWS * C_IN * D, name="project",
        scratch=[TRANSPOSE_SCRATCH],
    )
    conv_x = to_peers(conv_send, "seq")
    own_taps = lax.dynamic_slice_in_dim(conv_weight, seq * GW, GW, axis=0)
    taps = own_taps.transpose(0, 2, 1).reshape(GW, KW * GW)
    (band,) = call(toeplitz_kernel, [shape((D, TAP_BLOCKS * D), bf16)], taps, flops=10**7, name="toeplitz")

    whole = pl.BlockSpec((ROWS, D), lambda i: (0, 0))
    band_block = pl.BlockSpec((D, D), lambda i: (0, i))
    (conv_y,) = call(
        conv_kernel, [shape((ROWS, D), bf16)], conv_x, band, grid=(TAP_BLOCKS,), in_specs=[whole, band_block],
        out_specs=[whole], scratch=[pltpu.VMEM((ROWS, D), f32)], flops=2 * ROWS * D * D * TAP_BLOCKS, name="conv",
    )
    conv_back = to_peers(conv_y, "seq")
    conv_pre, hidden, qkv_send = call(
        qkv_kernel,
        [shape((ROWS, D), f32), shape((ROWS, D), f32), shape((SEQ, 192, 128), bf16)],
        conv_back, masked, vecs, qkv_weight, flops=2 * ROWS * D * 3 * D, name="qkv", scratch=[TRANSPOSE_SCRATCH],
    )
    qkv = to_peers(qkv_send, "seq")
    attended, logs = call(
        attend_kernel,
        [shape((1024, 128), bf16), shape((1024, 128), f32)],
        info, qkv, smem=(0,), flops=8 * 1024 * 1024 * 128, name="attend",
    )
    att_recv = to_peers(attended.reshape(SEQ, 64, 128), "seq")
    activations, grad_att_send, gmi, pair_send, pair_own, small_a = call(
        middle_kernel,
        [
            shape((ROWS, D), bf16), shape((SEQ, 64, 128), bf16), shape((ROWS, D), f32), shape((ROWS, S_END), bf16),
            shape((ROWS, 2560), bf16), shape((16, D), f32),
        ],
        info, att_recv, hidden, vecs, cot, output_weight, inner_weight, outer_weight, smem=(0,),
        scratch=[pltpu.VMEM((ROWS, FF), bf16), pltpu.VMEM((ROWS, FF), f32)],
        flops=2 * ROWS * (4 * D * FF + 2 * D * D), name="middle",
    )
    swap = [(i, i ^ 1) for i in range(8)]
    pair_got = lax.ppermute(pair_send, "batch", swap)
    grad_att = to_peers(grad_att_send, "seq").reshape(1024, 128)
    (dense,) = call(
        dense_grads_kernel, [shape((4096, D), bf16)], pair_own, pair_send, pair_got,
        flops=2 * 256 * D * (2048 + 1536 + 512), name="dense_grads",
    )
    dense_part = lax.psum_scatter(dense, "seq", scatter_dimension=0, tiled=True)
    dense_own = lax.psum_scatter(
        dense_part, "batch", scatter_dimension=0, tiled=True, axis_index_groups=Y_GROUPS
    ).astype(f32)

    (grad_qkv_send,) = call(
        attend_back_kernel, [shape((SEQ, 192, 128), bf16)], info, qkv, grad_att, logs, smem=(0,),
        scratch=[pltpu.VMEM((1024, 128), f32)] * 2, flops=20 * 1024 * 1024 * 128, name="attend_back",
    )
    grad_qkv = to_peers(grad_qkv_send, "seq")
    grad_summed, grad_conv_send, qkv_pair_send, qkv_pair_own, small_b = call(
        qkv_back_kernel,
        [
            shape((ROWS, D), f32), shape((ROWS, D), bf16), shape((ROWS, 512 + 3 * D), bf16), shape((ROWS, 512), bf16),
            shape((8, D), f32),
        ],
        info, grad_qkv, gmi, conv_pre, masked, vecs, qkv_weight, smem=(0,), scratch=[TRANSPOSE_SCRATCH],
        flops=2 * ROWS * D * 3 * D, name="qkv_back",
    )
    grad_conv = to_peers(grad_conv_send, "seq")
    qkv_pair_got = lax.ppermute(qkv_pair_send, "batch", swap)
    (qkv_grads,) = call(
        qkv_grad_kernel, [shape((1536, D), bf16)], qkv_pair_own, qkv_pair_send, qkv_pair_got,
        flops=2 * 256 * 512 * 3 * D, name="qkv_grads",
    )
    (grad_x,) = call(
        conv_back_kernel, [shape((ROWS, D), bf16)], grad_conv, band, grid=(TAP_BLOCKS,), in_specs=[whole, band_block],
        out_specs=[whole], scratch=[pltpu.VMEM((ROWS, D), f32)], flops=2 * ROWS * D * D * TAP_BLOCKS,
        name="conv_back",
    )
    grad_x_back = to_peers(grad_x, "seq")
    (tap_grads,) = call(
        conv_weight_kernel, [shape((8 * GW, D), f32)], grad_conv, conv_x, grid=(TAP_BLOCKS,), in_specs=[whole, whole],
        out_specs=[pl.BlockSpec((8 * GW, D), lambda i: (0, 0))], scratch=[pltpu.VMEM((TAP_BLOCKS, GW, D), f32), pltpu.VMEM((8 * GW, 128), f32)],
        flops=2 * ROWS * D * D * TAP_BLOCKS, name="conv_grads",
    )
    tap_part = lax.psum_scatter(tap_grads, "batch", scatter_dimension=0, tiled=True)
    moves = [(b * 16 + g, (g // 2) * 16 + 8 * (g % 2) + b) for b in range(8) for g in range(16)]
    tap_own = lax.ppermute(tap_part, ("batch", "seq"), moves)
    grad_conv_weight = tap_own.reshape(6, KW, GW).transpose(0, 2, 1)

    qkv_part = jnp.sum(to_peers(qkv_grads, "seq").reshape(SEQ, 96, D).astype(f32), axis=0).astype(bf16)
    qkv_own = jnp.sum(to_peers(qkv_part, "batch", Y_GROUPS).reshape(4, 24, D).astype(f32), axis=0)

    grad_feats, tail = call(
        feats_back_kernel,
        [shape((ROWS, C_IN), f32), shape((1024, 512), bf16)],
        info, grad_x_back, grad_summed, rows_in, vecs, proj_weight, small_a, small_b, smem=(0,),
        scratch=[TRANSPOSE_SCRATCH, pltpu.VMEM((1024, 128), f32)], flops=4 * ROWS * C_IN * D,
        name="feats_back",
    )
    tail_sum = jnp.sum(to_peers(tail, ("batch", "seq")).reshape(128, 8, 512).astype(f32), axis=0)
    grad_proj_weight = jnp.concatenate([tail_sum[:4, :384], tail_sum[4:, :384]], axis=1)
    small = tail_sum[0, 384:] + tail_sum[1, 384:]
    (
        g_proj_b, g_conv_b, g_enc_g, g_enc_s, g_q_b, g_v_b, g_out_b, g_mid_g, g_mid_s, g_outer_b, g_fin_g, g_fin_s,
    ) = [small[8 * k : 8 * k + 6] for k in range(12)]

    def heads(x, parts):
        return x.reshape(parts, 8, D)[:, :6].transpose(1, 0, 2).reshape(6, parts * D)

    return (
        activations.reshape(2, 64, D),
        grad_feats.reshape(2, 64, C_IN),
        small[120:124],
        small[124:128],
        grad_proj_weight,
        g_proj_b,
        grad_conv_weight,
        g_conv_b,
        g_enc_g,
        g_enc_s,
        heads(qkv_own, 3),
        g_q_b,
        g_v_b,
        dense_own[56:62],
        g_out_b,
        g_mid_g,
        g_mid_s,
        heads(dense_own[:32], 4),
        small[96:120],
        dense_own[32:56],
        g_outer_b,
        g_fin_g,
        g_fin_s,
    )


def solution(mesh):
    split = P("batch", "seq", None)
    both = ("batch", "seq")
    placed = (split, P("batch"), P("batch"), split) + (P(),) * 21
    row, matrix = P(both), P(both, None)
    return jax.shard_map(
        local,
        mesh=mesh,
        in_specs=placed,
        out_specs=(
            split, split, row, row, matrix, row, P(both, None, None), row, row, row, matrix, row, row, matrix, row,
            row, row, matrix, row, matrix, row, row, row,
        ),
        check_vma=False,
    )
```

```python
import functools

import jax
import jax.numpy as jnp
from jax import lax
from jax.experimental import pallas as pl
from jax.experimental.pallas import tpu as pltpu
from jax.sharding import PartitionSpec as P

f32 = jnp.float32
bf16 = jnp.bfloat16
i32 = jnp.int32

norm_eps = 1e-05
head_scale = 0.125
neg_fill = -1e30

D = 768
C_IN = 512
FF = 3072
GROUPS = 16
GW = 48
KW = 128
SUPER = 16
TAP_BLOCKS = 9
ROWS = 128
SEQ = 16
PAIRS = 6
MIB = 1024 * 1024
TRANSPOSE_SCRATCH = pltpu.VMEM((D, 128), f32)

def nn(a, b):
    return lax.dot_general(a, b, (((1,), (0,)), ((), ())), preferred_element_type=f32)


def nt(a, b):
    return lax.dot_general(a, b, (((1,), (1,)), ((), ())), preferred_element_type=f32)


def tn(a, b):
    return lax.dot_general(a, b, (((0,), (0,)), ((), ())), preferred_element_type=f32)


def iota(shape, dim):
    return lax.broadcasted_iota(i32, shape, dim)


def int_div(x, c):
    return ((x.astype(f32) + 0.5) * (1.0 / c)).astype(i32)


def stats(x):
    c = x - jnp.mean(x, axis=-1, keepdims=True)
    r = lax.rsqrt(jnp.mean(c * c, axis=-1, keepdims=True) + norm_eps)
    return c * r, r


def norm_back(xhat, r, gain, g):
    e = g * gain
    dx = r * (e - jnp.mean(e, axis=-1, keepdims=True) - xhat * jnp.mean(e * xhat, axis=-1, keepdims=True))
    return dx, jnp.sum(g * xhat, axis=0, keepdims=True), jnp.sum(g, axis=0, keepdims=True)


def cdf(x):
    return 0.5 * (1.0 + lax.erf(x * 0.7071067811865476))


def gelu(x):
    return x * cdf(x)


def gelu_slope(x):
    return cdf(x) + x * (0.3989422804014327 * jnp.exp(-0.5 * x * x))


def col_sum(x):
    return jnp.sum(x.astype(f32), axis=0, keepdims=True)


def vec(lazy):
    ref = lazy()
    return ref[...].astype(f32).reshape(1, ref.shape[0])


def swap_blocks(xs):
    ys = [pltpu.roll(x, f * GW, 1) if f else x for f, x in enumerate(xs)]
    lane = iota((8, 128), 1)
    outs = []
    for g in range(GROUPS):
        tiles = []
        for v in range(D // 128):
            lo, hi = (128 * v) // GW, (128 * v + 127) // GW
            tile = ys[(lo - g) % 16][:, v * 128 : (v + 1) * 128]
            for q in range(lo + 1, hi + 1):
                tile = jnp.where(lane >= q * GW - 128 * v, ys[(q - g) % 16][:, v * 128 : (v + 1) * 128], tile)
            tiles.append(tile)
        w = jnp.concatenate(tiles, axis=1)
        outs.append(pltpu.roll(w, D - g * GW, 1) if g else w)
    return outs


LANE_TILES = D // 128


def rows_to_groups(x, scratch, out_ref):
    for v in range(LANE_TILES):
        scratch[v * ROWS : (v + 1) * ROWS, :] = x[:, v * 128 : (v + 1) * 128]
    outs = swap_blocks(
        [
            jnp.concatenate([scratch[pl.ds(v * ROWS + f, 8, stride=SUPER), :] for v in range(LANE_TILES)], axis=1)
            for f in range(SUPER)
        ]
    )
    for g in range(0, GROUPS, 2):
        out_ref[g * 8 : g * 8 + 16, :] = jnp.concatenate(outs[g : g + 2], axis=0).astype(out_ref.dtype)


def groups_to_rows(in_ref, scratch):
    xs = [in_ref[g].astype(f32)[:8] for g in range(GROUPS)]
    for f, x in enumerate(swap_blocks(xs)):
        for v in range(LANE_TILES):
            scratch[pl.ds(v * ROWS + f, 8, stride=SUPER), :] = x[:, v * 128 : (v + 1) * 128]
    return jnp.concatenate([scratch[v * ROWS : (v + 1) * ROWS, :] for v in range(LANE_TILES)], axis=1)


class Hbm:
    def __init__(self, array):
        self.array = array


class Raw(Hbm):
    pass


class Smem(Hbm):
    pass


class Spill:
    def __init__(self, dims, dtype, parts=1):
        self.struct, self.parts = jax.ShapeDtypeStruct(dims, dtype), parts


class Flusher:
    def __init__(self, ref, target, sems, base, copies):
        self.ref, self.target, self.sems, self.next, self.copies = ref, target, sems, base, copies

    def put(self, value):
        self.ref[...] = value
        self.flush()

    def flush(self, *index):
        src, dst = (self.ref.at[index], self.target.at[index]) if index else (self.ref, self.target)
        copy = pltpu.make_async_copy(src, dst, self.sems.at[self.next])
        copy.start()
        self.next += 1
        self.copies.append(copy)


class Lazy:
    def __init__(self, copy, ref):
        self.copy, self.ref, self.waited = copy, ref, False

    def __call__(self):
        if not self.waited:
            self.copy.wait()
            self.waited = True
        return self.ref


def call(body, outs, *args, scratch=(), flops=0, name=None, mib=16):
    fetched = [k for k, a in enumerate(args) if type(a) in (Hbm, Smem)]
    spilled = [k for k, o in enumerate(outs) if isinstance(o, Spill)]
    arrays = [
        pltpu.with_memory_space_constraint(a.array, pltpu.HBM) if isinstance(a, Hbm) and not isinstance(a, Smem) else getattr(a,'array',a) for a in args
    ]
    structs = [o.struct if isinstance(o, Spill) else o for o in outs]
    near = {Hbm: pltpu.VMEM, Smem: pltpu.SMEM}
    own = [near[type(args[k])](arrays[k].shape, arrays[k].dtype) for k in fetched]
    own += [pltpu.VMEM(structs[k].shape, structs[k].dtype) for k in spilled]
    sem_count = len(fetched) + sum(outs[k].parts for k in spilled)
    if sem_count:
        own.append(pltpu.SemaphoreType.DMA((sem_count,)))

    def wrapped(*refs):
        n_in, n_out = len(args), len(outs)
        ins, out_refs, rest = list(refs[:n_in]), list(refs[n_in : n_in + n_out]), list(refs[n_in + n_out :])
        extra, rest = rest[: len(own)], rest[len(own) :]
        lazies, flushed = [], []
        for slot, k in enumerate(fetched):
            copy = pltpu.make_async_copy(ins[k], extra[slot], extra[-1].at[slot])
            copy.start()
            ins[k] = Lazy(copy, extra[slot])
            lazies.append(ins[k])
        base = len(fetched)
        for slot, k in enumerate(spilled):
            out_refs[k] = Flusher(extra[len(fetched) + slot], out_refs[k], extra[-1], base, flushed)
            base += outs[k].parts
        body(*ins, *out_refs, *rest)
        for lazy in lazies:
            lazy()
        for copy in flushed:
            copy.wait()

    bytes_accessed = sum(a.size * a.dtype.itemsize for a in arrays) + sum(o.size * o.dtype.itemsize for o in structs)
    return pl.pallas_call(
        wrapped,
        out_shape=[pltpu.HBM(o.struct.shape, o.struct.dtype) if isinstance(o, Spill) else o for o in outs],
        in_specs=[pl.BlockSpec(memory_space=pltpu.HBM if isinstance(a, Hbm) else pltpu.VMEM) for a in args],
        out_specs=[pl.BlockSpec(memory_space=pltpu.HBM if isinstance(o, Spill) else pltpu.VMEM) for o in outs],
        scratch_shapes=own + list(scratch),
        compiler_params=pltpu.CompilerParams(vmem_limit_bytes=mib * MIB),
        cost_estimate=pl.CostEstimate(flops=flops, bytes_accessed=bytes_accessed, transcendentals=0),
        name=name,
    )(*arrays)


def fetch(sems, *pairs):
    copies = [pltpu.make_async_copy(src, dst, sems.at[k]) for k, (src, dst) in enumerate(pairs)]
    for copy in copies:
        copy.start()
    return copies


def shape(dims, dtype):
    return jax.ShapeDtypeStruct(dims, dtype)


def live_rows(lengths):
    row = iota((ROWS, 1), 0)
    frame = (row & 63) + lax.axis_index("seq") * 64
    ref = lengths()
    length = jnp.where(row < 64, ref[0], ref[1])
    return (frame < length).astype(f32)


def head_utterance():
    return (lax.axis_index("seq") >= PAIRS).astype(i32)


def core_index():
    return lax.axis_index("batch") & 1


def project_kernel(lengths, feats, gain, shift, weight, bias, masked_out, send_out, scratch):
    xhat, _ = stats(feats()[...].astype(f32))
    normed = (xhat * vec(gain) + vec(shift)).astype(bf16)
    masked = (nn(normed, weight()[...]) + vec(bias)) * live_rows(lengths)
    masked_out.put(masked)
    rows_to_groups(masked, scratch, send_out)


def make_band(taps, out):
    flat = jnp.concatenate([taps[...].astype(f32), jnp.zeros((GW, D), f32)], axis=1)
    for f in range(SUPER):
        rolled = pltpu.roll(flat, f * GW, 1) if f else flat
        out[f * GW : (f + 1) * GW, :] = rolled.astype(bf16)


def shift_matrix(delta):
    r, c = iota((ROWS, ROWS), 0), iota((ROWS, ROWS), 1)
    frame_r = (r >> 3) * 4 + (r & 3)
    frame_c = (c >> 3) * 4 + (c & 3)
    return ((frame_c == frame_r + delta) & ((r & 4) == (c & 4))).astype(f32).astype(bf16)


def conv_kernel(x_in, taps, out, w):
    make_band(taps(), w)
    x = x_in()[...]
    windows = [nn(shift_matrix(i - 4), x).astype(bf16) for i in range(TAP_BLOCKS)]
    out[...] = nt(jnp.concatenate(windows, axis=1), w[...]).astype(out.dtype)


QKV_ROWS = 32
CHUNK = 40
Y_OUTER, Y_OUTPUT, Y_END = 96, 192, 224
HOP = 80


def conv_gradient(got):
    pieces = [got[g, QKV_ROWS:CHUNK, :].astype(f32) for g in range(GROUPS)]
    return jnp.concatenate(pieces, axis=0).astype(bf16)


def conv_back_kernel(got_in, taps, out, w):
    make_band(taps(), w)
    grad = conv_gradient(got_in())
    total = jnp.zeros((ROWS, D), f32)
    for i in range(TAP_BLOCKS):
        total += nn(nn(shift_matrix(4 - i), grad).astype(bf16), w[:, i * D : (i + 1) * D])
    out[...] = total.astype(bf16)


def conv_weight_kernel(got_in, other_in, x_in, x_other, out, *rest):
    tap_outs, (wide, acc, spread, chunks) = rest[:4], rest[4:]
    core = core_index()
    src, dst = iota((D, 384), 0), iota((D, 384), 1)
    f = int_div(dst, 24)
    y = int_div(dst - 24 * f, 6)
    own_taps = (src == f * GW + (2 * y + core) * 6 + (dst - 24 * f - 6 * y)).astype(f32).astype(bf16)
    grads, windows = [], []
    for ref, values in ((got_in(), x_in()), (other_in(), x_other())):
        grads.append(nn(conv_gradient(ref), own_taps).astype(bf16))
        x = values[...]
        windows.append(
            jnp.concatenate([nn(shift_matrix(i - 4), x).astype(bf16) for i in range(TAP_BLOCKS)], axis=1)
        )
    width = TAP_BLOCKS * D
    wide[...] = tn(jnp.concatenate(grads, axis=0), jnp.concatenate(windows, axis=0))
    acc[:, width - 384 :] = jnp.zeros((24, 384), f32)
    for f in range(7, -1, -1):
        acc[:, : width - 384] = (
            (pltpu.roll(acc[...], width - GW, 1)[:, : width - 384] if f < 7 else 0.0)
            + wide[f * 24 : f * 24 + 24, : width - 384]
            + wide[(f + 8) * 24 : (f + 8) * 24 + 24, 384:]
        )
    for v in range(LANE_TILES):
        lanes = slice(v * 128, (v + 1) * 128)
        for i in range(8):
            spread[pl.ds(i, 24, stride=8), :] = acc[:, i * D + v * 128 : i * D + (v + 1) * 128]
        for y in range(4):
            chunks[y, :, lanes] = spread[y * GW : (y + 1) * GW, :].astype(bf16)
    own_y = lax.axis_index("batch") >> 1
    for k, tap_out in enumerate(tap_outs):
        tap_out.put(chunks[(own_y + k) & 3])
    pairs = []
    for p in range(PAIRS):
        terms = [ref[n, :QKV_ROWS, :].astype(f32) for ref in (got_in(), other_in()) for n in (p, PAIRS + p)]
        pairs.append(terms[0] + terms[1] + terms[2] + terms[3])

    def chunk(x, b, k):
        rows = slice((b & 3) * 8, (b & 3) * 8 + 8)
        start = (b >> 2) * 384 + k * 128
        return x[rows, start : start + 128]

    for y in range(4):
        parts = [
            jnp.concatenate(
                [jnp.where(core == 0, chunk(x, 2 * y, k), chunk(x, 2 * y + 1, k)) for x in pairs], axis=1
            )
            for k in range(3)
        ]
        out[y] = jnp.concatenate(parts, axis=0).astype(bf16)


def conv_sum_kernel(*refs):
    total = refs[0]()[...].astype(f32)
    for ref in refs[1:-1]:
        total += ref()[...].astype(f32)
    refs[-1][...] = total


def hop_kernel(chunks_in, dense_in, spill):
    chunks = chunks_in()
    dense = dense_in()[...]
    dst, src = iota((ROWS, Y_END), 0), iota((ROWS, Y_END), 1)
    y, t = dst >> 5, dst & 31
    q = int_div(t, 6)
    row = q * 24 + y * 6 + (t - 6 * q) + jnp.where(q == 4, 96, 0)
    sixes = nn(((src == row) & (t < 30)).astype(f32).astype(bf16), dense)
    outer = dense[Y_OUTER:Y_OUTPUT].astype(f32)
    for y in range(4):
        pieces = [chunks[y].astype(f32), sixes[y * 32 : y * 32 + 32], outer[y * 24 : y * 24 + 24]]
        spill.ref[y * HOP : (y + 1) * HOP, :] = jnp.concatenate(pieces, axis=0).astype(bf16)
    spill.flush()


def hop_sum_kernel(total_in, qkv_out, inner_out, outer_out, output_out):
    total = total_in()[...].astype(f32)
    for k in range(3):
        qkv_out[:, k * D : (k + 1) * D] = total[8 * k : 8 * k + 6]
    dense = total[24:]
    for q in range(4):
        inner_out[:, q * D : (q + 1) * D] = dense[q * 6 : q * 6 + 6]
    output_out[...] = dense[24:30]
    outer_out[...] = dense[32:]


def hidden_order():
    src, dst = iota((D, 1024), 0), iota((D, 1024), 1)
    j = dst & 7
    col = ((dst >> 3) & 7) * 96 + (dst >> 6) * 6 + j
    return ((src == col) & (j < 6)).astype(f32).astype(bf16)


def qkv_kernel(
    conv, masked, conv_bias, gain, shift, weight, query_bias, value_bias,
    pre_out, hidden_out, send_out, order_out, scratch,
):
    pre = groups_to_rows(conv, scratch) + vec(conv_bias)
    pre_out.put(pre)
    xhat, _ = stats(masked()[...] + gelu(pre))
    hidden = xhat * vec(gain) + vec(shift)
    hidden_out.put(hidden)
    hidden_b = hidden.astype(bf16)
    order_out.put(nn(hidden_b, hidden_order()).astype(bf16))
    zero = jnp.zeros((1, D), f32)
    send = send_out.ref
    for slot, (block, bias) in enumerate(((1, zero), (2, vec(value_bias)), (0, vec(query_bias)))):
        part = (nn(hidden_b, weight()[:, block * D : (block + 1) * D]) + bias).astype(bf16)
        for u in range(2):
            for pair in range(PAIRS):
                send[u * PAIRS + pair, slot * 64 : (slot + 1) * 64, :] = part[
                    u * 64 : (u + 1) * 64, pair * 128 : (pair + 1) * 128
                ]
    send[2 * PAIRS :] = jnp.zeros((SEQ - 2 * PAIRS, 192, 128), bf16)
    send_out.flush()


Q_BLOCK = 256


def key_mask(lengths):
    ref = lengths()
    length = jnp.where(head_utterance() == 0, ref[0], ref[1])
    return iota((Q_BLOCK, 1024), 1) < length


def attend_kernel(lengths, qkv_in, out, log_spill):
    qkv, log_out = qkv_in(), log_spill.ref
    keys = qkv[:, 0:64, :].reshape(1024, 128)
    values = qkv[:, 64:128, :].reshape(1024, 128)
    left = iota((Q_BLOCK, 128), 1) < 64
    key_live = key_mask(lengths)
    per = Q_BLOCK // 64

    def step(n, carry):
        query = qkv[pl.ds(n * per, per), 128:192, :].reshape(Q_BLOCK, 128) * head_scale
        parts, logs = [], []
        for head in range(2):
            own = left if head == 0 else ~left
            scores = nt(jnp.where(own, query, jnp.zeros_like(query)), keys)
            scores = jnp.where(key_live, scores, neg_fill)
            top = jnp.max(scores, axis=-1, keepdims=True)
            e = jnp.exp(scores - top)
            total = jnp.sum(e, axis=-1, keepdims=True)
            parts.append(nn(e.astype(bf16), values) * (1.0 / total))
            logs.append(top + jnp.log(total))
        rows = pl.ds(pl.multiple_of(n * Q_BLOCK, Q_BLOCK), Q_BLOCK)
        out[rows, :] = jnp.where(left, parts[0], parts[1]).astype(bf16)
        log_out[rows, :] = jnp.where(left, logs[0], logs[1])
        return carry

    lax.fori_loop(0, 1024 // Q_BLOCK, step, 0)
    log_spill.flush()


def attend_back_kernel(lengths, qkv_in, grad, logs_in, spill, dk, dv):
    qkv, logs, out = qkv_in(), logs_in(), spill.ref
    keys = qkv[:, 0:64, :].reshape(1024, 128)
    values = qkv[:, 64:128, :].reshape(1024, 128)
    left = iota((Q_BLOCK, 128), 1) < 64
    key_live = key_mask(lengths)
    per = Q_BLOCK // 64
    dk[...] = jnp.zeros_like(dk)
    dv[...] = jnp.zeros_like(dv)

    def step(n, carry):
        query = qkv[pl.ds(n * per, per), 128:192, :].reshape(Q_BLOCK, 128) * head_scale
        rows = pl.ds(pl.multiple_of(n * Q_BLOCK, Q_BLOCK), Q_BLOCK)
        go = grad[rows, :]
        parts = []
        for head in range(2):
            own = left if head == 0 else ~left
            q_h = jnp.where(own, query, jnp.zeros_like(query))
            g_h = jnp.where(own, go, jnp.zeros_like(go))
            scores = jnp.where(key_live, nt(q_h, keys), neg_fill)
            probs = jnp.exp(scores - logs[rows, head * 64 : head * 64 + 1])
            grad_probs = nt(g_h, values)
            delta = jnp.sum(probs * grad_probs, axis=-1, keepdims=True)
            grad_scores = (probs * (grad_probs - delta)).astype(bf16)
            parts.append(nn(grad_scores, keys))
            dk[...] += tn(grad_scores, q_h)
            dv[...] += tn(probs.astype(bf16), g_h)
        grad_query = (jnp.where(left, parts[0], parts[1]) * head_scale).astype(bf16)
        out[pl.ds(n * per, per), 0:64, :] = grad_query.reshape(per, 64, 128)
        return carry

    lax.fori_loop(0, 1024 // Q_BLOCK, step, 0)
    out[:, 64:128, :] = dk[...].astype(bf16).reshape(SEQ, 64, 128)
    out[:, 128:192, :] = dv[...].astype(bf16).reshape(SEQ, 64, 128)
    spill.flush()


def head_grads_kernel(hidden_in, grads_in, spill):
    hidden, grads, out = hidden_in(), grads_in(), spill.ref
    rows = hidden[:, head_utterance()].reshape(1024, 1024)
    right = jnp.concatenate([grads[:, k * 64 : (k + 1) * 64, :].reshape(1024, 128) for k in range(3)], axis=1)
    res = tn(rows, right)
    for s in range(SEQ):
        for half in range(2):
            out[s * 32 : s * 32 + 32, half * 384 : half * 384 + 384] = res[
                s * 64 + half * 32 : s * 64 + half * 32 + 32
            ].astype(bf16)
    spill.flush()


def owner_order(core):
    src, dst = iota((D, D), 0), iota((D, D), 1)
    second = dst >= 384
    rest = dst - jnp.where(second, 384, 0)
    which = jnp.where(second, 1 - core, core)
    s = int_div(rest, 24)
    y = int_div(rest - 24 * s, 6)
    j = rest - 24 * s - 6 * y
    return (src == (2 * y + which) * 96 + s * 6 + j).astype(f32).astype(bf16)


S_MID, S_GI, S_INNER, S_GO, S_ATT, S_GA, S_END = 0, 384, 3456, 4992, 5760, 6144, 6912
O_MID, O_INNER, O_ATT, O_END = 0, 384, 1920, 2304


def middle_kernel(
    skip, recv, hidden, cot, out_w_in, out_b, mid_g_in, mid_s_in, inner_w_in, inner_b_in, outer_w_in, outer_b,
    fin_g_in, fin_s_in,
    act_out, grad_att_out, gmi_out, send_out, own_out, small_out,
    act, slope, out_w, inner_w, outer_w, sems,
):
    pairs = [(out_w_in, out_w)]
    for q in range(4):
        cols = slice(q * D, (q + 1) * D)
        pairs += [(inner_w_in.at[:, cols], inner_w.at[:, cols]), (outer_w_in.at[cols, :], outer_w.at[cols, :])]
    copies = fetch(sems, *pairs)
    core = core_index()
    keep = (1 - skip()[0]).astype(f32)
    mid_gain, fin_gain, inner_bias = vec(mid_g_in), vec(fin_g_in), vec(inner_b_in)
    att = jnp.concatenate(
        [jnp.concatenate([recv[u * PAIRS + p] for p in range(PAIRS)], axis=1) for u in range(2)], axis=0
    )
    copies[0].wait()
    middle_in = hidden()[...] + nn(att, out_w[...]) + vec(out_b)
    xm, rm = stats(middle_in)
    middle = xm * mid_gain + vec(mid_s_in)
    middle_b = middle.astype(bf16)
    order = owner_order(core)
    mid = nn(middle_b, order).astype(bf16)
    att_p = nn(att, order).astype(bf16)
    own, send = own_out, send_out

    own[:, O_MID : O_MID + 384] = mid[:, :384]
    own[:, O_ATT : O_ATT + 384] = att_p[:, :384]
    send[:, S_MID : S_MID + 384] = mid[:, 384:]
    send[:, S_ATT : S_ATT + 384] = att_p[:, 384:]
    outer = jnp.zeros((ROWS, D), f32)
    for q in range(4):
        cols = slice(q * D, (q + 1) * D)
        copies[1 + 2 * q].wait()
        pre = nn(middle_b, inner_w[:, cols]) + inner_bias[:, cols]
        c = cdf(pre)
        inner_b = (pre * c).astype(bf16)
        act[:, cols] = inner_b
        slope[:, cols] = c + pre * (0.3989422804014327 * jnp.exp(-0.5 * pre * pre))
        copies[2 + 2 * q].wait()
        outer += nn(inner_b, outer_w[cols, :])
    first = core == 0
    for y in range(4):
        even = act[:, 2 * y * 384 : (2 * y + 1) * 384]
        odd = act[:, (2 * y + 1) * 384 : (2 * y + 2) * 384]
        own[:, O_INNER + y * 384 : O_INNER + (y + 1) * 384] = jnp.where(first, even, odd)
        send[:, S_INNER + y * 384 : S_INNER + (y + 1) * 384] = jnp.where(first, odd, even)
    final_in = middle + keep * (outer + vec(outer_b))
    xf, rf = stats(final_in)
    act_out.put((xf * fin_gain + vec(fin_s_in)).astype(bf16))
    gfi, fin_g, fin_s = norm_back(xf, rf, fin_gain, cot()[...].astype(f32))
    grad_outer = (keep * gfi).astype(bf16)
    send[:, S_GO : S_GO + D] = grad_outer
    grad_middle = gfi
    for q in range(4):
        cols = slice(q * D, (q + 1) * D)
        grad_inner = (slope[:, cols] * nt(grad_outer, outer_w[cols, :])).astype(bf16)
        send[:, S_GI + q * D : S_GI + (q + 1) * D] = grad_inner
        small_out.ref[3 + q : 4 + q, :] = col_sum(grad_inner)
        grad_middle += nt(grad_inner, inner_w[:, cols])
    gmi, mid_g, mid_s = norm_back(xm, rm, mid_gain, grad_middle)
    gmi_out.put(gmi)
    grad_attn = gmi.astype(bf16)
    send[:, S_GA : S_GA + D] = grad_attn
    grad_att = nt(grad_attn, out_w[...]).astype(bf16)
    for u in range(2):
        for p in range(PAIRS):
            grad_att_out.ref[u * PAIRS + p] = grad_att[u * 64 : (u + 1) * 64, p * 128 : (p + 1) * 128]
    grad_att_out.ref[2 * PAIRS :] = jnp.zeros((SEQ - 2 * PAIRS, 64, 128), bf16)
    grad_att_out.flush()
    for row, value in ((0, fin_g), (1, fin_s), (2, col_sum(grad_outer)), (7, mid_g), (8, mid_s), (9, col_sum(grad_attn))):
        small_out.ref[row : row + 1, :] = value
    small_out.ref[10:16, :] = jnp.zeros((6, D), f32)
    small_out.flush()


def dense_grads_kernel(own, sent, got, spill):
    out = spill.ref

    def right(start):
        return jnp.concatenate([sent[:, start : start + D], got[:, start : start + D]], axis=0)

    def left(start, theirs, width):
        return jnp.concatenate([own[:, start : start + width], got[:, theirs : theirs + width]], axis=0)

    outer = tn(left(O_INNER, S_INNER, 1536), right(S_GO))
    for s in range(SEQ):
        rows = [outer[y * 384 + s * 24 : y * 384 + s * 24 + 24] for y in range(4)]
        out[s, Y_OUTER:Y_OUTPUT, :] = jnp.concatenate(rows, axis=0).astype(bf16)
    spill.flush(slice(None), slice(Y_OUTER, Y_OUTPUT))
    mid = left(O_MID, S_MID, 384)
    for half in range(2):
        res = [tn(mid, right(S_GI + (2 * half + k) * D)) for k in range(2)]
        for s in range(SEQ):
            rows = jnp.concatenate([r[s * 24 : s * 24 + 24] for r in res], axis=0)
            out[s, half * 48 : half * 48 + 48, :] = rows.astype(bf16)
        spill.flush(slice(None), slice(half * 48, half * 48 + 48))
    output = tn(left(O_ATT, S_ATT, 384), right(S_GA))
    for s in range(SEQ):
        rows = jnp.concatenate([output[s * 24 : s * 24 + 24], jnp.zeros((8, D), f32)], axis=0)
        out[s, Y_OUTPUT:, :] = rows.astype(bf16)
    spill.flush(slice(None), slice(Y_OUTPUT, Y_END))


def qkv_back_kernel(
    recv, gmi, pre_in, masked, gain_in, weight, qkv_sums, summed_out, send_out, small_out, scratch, conv_out
):
    pre = pre_in()[...]
    gain = vec(gain_in)
    xhat, r = stats(masked()[...] + gelu(pre))
    grad_hidden = gmi()[...]
    sums = []
    for slot in range(3):
        part = jnp.concatenate(
            [
                jnp.concatenate([recv[u * PAIRS + p, slot * 64 : (slot + 1) * 64, :] for p in range(PAIRS)], axis=1)
                for u in range(2)
            ],
            axis=0,
        )
        sums.append(col_sum(part))
        grad_hidden += nt(part, weight()[:, slot * D : (slot + 1) * D])
    grad_summed, enc_g, enc_s = norm_back(xhat, r, gain, grad_hidden)
    summed_out.put(grad_summed)
    grad_conv = (gelu_slope(pre) * grad_summed).astype(bf16).astype(f32)
    rows_to_groups(grad_conv, scratch, conv_out)
    for g in range(GROUPS):
        send_out[g, :QKV_ROWS, :] = qkv_sums()[g * QKV_ROWS : (g + 1) * QKV_ROWS, :]
        send_out[g, QKV_ROWS:, :] = conv_out[g * 8 : g * 8 + 8, :].astype(bf16)
    for row, value in enumerate((enc_g, enc_s, sums[0], sums[2], jnp.sum(grad_conv, axis=0, keepdims=True))):
        small_out.ref[row : row + 1, :] = value
    small_out.ref[5:8, :] = jnp.zeros((3, D), f32)
    small_out.flush()


def feats_back_kernel(
    lengths, conv, summed, feats, gain_in, shift, weight, small_a, small_b, feats_out, tail_out, rows, spread
):
    xhat, r = stats(feats()[...].astype(f32))
    gain = vec(gain_in)
    normed = (xhat * gain + vec(shift)).astype(bf16)
    grad_proj = ((summed()[...] + groups_to_rows(conv, rows)) * live_rows(lengths)).astype(bf16)
    grad_feats, in_g, in_s = norm_back(xhat, r, gain, nt(grad_proj, weight()[...]))
    feats_out.put(grad_feats)
    proj = tn(normed, grad_proj)
    upper = iota((8, 384), 0) < 4
    for n in range(0, 128, 2):
        a, b = proj[n * 4 : n * 4 + 8, :384], proj[n * 4 : n * 4 + 8, 384:]
        both = jnp.concatenate(
            [jnp.where(upper, a, pltpu.roll(b, 4, 0)), jnp.where(upper, pltpu.roll(a, 4, 0), b)], axis=0
        )
        tail_out[n * 8 : n * 8 + 16, :384] = both.astype(bf16)
    a = lambda k: small_a()[k : k + 1, :]
    b = lambda k: small_b()[k : k + 1, :]
    vectors = [col_sum(grad_proj), b(4), b(0), b(1), b(2), b(3), a(9), a(7), a(8), a(2), a(0), a(1)]
    lane = iota((8, D), 1)
    sub = iota((8, D), 0)
    slot6 = lane - 6 * int_div(lane, 6)
    main = jnp.concatenate([jnp.where(slot6 == sub, v, 0.0) for v in vectors] + [jnp.zeros((32, D), f32)], axis=0)
    lane24, sub24 = iota((24, D), 1), iota((24, D), 0)
    slot24 = lane24 - 24 * int_div(lane24, 24)
    inner = [
        jnp.concatenate(
            [jnp.zeros((96, D), f32), jnp.where(slot24 == sub24, a(3 + k), 0.0), jnp.zeros((8, D), f32)], axis=0
        )
        for k in range(4)
    ]
    lane4, sub4 = iota((8, C_IN), 1) & 3, iota((8, C_IN), 0)
    last = jnp.concatenate(
        [
            jnp.zeros((120, C_IN), f32),
            jnp.where(lane4 == sub4, in_g, 0.0) + jnp.where(lane4 == sub4 - 4, in_s, 0.0),
        ],
        axis=0,
    )
    own = iota((128, D), 0)
    col = iota((128, D), 1)
    pick6 = (int_div(col, 6) == own).astype(f32).astype(bf16)
    pick24 = [(int_div(col, 24) + 32 * k == own).astype(f32).astype(bf16) for k in range(4)]
    pick4 = ((iota((128, C_IN), 1) >> 2) == iota((128, C_IN), 0)).astype(f32).astype(bf16)
    spread[...] = jnp.zeros_like(spread)
    terms = [(pick6, main)] + list(zip(pick24, inner)) + [(pick4, last)]
    high = [(p, m.astype(bf16)) for p, m in terms]
    low = [(p, (m - h.astype(f32)).astype(bf16)) for (p, m), (_, h) in zip(terms, high)]
    for k, part in enumerate((high, low)):
        spread[pl.ds(k, 128, stride=8), :] = functools.reduce(lambda x, y: x + y, [nt(p, m) for p, m in part])
    tail_out[:, 384:] = spread[...].astype(bf16)


def tail_sum_kernel(got_in, proj_out, *vector_outs):
    got = got_in()

    def step(n, total):
        block = got[pl.ds(n * 8, 8)].astype(f32)
        for k in range(8):
            total += block[k]
        return total

    total = lax.fori_loop(0, 16, step, jnp.zeros((8, 512), f32))
    proj_out[:, :384] = total[:4, :384]
    proj_out[:, 384:] = total[4:, :384]
    small = total[0:1, 384:] + total[1:2, 384:]
    starts = [120, 124] + [8 * k for k in range(7)] + [56, 64, 96, 72, 80, 88]
    for start, out in zip(starts, vector_outs):
        out[...] = small[0, start : start + out.shape[0]]


def to_peers(x, axis, groups=None):
    return lax.all_to_all(x, axis, 0, 0, tiled=True, axis_index_groups=groups)


Y_GROUPS = [[0, 2, 4, 6], [1, 3, 5, 7]]


def local(
    feats, lengths, skip_flag, cotangent, input_gain, input_shift, proj_weight, proj_bias, conv_weight, conv_bias,
    encoder_gain, encoder_shift, qkv_weight, query_bias, value_bias, output_weight, output_bias, middle_gain,
    middle_shift, inner_weight, inner_bias, outer_weight, outer_bias, final_gain, final_shift,
):
    seq = lax.axis_index("seq")
    rows_in = feats.reshape(ROWS, C_IN)
    cot = cotangent.reshape(ROWS, D)

    masked, conv_send = call(
        project_kernel,
        [Spill((ROWS, D), f32), shape((ROWS, D), bf16)],
        Smem(lengths), Hbm(rows_in), Hbm(input_gain), Hbm(input_shift), Hbm(proj_weight), Hbm(proj_bias),
        flops=2 * ROWS * C_IN * D, name="project", scratch=[TRANSPOSE_SCRATCH],
    )
    conv_x = to_peers(conv_send, "seq")
    own_taps = lax.dynamic_slice_in_dim(conv_weight, seq * GW, GW, axis=0)
    taps = own_taps.transpose(0, 2, 1).reshape(GW, KW * GW)
    band = pltpu.VMEM((D, TAP_BLOCKS * D), bf16)
    conv_flops = 2 * ROWS * D * D * TAP_BLOCKS
    (conv_y,) = call(
        conv_kernel, [shape((ROWS, D), bf16)], Hbm(conv_x), Hbm(taps), scratch=[band], flops=conv_flops, name="conv", mib=24,
    )
    conv_back = to_peers(conv_y, "seq").reshape(GROUPS, 8, D)
    conv_pre, hidden, qkv_send, hidden_send = call(
        qkv_kernel,
        [
            Spill((ROWS, D), f32), Spill((ROWS, D), f32), Spill((SEQ, 192, 128), bf16), Spill((ROWS, 1024), bf16),
        ],
        conv_back, Hbm(masked), Hbm(conv_bias), Hbm(encoder_gain), Hbm(encoder_shift), Hbm(qkv_weight), Hbm(query_bias),
        Hbm(value_bias), flops=2 * ROWS * D * (3 * D + 1024), name="qkv", scratch=[TRANSPOSE_SCRATCH],
    )
    qkv = to_peers(qkv_send, "seq")
    hidden_all = lax.all_gather(hidden_send, "seq", axis=0, tiled=True).reshape(SEQ, 2, 64, 1024)
    attended, logs = call(
        attend_kernel, [shape((1024, 128), bf16), Spill((1024, 128), f32)], Smem(lengths), Hbm(qkv),
        flops=8 * 1024 * 1024 * 128, name="attend",
    )
    att_recv = to_peers(attended.reshape(SEQ, 64, 128), "seq")
    activations, grad_att_send, gmi, pair_send, pair_own, small_a = call(
        middle_kernel,
        [
            Spill((ROWS, D), bf16), Spill((SEQ, 64, 128), bf16), Spill((ROWS, D), f32),
            shape((ROWS, S_END), bf16), shape((ROWS, O_END), bf16), Spill((16, D), f32),
        ],
        Smem(skip_flag), att_recv, Hbm(hidden), Hbm(cot), Raw(output_weight), Hbm(output_bias), Hbm(middle_gain),
        Hbm(middle_shift), Raw(inner_weight), Hbm(inner_bias), Raw(outer_weight), Hbm(outer_bias), Hbm(final_gain),
        Hbm(final_shift),
        scratch=[
            pltpu.VMEM((ROWS, FF), bf16), pltpu.VMEM((ROWS, FF), f32), pltpu.VMEM((D, D), bf16),
            pltpu.VMEM((D, FF), bf16), pltpu.VMEM((FF, D), bf16), pltpu.SemaphoreType.DMA((9,)),
        ],
        flops=2 * ROWS * (4 * D * FF + 2 * D * D), name="middle", mib=32,
    )
    swap = [(i, i ^ 1) for i in range(8)]
    pair_got = lax.ppermute(pair_send, "batch", swap)
    grad_att = to_peers(grad_att_send, "seq").reshape(1024, 128)
    (dense,) = call(
        dense_grads_kernel, [Spill((SEQ, Y_END, D), bf16, parts=4)], pair_own, pair_send, pair_got,
        flops=2 * 256 * D * 3456, name="dense_grads", mib=24,
    )
    dense_part = lax.psum_scatter(dense.reshape(SEQ * Y_END, D), "seq", scatter_dimension=0, tiled=True)

    (grad_qkv_send,) = call(
        attend_back_kernel, [Spill((SEQ, 192, 128), bf16)], Smem(lengths), Hbm(qkv), grad_att, Hbm(logs),
        scratch=[pltpu.VMEM((1024, 128), f32)] * 2, flops=20 * 1024 * 1024 * 128, name="attend_back",
    )
    grad_qkv = to_peers(grad_qkv_send, "seq")
    (qkv_sums,) = call(
        head_grads_kernel, [Spill((SEQ * QKV_ROWS, D), bf16)], Hbm(hidden_all), Hbm(grad_qkv_send),
        flops=2 * 1024 * 1024 * 384, name="head_grads", mib=24,
    )
    grad_summed, back_send, small_b = call(
        qkv_back_kernel,
        [Spill((ROWS, D), f32), shape((SEQ, CHUNK, D), bf16), Spill((8, D), f32)],
        grad_qkv, Hbm(gmi), Hbm(conv_pre), Hbm(masked), Hbm(encoder_gain), Hbm(qkv_weight), Hbm(qkv_sums),
        scratch=[TRANSPOSE_SCRATCH, pltpu.VMEM((ROWS, D), f32)], flops=2 * ROWS * D * 3 * D, name="qkv_back",
    )
    back_got = to_peers(back_send, "seq")
    back_other = lax.ppermute(back_got, "batch", swap)
    x_other = lax.ppermute(conv_x, "batch", swap)
    (grad_x,) = call(
        conv_back_kernel, [shape((ROWS, D), bf16)], Hbm(back_got), Hbm(taps), scratch=[band], flops=conv_flops,
        name="conv_back", mib=24,
    )
    grad_x_got = to_peers(grad_x, "seq").reshape(GROUPS, 8, D)
    x_other, _ = lax.optimization_barrier((x_other, grad_x))
    qkv_chunks, *tap_chunks = call(
        conv_weight_kernel, [shape((4, 24, D), bf16)] + [Spill((GW, D), bf16) for _ in range(4)], Hbm(back_got), Hbm(back_other), Hbm(conv_x), Hbm(x_other),
        scratch=[
            pltpu.VMEM((384, TAP_BLOCKS * D), f32), pltpu.VMEM((24, TAP_BLOCKS * D), f32), pltpu.VMEM((192, 128), f32),
            pltpu.VMEM((4, GW, D), bf16),
        ],
        flops=conv_flops, name="conv_grads", mib=32,
    )
    dense_part, grad_x_got = lax.optimization_barrier((dense_part, grad_x_got))
    (hop_send,) = call(hop_kernel, [Spill((4 * HOP, D), bf16)], Hbm(qkv_chunks), Hbm(dense_part), name="hop")
    hop_send, small_b, *tap_chunks = lax.optimization_barrier((hop_send, small_b, *tap_chunks))
    hop_got = lax.psum_scatter(hop_send, "batch", scatter_dimension=0, tiled=True, axis_index_groups=Y_GROUPS)
    grad_qkv_weight, grad_inner_weight, grad_outer_weight, grad_output_weight = call(
        hop_sum_kernel,
        [shape((6, 3 * D), f32), shape((6, FF), f32), shape((24, D), f32), shape((6, D), f32)],
        Hbm(hop_got), name="hop_sum",
    )
    tap_got = []
    for k, piece in enumerate(tap_chunks):
        moves = [
            (b * 16 + g, (g // 2) * 16 + 8 * (g % 2) + 2 * ((b // 2 + k) % 4) + b % 2)
            for b in range(8)
            for g in range(GROUPS)
        ]
        tap_got.append(Hbm(lax.ppermute(piece, ("batch", "seq"), moves)))
    (tap_own,) = call(conv_sum_kernel, [shape((GW, D), f32)], *tap_got, name="conv_sum")
    grad_conv_weight = tap_own.reshape(6, KW, GW).transpose(0, 2, 1)

    grad_feats, tail = call(
        feats_back_kernel,
        [Spill((ROWS, C_IN), f32), shape((1024, 512), bf16)],
        Smem(lengths), grad_x_got, Hbm(grad_summed), Hbm(rows_in), Hbm(input_gain), Hbm(input_shift),
        Hbm(proj_weight), Hbm(small_a), Hbm(small_b),
        scratch=[TRANSPOSE_SCRATCH, pltpu.VMEM((1024, 128), f32)], flops=4 * ROWS * C_IN * D, name="feats_back",
    )
    tail_got = to_peers(tail, ("batch", "seq"))
    widths = [4, 4] + [6] * 9 + [24] + [6] * 3
    (
        grad_proj_weight, g_in_g, g_in_s, g_proj_b, g_conv_b, g_enc_g, g_enc_s, g_q_b, g_v_b, g_out_b, g_mid_g, g_mid_s,
        g_inner_b, g_outer_b, g_fin_g, g_fin_s,
    ) = call(
        tail_sum_kernel, [shape((4, D), f32)] + [shape((w,), f32) for w in widths], Hbm(tail_got.reshape(128, 8, 512)),
        name="tail_sum",
    )
    return (
        activations.reshape(2, 64, D), grad_feats.reshape(2, 64, C_IN), g_in_g, g_in_s, grad_proj_weight, g_proj_b,
        grad_conv_weight, g_conv_b, g_enc_g, g_enc_s, grad_qkv_weight, g_q_b, g_v_b, grad_output_weight, g_out_b,
        g_mid_g, g_mid_s, grad_inner_weight, g_inner_b, grad_outer_weight, g_outer_b, g_fin_g, g_fin_s,
    )


def solution(mesh):
    split = P("batch", "seq", None)
    both = ("batch", "seq")
    placed = (split, P("batch"), P("batch"), split) + (P(),) * 21
    row, matrix = P(both), P(both, None)
    return jax.shard_map(
        local,
        mesh=mesh,
        in_specs=placed,
        out_specs=(
            split, split, row, row, matrix, row, P(both, None, None), row, row, row, matrix, row, row, matrix, row,
            row, row, matrix, row, matrix, row, row, row,
        ),
        check_vma=False,
    )
```

```python
import functools

import jax
import jax.numpy as jnp
from jax import lax
from jax.experimental import pallas as pl
from jax.experimental.pallas import tpu as pltpu
from jax.sharding import PartitionSpec as P

f32 = jnp.float32
bf16 = jnp.bfloat16
i32 = jnp.int32

norm_eps = 1e-05
head_scale = 0.125
neg_fill = -1e30

D = 768
C_IN = 512
FF = 3072
GROUPS = 16
GW = 48
KW = 128
SUPER = 16
TAP_BLOCKS = 9
ROWS = 128
SEQ = 16
PAIRS = 6
MIB = 1024 * 1024
TRANSPOSE_SCRATCH = pltpu.VMEM((D, 128), f32)

def nn(a, b):
    return lax.dot_general(a, b, (((1,), (0,)), ((), ())), preferred_element_type=f32)


def nt(a, b):
    return lax.dot_general(a, b, (((1,), (1,)), ((), ())), preferred_element_type=f32)


def tn(a, b):
    return lax.dot_general(a, b, (((0,), (0,)), ((), ())), preferred_element_type=f32)


def iota(shape, dim):
    return lax.broadcasted_iota(i32, shape, dim)


def int_div(x, c):
    return ((x.astype(f32) + 0.5) * (1.0 / c)).astype(i32)


def stats(x):
    c = x - jnp.mean(x, axis=-1, keepdims=True)
    r = lax.rsqrt(jnp.mean(c * c, axis=-1, keepdims=True) + norm_eps)
    return c * r, r


def norm_back(xhat, r, gain, g):
    e = g * gain
    dx = r * (e - jnp.mean(e, axis=-1, keepdims=True) - xhat * jnp.mean(e * xhat, axis=-1, keepdims=True))
    return dx, jnp.sum(g * xhat, axis=0, keepdims=True), jnp.sum(g, axis=0, keepdims=True)


def normal(x):
    bell = jnp.exp(-0.5 * x * x)
    t = 1.0 / (1.0 + (0.3275911 * 0.7071067811865476) * jnp.abs(x))
    poly = t * (0.127414796 + t * (-0.142248368 + t * (0.7107068705 + t * (-0.7265760135 + t * 0.5307027145))))
    tail = poly * bell
    return jnp.where(x < 0, tail, 1.0 - tail), 0.3989422804014327 * bell


def gelu(x):
    return x * normal(x)[0]


def gelu_slope(x):
    c, density = normal(x)
    return c + x * density


def col_sum(x):
    return jnp.sum(x.astype(f32), axis=0, keepdims=True)


def vec(lazy):
    ref = lazy()
    return ref[...].astype(f32).reshape(1, ref.shape[0])


def swap_blocks(xs):
    ys = [pltpu.roll(x, f * GW, 1) if f else x for f, x in enumerate(xs)]
    lane = iota((8, 128), 1)
    outs = []
    for g in range(GROUPS):
        tiles = []
        for v in range(D // 128):
            lo, hi = (128 * v) // GW, (128 * v + 127) // GW
            tile = ys[(lo - g) % 16][:, v * 128 : (v + 1) * 128]
            for q in range(lo + 1, hi + 1):
                tile = jnp.where(lane >= q * GW - 128 * v, ys[(q - g) % 16][:, v * 128 : (v + 1) * 128], tile)
            tiles.append(tile)
        w = jnp.concatenate(tiles, axis=1)
        outs.append(pltpu.roll(w, D - g * GW, 1) if g else w)
    return outs


LANE_TILES = D // 128


def rows_to_groups(x, scratch, out_ref):
    for v in range(LANE_TILES):
        scratch[v * ROWS : (v + 1) * ROWS, :] = x[:, v * 128 : (v + 1) * 128]
    outs = swap_blocks(
        [
            jnp.concatenate([scratch[pl.ds(v * ROWS + f, 8, stride=SUPER), :] for v in range(LANE_TILES)], axis=1)
            for f in range(SUPER)
        ]
    )
    for g in range(0, GROUPS, 2):
        out_ref[g * 8 : g * 8 + 16, :] = jnp.concatenate(outs[g : g + 2], axis=0).astype(out_ref.dtype)


def groups_to_rows(in_ref, scratch):
    xs = [in_ref[g].astype(f32)[:8] for g in range(GROUPS)]
    for f, x in enumerate(swap_blocks(xs)):
        for v in range(LANE_TILES):
            scratch[pl.ds(v * ROWS + f, 8, stride=SUPER), :] = x[:, v * 128 : (v + 1) * 128]
    return jnp.concatenate([scratch[v * ROWS : (v + 1) * ROWS, :] for v in range(LANE_TILES)], axis=1)


class Hbm:
    def __init__(self, array):
        self.array = array


class Raw(Hbm):
    pass


class Smem(Hbm):
    pass


class Spill:
    def __init__(self, dims, dtype, parts=1):
        self.struct, self.parts = jax.ShapeDtypeStruct(dims, dtype), parts


class Flusher:
    def __init__(self, ref, target, sems, base, copies):
        self.ref, self.target, self.sems, self.next, self.copies = ref, target, sems, base, copies

    def put(self, value):
        self.ref[...] = value
        self.flush()

    def flush(self, *index):
        src, dst = (self.ref.at[index], self.target.at[index]) if index else (self.ref, self.target)
        copy = pltpu.make_async_copy(src, dst, self.sems.at[self.next])
        copy.start()
        self.next += 1
        self.copies.append(copy)


class Lazy:
    def __init__(self, copy, ref):
        self.copy, self.ref, self.waited = copy, ref, False

    def __call__(self):
        if not self.waited:
            self.copy.wait()
            self.waited = True
        return self.ref


def call(body, outs, *args, scratch=(), flops=0, name=None, mib=16):
    fetched = [k for k, a in enumerate(args) if type(a) in (Hbm, Smem)]
    spilled = [k for k, o in enumerate(outs) if isinstance(o, Spill)]
    arrays = [
        pltpu.with_memory_space_constraint(a.array, pltpu.HBM) if isinstance(a, Hbm) and not isinstance(a, Smem) else getattr(a,'array',a) for a in args
    ]
    structs = [o.struct if isinstance(o, Spill) else o for o in outs]
    near = {Hbm: pltpu.VMEM, Smem: pltpu.SMEM}
    own = [near[type(args[k])](arrays[k].shape, arrays[k].dtype) for k in fetched]
    own += [pltpu.VMEM(structs[k].shape, structs[k].dtype) for k in spilled]
    sem_count = len(fetched) + sum(outs[k].parts for k in spilled)
    if sem_count:
        own.append(pltpu.SemaphoreType.DMA((sem_count,)))

    def wrapped(*refs):
        n_in, n_out = len(args), len(outs)
        ins, out_refs, rest = list(refs[:n_in]), list(refs[n_in : n_in + n_out]), list(refs[n_in + n_out :])
        extra, rest = rest[: len(own)], rest[len(own) :]
        lazies, flushed = [], []
        for slot, k in enumerate(fetched):
            copy = pltpu.make_async_copy(ins[k], extra[slot], extra[-1].at[slot])
            copy.start()
            ins[k] = Lazy(copy, extra[slot])
            lazies.append(ins[k])
        base = len(fetched)
        for slot, k in enumerate(spilled):
            out_refs[k] = Flusher(extra[len(fetched) + slot], out_refs[k], extra[-1], base, flushed)
            base += outs[k].parts
        body(*ins, *out_refs, *rest)
        for lazy in lazies:
            lazy()
        for copy in flushed:
            copy.wait()

    bytes_accessed = sum(a.size * a.dtype.itemsize for a in arrays) + sum(o.size * o.dtype.itemsize for o in structs)
    return pl.pallas_call(
        wrapped,
        out_shape=[pltpu.HBM(o.struct.shape, o.struct.dtype) if isinstance(o, Spill) else o for o in outs],
        in_specs=[pl.BlockSpec(memory_space=pltpu.HBM if isinstance(a, Hbm) else pltpu.VMEM) for a in args],
        out_specs=[pl.BlockSpec(memory_space=pltpu.HBM if isinstance(o, Spill) else pltpu.VMEM) for o in outs],
        scratch_shapes=own + list(scratch),
        compiler_params=pltpu.CompilerParams(vmem_limit_bytes=mib * MIB),
        cost_estimate=pl.CostEstimate(flops=flops, bytes_accessed=bytes_accessed, transcendentals=0),
        name=name,
    )(*arrays)


def fetch(sems, *pairs):
    copies = [pltpu.make_async_copy(src, dst, sems.at[k]) for k, (src, dst) in enumerate(pairs)]
    for copy in copies:
        copy.start()
    return copies


def shape(dims, dtype):
    return jax.ShapeDtypeStruct(dims, dtype)


def live_rows(lengths):
    row = iota((ROWS, 1), 0)
    frame = (row & 63) + lax.axis_index("seq") * 64
    ref = lengths()
    length = jnp.where(row < 64, ref[0], ref[1])
    return (frame < length).astype(f32)


def head_utterance():
    return (lax.axis_index("seq") >= PAIRS).astype(i32)


def core_index():
    return lax.axis_index("batch") & 1


def project_kernel(lengths, feats, gain, shift, weight, bias, masked_out, send_out, scratch):
    xhat, _ = stats(feats()[...].astype(f32))
    normed = (xhat * vec(gain) + vec(shift)).astype(bf16)
    masked = (nn(normed, weight()[...]) + vec(bias)) * live_rows(lengths)
    masked_out.put(masked)
    rows_to_groups(masked, scratch, send_out)


def make_band(taps, out):
    flat = jnp.concatenate([taps[...].astype(f32), jnp.zeros((GW, D), f32)], axis=1)
    for f in range(SUPER):
        rolled = pltpu.roll(flat, f * GW, 1) if f else flat
        out[f * GW : (f + 1) * GW, :] = rolled.astype(bf16)


def shift_matrix(delta):
    r, c = iota((ROWS, ROWS), 0), iota((ROWS, ROWS), 1)
    frame_r = (r >> 3) * 4 + (r & 3)
    frame_c = (c >> 3) * 4 + (c & 3)
    return ((frame_c == frame_r + delta) & ((r & 4) == (c & 4))).astype(f32).astype(bf16)


def conv_kernel(x_in, taps, out, w):
    make_band(taps(), w)
    x = x_in()[...]
    windows = [nn(shift_matrix(i - 4), x).astype(bf16) for i in range(TAP_BLOCKS)]
    out[...] = nt(jnp.concatenate(windows, axis=1), w[...]).astype(out.dtype)


CHUNK = 56


def conv_part(got, start):
    return jnp.concatenate([got[g, start : start + 8, :].astype(f32) for g in range(GROUPS)], axis=0)


def conv_back_kernel(lengths, got_in, taps, out, w):
    make_band(taps(), w)
    got = got_in()
    grad = conv_part(got, 0).astype(bf16)
    total = conv_part(got, 8)
    for i in range(TAP_BLOCKS):
        total += nn(nn(shift_matrix(4 - i), grad).astype(bf16), w[:, i * D : (i + 1) * D])
    row, f = iota((ROWS, D), 0), int_div(iota((1, D), 1), GW)
    ref = lengths()
    length = jnp.where((row & 4) == 0, ref[0], ref[1])
    live = (row >> 3) * 64 + (row & 3) * SUPER + f < length
    out[...] = jnp.where(live, total, 0.0).astype(bf16)


def conv_weight_kernel(got_in, other_in, x_in, x_other, *rest):
    tap_outs, (wide, acc, spread, chunks) = rest[:4], rest[4:]
    core = core_index()
    src, dst = iota((D, 384), 0), iota((1, 384), 1)
    f = int_div(dst, 24)
    y = int_div(dst - 24 * f, 6)
    own_taps = (src == f * GW + (2 * y + core) * 6 + (dst - 24 * f - 6 * y)).astype(f32).astype(bf16)
    grads, windows = [], []
    for ref, values in ((got_in(), x_in()), (other_in(), x_other())):
        grads.append(nn(conv_part(ref, 0).astype(bf16), own_taps).astype(bf16))
        x = values[...]
        windows.append(
            jnp.concatenate([nn(shift_matrix(i - 4), x).astype(bf16) for i in range(TAP_BLOCKS)], axis=1)
        )
    width = TAP_BLOCKS * D
    wide[...] = tn(jnp.concatenate(grads, axis=0), jnp.concatenate(windows, axis=0))
    acc[:, width - 384 :] = jnp.zeros((24, 384), f32)
    for f in range(7, -1, -1):
        acc[:, : width - 384] = (
            (pltpu.roll(acc[...], width - GW, 1)[:, : width - 384] if f < 7 else 0.0)
            + wide[f * 24 : f * 24 + 24, : width - 384]
            + wide[(f + 8) * 24 : (f + 8) * 24 + 24, 384:]
        )
    for v in range(LANE_TILES):
        lanes = slice(v * 128, (v + 1) * 128)
        for i in range(8):
            spread[pl.ds(i, 24, stride=8), :] = acc[:, i * D + v * 128 : i * D + (v + 1) * 128]
        for y in range(4):
            chunks[y, :, lanes] = spread[y * GW : (y + 1) * GW, :].astype(bf16)
    own_y = lax.axis_index("batch") >> 1
    for k, tap_out in enumerate(tap_outs):
        tap_out.put(chunks[(own_y + k) & 3])


def conv_sum_kernel(*refs):
    total = refs[0]()[...].astype(f32)
    for ref in refs[1:-1]:
        total += ref()[...].astype(f32)
    refs[-1][...] = total


def dense_sum_kernel(total_in, inner_out, outer_out, output_out):
    total = total_in()[...].astype(f32)
    for q in range(4):
        inner_out[:, q * D : (q + 1) * D] = total[q * 6 : q * 6 + 6]
    output_out[...] = total[24:30]
    outer_out[...] = total[32:]


def qkv_kernel(
    conv, masked, conv_bias, gain, shift, weight, query_bias, value_bias, feats,
    pre_out, hidden_out, send_out, rows_out, scratch,
):
    pre = groups_to_rows(conv, scratch) + vec(conv_bias)
    pre_out.put(pre)
    xhat, _ = stats(masked()[...] + gelu(pre))
    hidden = xhat * vec(gain) + vec(shift)
    hidden_out.put(hidden)
    hidden_b = hidden.astype(bf16)
    rows_out.ref[:, :D] = hidden_b
    rows_out.ref[:, D:] = feats()[...]
    rows_out.flush()
    zero = jnp.zeros((1, D), f32)
    send = send_out.ref
    for slot, (block, bias) in enumerate(((1, zero), (2, vec(value_bias)), (0, vec(query_bias)))):
        part = (nn(hidden_b, weight()[:, block * D : (block + 1) * D]) + bias).astype(bf16)
        for u in range(2):
            for pair in range(PAIRS):
                send[u * PAIRS + pair, slot * 64 : (slot + 1) * 64, :] = part[
                    u * 64 : (u + 1) * 64, pair * 128 : (pair + 1) * 128
                ]
        part_rows = slice(slot * 64, (slot + 1) * 64)
        send[2 * PAIRS :, part_rows, :] = jnp.zeros((SEQ - 2 * PAIRS, 64, 128), bf16)
        send_out.flush(slice(None), part_rows)


Q_BLOCK = 512


def columns(*values):
    rows = max(v.shape[0] for v in values)
    lane = iota((rows, 128), 1)
    out = jnp.zeros((rows, 128), f32)
    for k, v in enumerate(values):
        out = jnp.where(lane == k, v, out)
    return out.astype(bf16)


def three_terms(x):
    high = x.astype(bf16).astype(f32)
    mid = (x - high).astype(bf16).astype(f32)
    return high, mid, x - high - mid


def key_bias(lengths):
    ref = lengths()
    length = jnp.where(head_utterance() == 0, ref[0], ref[1])
    return jnp.where(iota((1024, 1), 0) < length, 0.0, neg_fill)


def attend_kernel(lengths, qkv_in, out, log_spill, out_spill):
    qkv, log_out, full_out = qkv_in(), log_spill.ref, out_spill.ref
    keys = jnp.concatenate([qkv[:, 0:64, :].reshape(1024, 128), columns(key_bias(lengths))], axis=1)
    values = jnp.concatenate([qkv[:, 64:128, :].reshape(1024, 128), columns(jnp.ones((1024, 1), f32))], axis=1)
    left = iota((Q_BLOCK, 128), 1) < 64
    per = Q_BLOCK // 64
    ones = columns(jnp.ones((Q_BLOCK, 1), f32))

    def step(n, carry):
        query = qkv[pl.ds(n * per, per), 128:192, :].reshape(Q_BLOCK, 128) * head_scale
        parts, logs = [], []
        for head in range(2):
            own = left if head == 0 else ~left
            q_h = jnp.concatenate([jnp.where(own, query, jnp.zeros_like(query)), ones], axis=1)
            scores = nt(q_h, keys)
            top = jnp.max(scores, axis=-1, keepdims=True)
            e = jnp.exp(scores - top).astype(bf16)
            sums = nn(e, values)
            total = sums[:, 128:129]
            parts.append(sums[:, :128] * (1.0 / total))
            logs.append(top + jnp.log(total))
        rows = pl.ds(pl.multiple_of(n * Q_BLOCK, Q_BLOCK), Q_BLOCK)
        both = jnp.where(left, parts[0], parts[1])
        out[rows, :] = both.astype(bf16)
        full_out[rows, :] = both
        log_out[rows, :] = jnp.where(left, logs[0], logs[1])
        return carry

    lax.fori_loop(0, 1024 // Q_BLOCK, step, 0)
    log_spill.flush()
    out_spill.flush()


def attend_back_kernel(lengths, qkv_in, grad, logs_in, full_in, spill, dk, dv):
    qkv, logs, full, out = qkv_in(), logs_in(), full_in(), spill.ref
    one = jnp.ones((1024, 1), f32)
    keys_only = qkv[:, 0:64, :].reshape(1024, 128)
    keys = jnp.concatenate([keys_only, columns(key_bias(lengths), one, one, one)], axis=1)
    values = jnp.concatenate([qkv[:, 64:128, :].reshape(1024, 128), columns(one, one, one)], axis=1)
    keys_t = keys_only.T
    left = iota((Q_BLOCK, 128), 1) < 64
    top_rows = iota((128, Q_BLOCK), 0) < 64
    per = Q_BLOCK // 64
    dk[...] = jnp.zeros_like(dk)
    dv[...] = jnp.zeros_like(dv)

    def step(n, carry):
        query = qkv[pl.ds(n * per, per), 128:192, :].reshape(Q_BLOCK, 128) * head_scale
        rows = pl.ds(pl.multiple_of(n * Q_BLOCK, Q_BLOCK), Q_BLOCK)
        go = grad[rows, :]
        weighted = go.astype(f32) * full[rows, :]
        parts = []
        for head in range(2):
            own = left if head == 0 else ~left
            q_h = jnp.where(own, query, jnp.zeros_like(query))
            g_h = jnp.where(own, go, jnp.zeros_like(go))
            log = logs[rows, head * 64 : head * 64 + 1]
            delta = jnp.sum(jnp.where(own, weighted, 0.0), axis=-1, keepdims=True)
            q_more = jnp.concatenate([q_h, columns(jnp.ones((Q_BLOCK, 1), f32), *three_terms(-log))], axis=1)
            g_more = jnp.concatenate([g_h, columns(*three_terms(-delta))], axis=1)
            probs = jnp.exp(nt(keys, q_more))
            grad_scores = (probs * nt(values, g_more)).astype(bf16)
            parts.append(nn(keys_t, grad_scores))
            dk[...] += nn(grad_scores, q_h)
            dv[...] += nn(probs.astype(bf16), g_h)
        grad_query = (jnp.where(top_rows, parts[0], parts[1]) * head_scale).T.astype(bf16)
        out[pl.ds(n * per, per), 0:64, :] = grad_query.reshape(per, 64, 128)
        return carry

    lax.fori_loop(0, 1024 // Q_BLOCK, step, 0)
    out[:, 64:128, :] = dk[...].astype(bf16).reshape(SEQ, 64, 128)
    out[:, 128:192, :] = dv[...].astype(bf16).reshape(SEQ, 64, 128)
    spill.flush()


def frames_kernel(rows_in, gain, shift, normed_out, high_out, low_out, feats, sem):
    copy = pltpu.make_async_copy(rows_in.at[:, :, :, D : D + C_IN], feats, sem.at[0])
    copy.start()
    copy.wait()
    xhat, _ = stats(feats[...].reshape(2048, C_IN).astype(f32))
    normed_out.put((xhat * vec(gain) + vec(shift)).astype(bf16))
    high = xhat.astype(bf16)
    high_out.put(high)
    low_out.put((xhat - high.astype(f32)).astype(bf16))


def head_grads_kernel(rows_in, grads_in, spill, hidden, sem):
    copy = pltpu.make_async_copy(rows_in.at[:, head_utterance(), :, 0:D], hidden, sem.at[0])
    copy.start()
    grads = grads_in()
    right = jnp.concatenate([grads[:, k * 64 : (k + 1) * 64, :].reshape(1024, 128) for k in range(3)], axis=1)
    dst, src = iota((1024, 1), 0), iota((1024, D), 1)
    row = jnp.where((dst & 7) < 6, (dst >> 3) * 6 + (dst & 7), -1)
    spread = (src == row).astype(f32).astype(bf16)
    copy.wait()
    res = tn(hidden[...].reshape(1024, D), right).astype(bf16)
    spill.put(nn(spread, res).astype(bf16))


def owner_order(core):
    src, dst = iota((D, D), 0), iota((1, D), 1)
    second = dst >= 384
    rest = dst - jnp.where(second, 384, 0)
    which = jnp.where(second, 1 - core, core)
    s = int_div(rest, 24)
    y = int_div(rest - 24 * s, 6)
    j = rest - 24 * s - 6 * y
    return (src == (2 * y + which) * 96 + s * 6 + j).astype(f32).astype(bf16)


S_MID, S_GI, S_INNER, S_GO, S_ATT, S_GA, S_END = 0, 384, 3456, 4992, 5760, 6144, 6912
O_MID, O_INNER, O_ATT, O_END = 0, 384, 1920, 2304


def middle_kernel(
    skip, recv, hidden, cot, out_w_in, out_b, mid_g_in, mid_s_in, inner_w_in, inner_b_in, outer_w_in, outer_b,
    fin_g_in, fin_s_in,
    act_out, grad_att_out, gmi_out, send_out, own_out, small_out,
    act, slope, out_w, inner_w, outer_w, sems,
):
    pairs = [(out_w_in, out_w)]
    for q in range(4):
        cols = slice(q * D, (q + 1) * D)
        pairs += [(inner_w_in.at[:, cols], inner_w.at[:, cols]), (outer_w_in.at[cols, :], outer_w.at[cols, :])]
    copies = fetch(sems, *pairs)
    core = core_index()
    keep = (1 - skip()[0]).astype(f32)
    mid_gain, fin_gain, inner_bias = vec(mid_g_in), vec(fin_g_in), vec(inner_b_in)
    att = jnp.concatenate(
        [jnp.concatenate([recv[u * PAIRS + p] for p in range(PAIRS)], axis=1) for u in range(2)], axis=0
    )
    copies[0].wait()
    middle_in = hidden()[...] + nn(att, out_w[...]) + vec(out_b)
    xm, rm = stats(middle_in)
    middle = xm * mid_gain + vec(mid_s_in)
    middle_b = middle.astype(bf16)
    order = owner_order(core)
    mid = nn(middle_b, order).astype(bf16)
    att_p = nn(att, order).astype(bf16)
    own, send = own_out, send_out

    own[:, O_MID : O_MID + 384] = mid[:, :384]
    own[:, O_ATT : O_ATT + 384] = att_p[:, :384]
    send[:, S_MID : S_MID + 384] = mid[:, 384:]
    send[:, S_ATT : S_ATT + 384] = att_p[:, 384:]
    outer = jnp.zeros((ROWS, D), f32)
    for q in range(4):
        cols = slice(q * D, (q + 1) * D)
        copies[1 + 2 * q].wait()
        pre = nn(middle_b, inner_w[:, cols]) + inner_bias[:, cols]
        c, density = normal(pre)
        inner_b = (pre * c).astype(bf16)
        act[:, cols] = inner_b
        slope[:, cols] = c + pre * density
        copies[2 + 2 * q].wait()
        outer += nn(inner_b, outer_w[cols, :])
    first = core == 0
    for y in range(4):
        even = act[:, 2 * y * 384 : (2 * y + 1) * 384]
        odd = act[:, (2 * y + 1) * 384 : (2 * y + 2) * 384]
        own[:, O_INNER + y * 384 : O_INNER + (y + 1) * 384] = jnp.where(first, even, odd)
        send[:, S_INNER + y * 384 : S_INNER + (y + 1) * 384] = jnp.where(first, odd, even)
    final_in = middle + keep * (outer + vec(outer_b))
    xf, rf = stats(final_in)
    act_out.put((xf * fin_gain + vec(fin_s_in)).astype(bf16))
    gfi, fin_g, fin_s = norm_back(xf, rf, fin_gain, cot()[...].astype(f32))
    grad_outer = (keep * gfi).astype(bf16)
    send[:, S_GO : S_GO + D] = grad_outer
    grad_middle = gfi
    for q in range(4):
        cols = slice(q * D, (q + 1) * D)
        grad_inner = (slope[:, cols] * nt(grad_outer, outer_w[cols, :])).astype(bf16)
        send[:, S_GI + q * D : S_GI + (q + 1) * D] = grad_inner
        small_out.ref[3 + q : 4 + q, :] = col_sum(grad_inner)
        grad_middle += nt(grad_inner, inner_w[:, cols])
    gmi, mid_g, mid_s = norm_back(xm, rm, mid_gain, grad_middle)
    gmi_out.put(gmi)
    grad_attn = gmi.astype(bf16)
    send[:, S_GA : S_GA + D] = grad_attn
    grad_att = nt(grad_attn, out_w[...]).astype(bf16)
    for u in range(2):
        for p in range(PAIRS):
            grad_att_out.ref[u * PAIRS + p] = grad_att[u * 64 : (u + 1) * 64, p * 128 : (p + 1) * 128]
    grad_att_out.ref[2 * PAIRS :] = jnp.zeros((SEQ - 2 * PAIRS, 64, 128), bf16)
    grad_att_out.flush()
    for row, value in ((0, fin_g), (1, fin_s), (2, col_sum(grad_outer)), (7, mid_g), (8, mid_s), (9, col_sum(grad_attn))):
        small_out.ref[row : row + 1, :] = value
    small_out.ref[10:16, :] = jnp.zeros((6, D), f32)
    small_out.flush()


def dense_grads_kernel(own, sent, got, spill):
    out = spill.ref

    def right(start):
        return jnp.concatenate([sent[:, start : start + D], got[:, start : start + D]], axis=0)

    def left(start, theirs, width):
        return jnp.concatenate([own[:, start : start + width], got[:, theirs : theirs + width]], axis=0)

    mid = left(O_MID, S_MID, 384)
    mid_t = mid.T
    sixes = [nn(mid_t, right(S_GI + q * D)).astype(bf16) for q in range(4)]
    sixes.append(nn(left(O_ATT, S_ATT, 384).T, right(S_GA)).astype(bf16))
    outer = nn(left(O_INNER, S_INNER, 1536).T, right(S_GO))
    dst, src = iota((512, 480), 0), iota((1, 480), 1)
    q = int_div(src, 96)
    n = int_div(src - 96 * q, 6)
    j = src - 96 * q - 6 * n
    order = (dst == n * 32 + q * 6 + j).astype(f32).astype(bf16)
    for quarter in range(4):
        rows = slice(quarter * 96, quarter * 96 + 96)
        block = nn(order, jnp.concatenate([x[rows] for x in sixes], axis=0))
        for k in range(4):
            s = quarter * 4 + k
            for y in range(0, 4, 2):
                pieces = []
                for m in (y, y + 1):
                    pieces.append(block[(k * 4 + m) * 32 : (k * 4 + m) * 32 + 32])
                    pieces.append(outer[m * 384 + s * 24 : m * 384 + s * 24 + 24])
                out[s, y * CHUNK : (y + 2) * CHUNK, :] = jnp.concatenate(pieces, axis=0).astype(bf16)
        spill.flush(slice(quarter * 4, quarter * 4 + 4))


def qkv_back_kernel(
    recv, gmi, pre_in, masked, gain_in, weight, send_out, small_out, scratch, conv_out, summed_out
):
    pre = pre_in()[...]
    gain = vec(gain_in)
    xhat, r = stats(masked()[...] + gelu(pre))
    grad_hidden = gmi()[...]
    sums = []
    for slot in range(3):
        part = jnp.concatenate(
            [
                jnp.concatenate([recv[u * PAIRS + p, slot * 64 : (slot + 1) * 64, :] for p in range(PAIRS)], axis=1)
                for u in range(2)
            ],
            axis=0,
        )
        sums.append(col_sum(part))
        grad_hidden += nt(part, weight()[:, slot * D : (slot + 1) * D])
    grad_summed, enc_g, enc_s = norm_back(xhat, r, gain, grad_hidden)
    grad_conv = (gelu_slope(pre) * grad_summed).astype(bf16).astype(f32)
    rows_to_groups(grad_conv, scratch, conv_out)
    rows_to_groups(grad_summed, scratch, summed_out)
    for g in range(GROUPS):
        rows = slice(g * 8, g * 8 + 8)
        send_out[g] = jnp.concatenate([conv_out[rows, :], summed_out[rows, :]], axis=0).astype(bf16)
    for row, value in enumerate((enc_g, enc_s, sums[0], sums[2], jnp.sum(grad_conv, axis=0, keepdims=True))):
        small_out.ref[row : row + 1, :] = value
    small_out.ref[5:8, :] = jnp.zeros((3, D), f32)
    small_out.flush()


def feats_back_kernel(grad, feats, gain_in, weight, feats_out, scratch):
    grad_proj = groups_to_rows(grad, scratch).astype(bf16)
    xhat, r = stats(feats()[...].astype(f32))
    feats_out[...] = norm_back(xhat, r, vec(gain_in), nt(grad_proj, weight()[...]))[0]


def tail_kernel(
    grad_in, normed, high, low, weight, small_a, small_b, qkv_rows, tail_out, frames, spread, by_four
):
    group = lax.axis_index("seq")
    lane = iota((1, 128), 1)
    grad = grad_in()[...].astype(f32)
    for f in range(SUPER):
        start = f * GW // 128 * 128
        tile = jnp.concatenate([grad[:, start : start + 128], grad[:, (start + 128) % D : (start + 128) % D + 128]], axis=1)
        tile = pltpu.roll(tile, 256 - (f * GW - start), 1) if f * GW > start else tile
        frames[pl.ds(f, ROWS, stride=SUPER), :] = jnp.where(lane < GW, tile[:, :128], 0.0)
    grads = frames[...].astype(bf16)
    grads_t = grads.T
    pick = (iota((128, D), 1) == iota((128, D), 0) + group * GW) & (iota((128, 1), 0) < GW)
    own_weight = nt(pick.astype(f32).astype(bf16), weight()[...])
    sums = jnp.sum(grads_t.astype(f32), axis=1, keepdims=True)
    in_g = jnp.sum(own_weight * (nn(grads_t, high()[...]) + nn(grads_t, low()[...])), axis=0, keepdims=True)
    in_s = jnp.sum(own_weight * sums, axis=0, keepdims=True)
    by_four[...] = nn(grads_t, normed()[...]).T
    bias = jnp.sum(grads.astype(f32), axis=0, keepdims=True)
    place = pick.astype(f32).astype(bf16)
    bias_high = bias.astype(bf16)
    bias_low = (bias - bias_high.astype(f32)).astype(bf16)
    proj_b = nn(jnp.concatenate([bias_high] * 8, axis=0), place) + nn(jnp.concatenate([bias_low] * 8, axis=0), place)
    a = lambda k: small_a()[k : k + 1, :]
    b = lambda k: small_b()[k : k + 1, :]
    vectors = [proj_b[:1], b(4), b(0), b(1), b(2), b(3), a(9), a(7), a(8), a(2), a(0), a(1)]
    lane6 = iota((1, D), 1)
    slot6 = lane6 - 6 * int_div(lane6, 6)
    sub = iota((8, D), 0)
    main = jnp.concatenate([jnp.where(slot6 == sub, v, 0.0) for v in vectors] + [jnp.zeros((32, D), f32)], axis=0)
    sub24 = iota((24, D), 0)
    slot24 = lane6 - 24 * int_div(lane6, 24)
    inner = [
        jnp.concatenate(
            [jnp.zeros((96, D), f32), jnp.where(slot24 == sub24, a(3 + k), 0.0), jnp.zeros((8, D), f32)], axis=0
        )
        for k in range(4)
    ]
    lane4, sub4 = iota((8, C_IN), 1) & 3, iota((8, C_IN), 0)
    last = jnp.concatenate(
        [
            jnp.zeros((120, C_IN), f32),
            jnp.where(lane4 == sub4, in_g, 0.0) + jnp.where(lane4 == sub4 - 4, in_s, 0.0),
        ],
        axis=0,
    )
    own = iota((128, D), 0)
    pick6 = (int_div(lane6, 6) == own).astype(f32).astype(bf16)
    pick24 = [(int_div(lane6, 24) + 32 * k == own).astype(f32).astype(bf16) for k in range(4)]
    pick4 = ((iota((1, C_IN), 1) >> 2) == iota((128, C_IN), 0)).astype(f32).astype(bf16)
    spread[...] = jnp.zeros_like(spread)
    terms = [(pick6, main)] + list(zip(pick24, inner)) + [(pick4, last)]
    upper = [(p, m.astype(bf16)) for p, m in terms]
    lower = [(p, (m - h.astype(f32)).astype(bf16)) for (p, m), (_, h) in zip(terms, upper)]
    for k, part in enumerate((upper, lower)):
        spread[pl.ds(k * 1024 + 6, 128, stride=8), :] = functools.reduce(lambda x, y: x + y, [nt(p, m) for p, m in part])
    for k in range(2):
        first, second = [by_four[pl.ds(2 * k + n, 128, stride=4), :] for n in range(2)]
        spread[pl.ds(2048 + 6 + k, 128, stride=8), :] = first + pltpu.roll(second, GW, 1)
    rows = qkv_rows()
    for k in range(3):
        lanes = slice(k * 128, (k + 1) * 128)
        tail_out[:, lanes] = (rows[:, lanes].astype(f32) + spread[k * 1024 : (k + 1) * 1024, :]).astype(bf16)


def tail_sum_kernel(got, qkv_out, proj_out, *vector_outs):
    small = jnp.zeros((1, 128), f32)
    proj = [jnp.zeros((1, D), f32)] * 4
    sums = []
    for d in range(SEQ):
        total = got[d].astype(f32)
        for b in range(1, 8):
            total += got[b * SEQ + d].astype(f32)
        sums.append(total)
        small += total[6:7, :128] + total[6:7, 128:256]
        for k in range(4):
            piece = total[6 + k // 2 : 7 + k // 2, 256:]
            wide = jnp.concatenate([piece, jnp.zeros((1, D - 128), f32)], axis=1)
            shift = (d * GW - (k % 2) * GW) % D
            lane = iota((1, D), 1)
            start = (k % 2) * GW
            wide = jnp.where((lane >= start) & (lane < start + GW), wide, 0.0)
            proj[k] += pltpu.roll(wide, shift, 1) if shift else wide
    for p in range(PAIRS):
        pair = sums[p] + sums[PAIRS + p]
        for k in range(3):
            start = k * D + p * 128
            qkv_out[:, start : start + 128] = pair[:6, k * 128 : (k + 1) * 128]
    for k in range(4):
        proj_out[k : k + 1, :] = proj[k]
    starts = [120, 124] + [8 * k for k in range(7)] + [56, 64, 96, 72, 80, 88]
    for start, out in zip(starts, vector_outs):
        out[...] = small[0, start : start + out.shape[0]]


def to_peers(x, axis, groups=None):
    return lax.all_to_all(x, axis, 0, 0, tiled=True, axis_index_groups=groups)


Y_GROUPS = [[0, 2, 4, 6], [1, 3, 5, 7]]


def local(
    feats, lengths, skip_flag, cotangent, input_gain, input_shift, proj_weight, proj_bias, conv_weight, conv_bias,
    encoder_gain, encoder_shift, qkv_weight, query_bias, value_bias, output_weight, output_bias, middle_gain,
    middle_shift, inner_weight, inner_bias, outer_weight, outer_bias, final_gain, final_shift,
):
    seq = lax.axis_index("seq")
    rows_in = feats.reshape(ROWS, C_IN)
    cot = cotangent.reshape(ROWS, D)

    masked, conv_send = call(
        project_kernel,
        [Spill((ROWS, D), f32), shape((ROWS, D), bf16)],
        Smem(lengths), Hbm(rows_in), Hbm(input_gain), Hbm(input_shift), Hbm(proj_weight), Hbm(proj_bias),
        flops=2 * ROWS * C_IN * D, name="project", scratch=[TRANSPOSE_SCRATCH],
    )
    conv_x = to_peers(conv_send, "seq")
    own_taps = lax.dynamic_slice_in_dim(conv_weight, seq * GW, GW, axis=0)
    taps = own_taps.transpose(0, 2, 1).reshape(GW, KW * GW)
    band = pltpu.VMEM((D, TAP_BLOCKS * D), bf16)
    conv_flops = 2 * ROWS * D * D * TAP_BLOCKS
    (conv_y,) = call(
        conv_kernel, [shape((ROWS, D), bf16)], Hbm(conv_x), Hbm(taps), scratch=[band], flops=conv_flops, name="conv", mib=24,
    )
    conv_back = to_peers(conv_y, "seq").reshape(GROUPS, 8, D)
    conv_pre, hidden, qkv_send, rows_send = call(
        qkv_kernel,
        [
            Spill((ROWS, D), f32), Spill((ROWS, D), f32), Spill((SEQ, 192, 128), bf16, parts=3),
            Spill((ROWS, D + C_IN), bf16),
        ],
        conv_back, Hbm(masked), Hbm(conv_bias), Hbm(encoder_gain), Hbm(encoder_shift), Hbm(qkv_weight), Hbm(query_bias),
        Hbm(value_bias), Hbm(rows_in), flops=2 * ROWS * D * 3 * D, name="qkv", scratch=[TRANSPOSE_SCRATCH],
    )
    qkv = to_peers(qkv_send, "seq")
    rows_all = lax.all_gather(rows_send, "seq", axis=0, tiled=True).reshape(SEQ, 2, 64, D + C_IN)
    attended, logs, attended_full = call(
        attend_kernel, [shape((1024, 128), bf16), Spill((1024, 128), f32), Spill((1024, 128), f32)], Smem(lengths), Hbm(qkv),
        flops=8 * 1024 * 1024 * 128, name="attend",
    )
    att_recv = to_peers(attended.reshape(SEQ, 64, 128), "seq")
    activations, grad_att_send, gmi, pair_send, pair_own, small_a = call(
        middle_kernel,
        [
            Spill((ROWS, D), bf16), Spill((SEQ, 64, 128), bf16), Spill((ROWS, D), f32),
            shape((ROWS, S_END), bf16), shape((ROWS, O_END), bf16), Spill((16, D), f32),
        ],
        Smem(skip_flag), att_recv, Hbm(hidden), Hbm(cot), Raw(output_weight), Hbm(output_bias), Hbm(middle_gain),
        Hbm(middle_shift), Raw(inner_weight), Hbm(inner_bias), Raw(outer_weight), Hbm(outer_bias), Hbm(final_gain),
        Hbm(final_shift),
        scratch=[
            pltpu.VMEM((ROWS, FF), bf16), pltpu.VMEM((ROWS, FF), f32), pltpu.VMEM((D, D), bf16),
            pltpu.VMEM((D, FF), bf16), pltpu.VMEM((FF, D), bf16), pltpu.SemaphoreType.DMA((9,)),
        ],
        flops=2 * ROWS * (4 * D * FF + 2 * D * D), name="middle", mib=32,
    )
    swap = [(i, i ^ 1) for i in range(8)]
    pair_got = lax.ppermute(pair_send, "batch", swap)
    grad_att = to_peers(grad_att_send, "seq").reshape(1024, 128)
    (dense,) = call(
        dense_grads_kernel, [Spill((SEQ, 4 * CHUNK, D), bf16, parts=4)], pair_own, pair_send, pair_got,
        flops=2 * 256 * D * 3456, name="dense_grads", mib=24,
    )
    dense, grad_att = lax.optimization_barrier((dense, grad_att))
    dense_part = lax.psum_scatter(dense.reshape(SEQ * 4 * CHUNK, D), "seq", scatter_dimension=0, tiled=True)

    (grad_qkv_send,) = call(
        attend_back_kernel, [Spill((SEQ, 192, 128), bf16)], Smem(lengths), Hbm(qkv), grad_att, Hbm(logs), Hbm(attended_full),
        scratch=[pltpu.VMEM((1024, 128), f32)] * 2, flops=20 * 1024 * 1024 * 128, name="attend_back",
    )
    grad_qkv = to_peers(grad_qkv_send, "seq")
    (qkv_rows,) = call(
        head_grads_kernel, [Spill((1024, 384), bf16)], Raw(rows_all), Hbm(grad_qkv_send),
        scratch=[pltpu.VMEM((SEQ, 64, D), bf16), pltpu.SemaphoreType.DMA((1,))], flops=4 * 1024 * D * 384,
        name="head_grads", mib=24,
    )
    frames_normed, frames_high, frames_low = call(
        frames_kernel, [Spill((2048, C_IN), bf16) for _ in range(3)], Raw(rows_all), Hbm(input_gain), Hbm(input_shift),
        scratch=[pltpu.VMEM((SEQ, 2, 64, C_IN), bf16), pltpu.SemaphoreType.DMA((1,))], name="frames", mib=32,
    )
    gmi, qkv_rows, frames_normed = lax.optimization_barrier((gmi, qkv_rows, frames_normed))
    back_send, small_b = call(
        qkv_back_kernel, [shape((SEQ, 16, D), bf16), Spill((8, D), f32)],
        grad_qkv, Hbm(gmi), Hbm(conv_pre), Hbm(masked), Hbm(encoder_gain), Hbm(qkv_weight),
        scratch=[TRANSPOSE_SCRATCH] + [pltpu.VMEM((ROWS, D), f32)] * 2, flops=2 * ROWS * D * 3 * D, name="qkv_back",
    )
    back_got = to_peers(back_send, "seq")
    back_other = lax.ppermute(back_got, "batch", swap)
    x_other = lax.ppermute(conv_x, "batch", swap)
    (grad_proj,) = call(
        conv_back_kernel, [shape((ROWS, D), bf16)], Smem(lengths), Hbm(back_got), Hbm(taps), scratch=[band],
        flops=conv_flops, name="conv_back", mib=24,
    )
    grad_proj_got = to_peers(grad_proj, "seq").reshape(GROUPS, 8, D)
    (tail,) = call(
        tail_kernel, [shape((1024, 384), bf16)], Hbm(grad_proj), Hbm(frames_normed), Hbm(frames_high), Hbm(frames_low),
        Hbm(proj_weight), Hbm(small_a), Hbm(small_b), Hbm(qkv_rows),
        scratch=[pltpu.VMEM((2048, 128), f32), pltpu.VMEM((3072, 128), f32), pltpu.VMEM((C_IN, 128), f32)],
        flops=6 * 2048 * C_IN * 128, name="tail", mib=32,
    )
    x_other, _ = lax.optimization_barrier((x_other, tail))
    tap_chunks = call(
        conv_weight_kernel, [Spill((GW, D), bf16) for _ in range(4)], Hbm(back_got), Hbm(back_other), Hbm(conv_x),
        Hbm(x_other),
        scratch=[
            pltpu.VMEM((384, TAP_BLOCKS * D), f32), pltpu.VMEM((24, TAP_BLOCKS * D), f32), pltpu.VMEM((192, 128), f32),
            pltpu.VMEM((4, GW, D), bf16),
        ],
        flops=conv_flops, name="conv_grads", mib=32,
    )
    tail, grad_proj_got, *tap_chunks = lax.optimization_barrier((tail, grad_proj_got, *tap_chunks))
    tap_got = []
    for k, piece in enumerate(tap_chunks):
        moves = [
            (b * 16 + g, (g // 2) * 16 + 8 * (g % 2) + 2 * ((b // 2 + k) % 4) + b % 2)
            for b in range(8)
            for g in range(GROUPS)
        ]
        tap_got.append(lax.ppermute(piece, ("batch", "seq"), moves))
    tail_got = to_peers(tail, ("batch", "seq"))
    (tap_own,) = call(conv_sum_kernel, [shape((GW, D), f32)], *[Hbm(x) for x in tap_got], name="conv_sum")
    grad_conv_weight = tap_own.reshape(6, KW, GW).transpose(0, 2, 1)
    dense_own = lax.psum_scatter(dense_part, "batch", scatter_dimension=0, tiled=True, axis_index_groups=Y_GROUPS)
    (grad_feats,) = call(
        feats_back_kernel, [shape((ROWS, C_IN), f32)], grad_proj_got, Hbm(rows_in), Hbm(input_gain), Hbm(proj_weight),
        scratch=[TRANSPOSE_SCRATCH], flops=2 * ROWS * C_IN * D, name="feats_back",
    )
    grad_inner_weight, grad_outer_weight, grad_output_weight = call(
        dense_sum_kernel, [shape((6, FF), f32), shape((24, D), f32), shape((6, D), f32)], Hbm(dense_own),
        name="dense_sum",
    )
    widths = [4, 4] + [6] * 9 + [24] + [6] * 3
    (
        grad_qkv_weight, grad_proj_weight, g_in_g, g_in_s, g_proj_b, g_conv_b, g_enc_g, g_enc_s, g_q_b, g_v_b, g_out_b, g_mid_g, g_mid_s,
        g_inner_b, g_outer_b, g_fin_g, g_fin_s,
    ) = call(
        tail_sum_kernel, [shape((6, 3 * D), f32), shape((4, D), f32)] + [shape((w,), f32) for w in widths],
        tail_got.reshape(128, 8, 384),
        name="tail_sum",
    )
    return (
        activations.reshape(2, 64, D), grad_feats.reshape(2, 64, C_IN), g_in_g, g_in_s, grad_proj_weight, g_proj_b,
        grad_conv_weight, g_conv_b, g_enc_g, g_enc_s, grad_qkv_weight, g_q_b, g_v_b, grad_output_weight, g_out_b,
        g_mid_g, g_mid_s, grad_inner_weight, g_inner_b, grad_outer_weight, g_outer_b, g_fin_g, g_fin_s,
    )


def solution(mesh):
    split = P("batch", "seq", None)
    both = ("batch", "seq")
    placed = (split, P("batch"), P("batch"), split) + (P(),) * 21
    row, matrix = P(both), P(both, None)
    return jax.shard_map(
        local,
        mesh=mesh,
        in_specs=placed,
        out_specs=(
            split, split, row, row, matrix, row, P(both, None, None), row, row, row, matrix, row, row, matrix, row,
            row, row, matrix, row, matrix, row, row, row,
        ),
        check_vma=False,
    )
```

```python
import functools

import jax
import jax.numpy as jnp
from jax import lax
from jax.experimental import pallas as pl
from jax.experimental.pallas import tpu as pltpu
from jax.sharding import PartitionSpec as P

f32 = jnp.float32
bf16 = jnp.bfloat16
i32 = jnp.int32

norm_eps = 1e-05
head_scale = 0.125
neg_fill = -1e30

D = 768
C_IN = 512
FF = 3072
GROUPS = 16
GW = 48
KW = 128
SUPER = 8
SW = SUPER * GW
TAP_BLOCKS = 17
BAND = TAP_BLOCKS * SW
ROWS = 128
SEQ = 16
PAIRS = 6
MIB = 1024 * 1024
TRANSPOSE_SCRATCH = pltpu.VMEM((D, 128), f32)

def nn(a, b):
    return lax.dot_general(a, b, (((1,), (0,)), ((), ())), preferred_element_type=f32)


def nt(a, b):
    return lax.dot_general(a, b, (((1,), (1,)), ((), ())), preferred_element_type=f32)


def tn(a, b):
    return lax.dot_general(a, b, (((0,), (0,)), ((), ())), preferred_element_type=f32)


def iota(shape, dim):
    return lax.broadcasted_iota(i32, shape, dim)


def int_div(x, c):
    return ((x.astype(f32) + 0.5) * (1.0 / c)).astype(i32)


def stats(x):
    c = x - jnp.mean(x, axis=-1, keepdims=True)
    r = lax.rsqrt(jnp.mean(c * c, axis=-1, keepdims=True) + norm_eps)
    return c * r, r


def norm_back(xhat, r, gain, g):
    e = g * gain
    dx = r * (e - jnp.mean(e, axis=-1, keepdims=True) - xhat * jnp.mean(e * xhat, axis=-1, keepdims=True))
    return dx, jnp.sum(g * xhat, axis=0, keepdims=True), jnp.sum(g, axis=0, keepdims=True)


def normal(x):
    bell = jnp.exp(-0.5 * x * x)
    t = 1.0 / (1.0 + (0.3275911 * 0.7071067811865476) * jnp.abs(x))
    poly = t * (0.127414796 + t * (-0.142248368 + t * (0.7107068705 + t * (-0.7265760135 + t * 0.5307027145))))
    tail = poly * bell
    return jnp.where(x < 0, tail, 1.0 - tail), 0.3989422804014327 * bell


def gelu(x):
    return x * normal(x)[0]


def gelu_slope(x):
    c, density = normal(x)
    return c + x * density


def col_sum(x):
    return jnp.sum(x.astype(f32), axis=0, keepdims=True)


def vec(lazy):
    ref = lazy()
    return ref[...].astype(f32).reshape(1, ref.shape[0])


def swap_blocks(xs):
    ys = [pltpu.roll(x, f * GW, 1) if f else x for f, x in enumerate(xs)]
    lane = iota((16, 128), 1)
    outs = []
    for g in range(SUPER):
        tiles = []
        for v in range(SW // 128):
            lo, hi = (128 * v) // GW, (128 * v + 127) // GW
            tile = ys[(lo - g) % SUPER][:, v * 128 : (v + 1) * 128]
            for q in range(lo + 1, hi + 1):
                tile = jnp.where(lane >= q * GW - 128 * v, ys[(q - g) % SUPER][:, v * 128 : (v + 1) * 128], tile)
            tiles.append(tile)
        w = jnp.concatenate(tiles, axis=1)
        outs.append(pltpu.roll(w, SW - g * GW, 1) if g else w)
    return outs


LANE_TILES = D // 128


def rows_to_groups(x, scratch):
    for v in range(LANE_TILES):
        scratch[v * ROWS : (v + 1) * ROWS, :] = x[:, v * 128 : (v + 1) * 128]
    outs = []
    for half in range(2):
        tiles = range(half * 3, half * 3 + 3)
        outs += swap_blocks(
            [
                jnp.concatenate([scratch[pl.ds(v * ROWS + f, 16, stride=SUPER), :] for v in tiles], axis=1)
                for f in range(SUPER)
            ]
        )
    return outs


def groups_to_rows(in_ref, scratch):
    for half in range(2):
        xs = [in_ref[half * 8 + g].astype(f32) for g in range(SUPER)]
        for f, x in enumerate(swap_blocks(xs)):
            for v in range(3):
                row = (half * 3 + v) * ROWS + f
                scratch[pl.ds(row, 16, stride=SUPER), :] = x[:, v * 128 : (v + 1) * 128]
    return jnp.concatenate([scratch[v * ROWS : (v + 1) * ROWS, :] for v in range(LANE_TILES)], axis=1)


class Hbm:
    def __init__(self, array):
        self.array = array


class Raw(Hbm):
    pass


class Smem(Hbm):
    pass


class Spill:
    def __init__(self, dims, dtype, parts=1):
        self.struct, self.parts = jax.ShapeDtypeStruct(dims, dtype), parts


class Copy:
    parts = 1

    def __init__(self, dims, dtype, operand):
        self.struct, self.operand = jax.ShapeDtypeStruct(dims, dtype), operand


class Flusher:
    def __init__(self, ref, target, sems, base, copies):
        self.ref, self.target, self.sems, self.next, self.copies = ref, target, sems, base, copies

    def put(self, value):
        self.ref[...] = value
        self.flush()

    def flush(self, *index):
        src, dst = (self.ref.at[index], self.target.at[index]) if index else (self.ref, self.target)
        copy = pltpu.make_async_copy(src, dst, self.sems.at[self.next])
        copy.start()
        self.next += 1
        self.copies.append(copy)


class Lazy:
    def __init__(self, copy, ref):
        self.copy, self.ref, self.waited = copy, ref, False

    def __call__(self):
        if not self.waited:
            self.copy.wait()
            self.waited = True
        return self.ref


def call(body, outs, *args, scratch=(), flops=0, name=None, mib=16):
    fetched = [k for k, a in enumerate(args) if type(a) in (Hbm, Smem)]
    spilled = [k for k, o in enumerate(outs) if isinstance(o, Spill)]
    copied = [k for k, o in enumerate(outs) if isinstance(o, Copy)]
    arrays = [
        pltpu.with_memory_space_constraint(a.array, pltpu.HBM) if isinstance(a, Hbm) and not isinstance(a, Smem) else getattr(a,'array',a) for a in args
    ]
    structs = [o.struct if isinstance(o, (Spill, Copy)) else o for o in outs]
    near = {Hbm: pltpu.VMEM, Smem: pltpu.SMEM}
    own = [near[type(args[k])](arrays[k].shape, arrays[k].dtype) for k in fetched]
    own += [pltpu.VMEM(structs[k].shape, structs[k].dtype) for k in spilled]
    sem_count = len(fetched) + sum(outs[k].parts for k in spilled) + len(copied)
    if sem_count:
        own.append(pltpu.SemaphoreType.DMA((sem_count,)))

    def wrapped(*refs):
        n_in, n_out = len(args), len(outs)
        ins, out_refs, rest = list(refs[:n_in]), list(refs[n_in : n_in + n_out]), list(refs[n_in + n_out :])
        extra, rest = rest[: len(own)], rest[len(own) :]
        lazies, flushed = [], []
        for slot, k in enumerate(fetched):
            copy = pltpu.make_async_copy(ins[k], extra[slot], extra[-1].at[slot])
            copy.start()
            ins[k] = Lazy(copy, extra[slot])
            lazies.append(ins[k])
        base = len(fetched)
        for slot, k in enumerate(spilled):
            out_refs[k] = Flusher(extra[len(fetched) + slot], out_refs[k], extra[-1], base, flushed)
            base += outs[k].parts
        for k in copied:
            out_refs[k] = Flusher(refs[outs[k].operand], out_refs[k], extra[-1], base, flushed)
            base += 1
        body(*ins, *out_refs, *rest)
        for lazy in lazies:
            lazy()
        for copy in flushed:
            copy.wait()

    bytes_accessed = sum(a.size * a.dtype.itemsize for a in arrays) + sum(o.size * o.dtype.itemsize for o in structs)
    return pl.pallas_call(
        wrapped,
        out_shape=[pltpu.HBM(o.struct.shape, o.struct.dtype) if isinstance(o, (Spill, Copy)) else o for o in outs],
        in_specs=[pl.BlockSpec(memory_space=pltpu.HBM if isinstance(a, Hbm) else pltpu.VMEM) for a in args],
        out_specs=[pl.BlockSpec(memory_space=pltpu.HBM if isinstance(o, (Spill, Copy)) else pltpu.VMEM) for o in outs],
        scratch_shapes=own + list(scratch),
        compiler_params=pltpu.CompilerParams(vmem_limit_bytes=mib * MIB),
        cost_estimate=pl.CostEstimate(flops=flops, bytes_accessed=bytes_accessed, transcendentals=0),
        name=name,
    )(*arrays)


def fetch(sems, *pairs):
    copies = [pltpu.make_async_copy(src, dst, sems.at[k]) for k, (src, dst) in enumerate(pairs)]
    for copy in copies:
        copy.start()
    return copies


def shape(dims, dtype):
    return jax.ShapeDtypeStruct(dims, dtype)


def live_rows(lengths):
    row = iota((ROWS, 1), 0)
    frame = (row & 63) + lax.axis_index("seq") * 64
    ref = lengths()
    length = jnp.where(row < 64, ref[0], ref[1])
    return (frame < length).astype(f32)


def head_utterance():
    return (lax.axis_index("seq") >= PAIRS).astype(i32)


def core_index():
    return lax.axis_index("batch") & 1


def project_kernel(lengths, feats, gain, shift, weight, bias, masked_out, send_out, scratch):
    xhat, _ = stats(feats()[...].astype(f32))
    normed = (xhat * vec(gain) + vec(shift)).astype(bf16)
    masked = (nn(normed, weight()[...]) + vec(bias)) * live_rows(lengths)
    masked_out.put(masked)
    for g, x in enumerate(rows_to_groups(masked, scratch)):
        send_out[g] = x.astype(bf16)


def band_rows(taps):
    flat = jnp.concatenate([taps[...].astype(f32), jnp.zeros((GW, SW), f32)], axis=1)
    return [(pltpu.roll(flat, f * GW, 1) if f else flat).astype(bf16) for f in range(SUPER)]


def padded(pieces, scratch):
    for u in range(2):
        scratch[u, 0:8, :] = jnp.zeros((8, SW), f32)
        scratch[u, 136:144, :] = jnp.zeros((8, SW), f32)
        for p, x in enumerate(pieces):
            scratch[u, 8 + p * 8 : 16 + p * 8, :] = x[u * 8 : u * 8 + 8]


def windows(scratch, starts):
    parts = [
        jnp.concatenate([scratch[u, start : start + 128, :] for u in range(2)], axis=0).astype(bf16) for start in starts
    ]
    return jnp.concatenate(parts, axis=1)


def by_seq(x, p):
    return jnp.concatenate([x[u * 128 + p * 8 : u * 128 + p * 8 + 8] for u in range(2)], axis=0)


def conv_kernel(x, taps, out, x_out, w, scratch):
    x_out.flush()
    for f, rows in enumerate(band_rows(taps())):
        w[f * GW : (f + 1) * GW, :] = rows
    padded([x[p].astype(f32) for p in range(SEQ)], scratch)
    res = nt(windows(scratch, range(TAP_BLOCKS)), w[...])
    for p in range(SEQ):
        out[p] = by_seq(res, p).astype(bf16)


CHUNK = 56


def conv_back_kernel(lengths, got_in, taps, out, w, scratch):
    for f, rows in enumerate(band_rows(taps())):
        for i in range(TAP_BLOCKS):
            w[i * SW + f * GW : i * SW + (f + 1) * GW, :] = rows[:, i * SW : (i + 1) * SW]
    got = got_in()
    padded([got[p, :16, :].astype(f32) for p in range(SEQ)], scratch)
    res = nn(windows(scratch, range(16, -1, -1)), w[...])
    row, f = iota((16, SW), 0), int_div(iota((1, SW), 1), GW)
    ref = lengths()
    length = jnp.where(row < 8, ref[0], ref[1])
    for p in range(SEQ):
        total = by_seq(res, p) + got[p, 16:, :].astype(f32)
        live = p * 64 + (row & 7) * SUPER + f < length
        out[p] = jnp.where(live, total, 0.0).astype(bf16)


def conv_weight_kernel(got_in, other_in, x_in, x_other, *rest):
    tap_outs, (wide, acc, spread, chunks, scratch) = rest[:4], rest[4:]
    core = core_index()
    src, dst = iota((SW, 192), 0), iota((1, 192), 1)
    f = int_div(dst, 24)
    y = int_div(dst - 24 * f, 6)
    own_taps = (src == f * GW + (2 * y + core) * 6 + (dst - 24 * f - 6 * y)).astype(f32).astype(bf16)
    grads, parts = [], []
    for k, (got, x) in enumerate(((got_in(), x_in()), (other_in(), x_other()))):
        grad = jnp.concatenate([got[p, :16, :] for p in range(SEQ)], axis=0)
        grad = nn(grad, own_taps)
        grads.append(jnp.concatenate([grad[p * 16 + u * 8 : p * 16 + u * 8 + 8] for u in range(2) for p in range(SEQ)], axis=0))
        padded([x[p].astype(f32) for p in range(SEQ)], scratch.at[k])
        parts.append(windows(scratch.at[k], range(TAP_BLOCKS)))
    wide[...] = nn(jnp.concatenate(grads, axis=0).astype(bf16).T, jnp.concatenate(parts, axis=0))
    acc[...] = wide[7 * 24 :, :]
    for f in range(6, -1, -1):
        acc[...] = pltpu.roll(acc[...], BAND - GW, 1) + wide[f * 24 : f * 24 + 24, :]
    for v in range(LANE_TILES):
        lanes = slice(v * 128, (v + 1) * 128)
        for i in range(8):
            spread[pl.ds(i, 24, stride=8), :] = acc[:, i * D + v * 128 : i * D + (v + 1) * 128]
        for y in range(4):
            chunks[y, :, lanes] = spread[y * GW : (y + 1) * GW, :].astype(bf16)
    own_y = lax.axis_index("batch") >> 1
    for k, tap_out in enumerate(tap_outs):
        tap_out.put(chunks[(own_y + k) & 3])


def conv_sum_kernel(*refs):
    total = refs[0]()[...].astype(f32)
    for ref in refs[1:-1]:
        total += ref()[...].astype(f32)
    refs[-1][...] = total


def dense_sum_kernel(total_in, inner_out, outer_out, output_out):
    total = total_in()[...].astype(f32)
    for q in range(4):
        inner_out[:, q * D : (q + 1) * D] = total[q * 6 : q * 6 + 6]
    output_out[...] = total[24:30]
    outer_out[...] = total[32:]


def qkv_kernel(
    conv, masked, conv_bias, gain, shift, weight, query_bias, value_bias, feats,
    pre_out, hidden_out, send_out, rows_out, scratch,
):
    pre = groups_to_rows(conv, scratch) + vec(conv_bias)
    pre_out.put(pre)
    xhat, _ = stats(masked()[...] + gelu(pre))
    hidden = xhat * vec(gain) + vec(shift)
    hidden_out.put(hidden)
    hidden_b = hidden.astype(bf16)
    rows_out.ref[:, :D] = hidden_b
    rows_out.ref[:, D:] = feats()[...]
    rows_out.flush()
    zero = jnp.zeros((1, D), f32)
    send = send_out.ref
    for slot, (block, bias) in enumerate(((1, zero), (2, vec(value_bias)), (0, vec(query_bias)))):
        part = (nn(hidden_b, weight()[:, block * D : (block + 1) * D]) + bias).astype(bf16)
        for u in range(2):
            for pair in range(PAIRS):
                send[u * PAIRS + pair, slot * 64 : (slot + 1) * 64, :] = part[
                    u * 64 : (u + 1) * 64, pair * 128 : (pair + 1) * 128
                ]
        part_rows = slice(slot * 64, (slot + 1) * 64)
        send[2 * PAIRS :, part_rows, :] = jnp.zeros((SEQ - 2 * PAIRS, 64, 128), bf16)
        send_out.flush(slice(None), part_rows)


Q_BLOCK = 512


def columns(*values):
    rows = max(v.shape[0] for v in values)
    lane = iota((rows, 128), 1)
    out = jnp.zeros((rows, 128), f32)
    for k, v in enumerate(values):
        out = jnp.where(lane == k, v, out)
    return out.astype(bf16)


def three_terms(x):
    high = x.astype(bf16).astype(f32)
    mid = (x - high).astype(bf16).astype(f32)
    return high, mid, x - high - mid


def key_bias(lengths):
    ref = lengths()
    length = jnp.where(head_utterance() == 0, ref[0], ref[1])
    return jnp.where(iota((1024, 1), 0) < length, 0.0, neg_fill)


def attend_kernel(lengths, qkv, out, log_spill, out_spill, copy_spill):
    log_out, full_out = log_spill.ref, out_spill.ref
    copy_spill.flush()
    keys = jnp.concatenate([qkv[:, 0:64, :].reshape(1024, 128), columns(key_bias(lengths))], axis=1)
    values = jnp.concatenate([qkv[:, 64:128, :].reshape(1024, 128), columns(jnp.ones((1024, 1), f32))], axis=1)
    left = iota((1024, 128), 1) < 64
    query = qkv[:, 128:192, :].reshape(1024, 128) * head_scale
    parts, logs = [], []
    for head in range(2):
        own = left if head == 0 else ~left
        q_h = jnp.concatenate([jnp.where(own, query, jnp.zeros_like(query)), columns(jnp.ones((1024, 1), f32))], axis=1)
        scores = nt(q_h, keys)
        top = jnp.max(scores, axis=-1, keepdims=True)
        e = jnp.exp(scores - top).astype(bf16)
        sums = nn(e, values)
        total = sums[:, 128:129]
        parts.append(sums[:, :128] * (1.0 / total))
        logs.append(top + jnp.log(total))
    both = jnp.where(left, parts[0], parts[1])
    out[...] = both.astype(bf16)
    full_out[...] = both
    log_out[...] = jnp.where(left, logs[0], logs[1])
    log_spill.flush()
    out_spill.flush()


def attend_back_kernel(lengths, qkv_in, grad, logs_in, full_in, spill, dk, dv):
    qkv, logs, full, out = qkv_in(), logs_in(), full_in(), spill.ref
    one = jnp.ones((1024, 1), f32)
    keys_only = qkv[:, 0:64, :].reshape(1024, 128)
    keys = jnp.concatenate([keys_only, columns(key_bias(lengths), one, one, one)], axis=1)
    values = jnp.concatenate([qkv[:, 64:128, :].reshape(1024, 128), columns(one, one, one)], axis=1)
    keys_t = keys_only.T
    left = iota((Q_BLOCK, 128), 1) < 64
    top_rows = iota((128, Q_BLOCK), 0) < 64
    per = Q_BLOCK // 64
    dk[...] = jnp.zeros_like(dk)
    dv[...] = jnp.zeros_like(dv)

    def step(n, carry):
        query = qkv[pl.ds(n * per, per), 128:192, :].reshape(Q_BLOCK, 128) * head_scale
        rows = pl.ds(pl.multiple_of(n * Q_BLOCK, Q_BLOCK), Q_BLOCK)
        go = grad[rows, :]
        weighted = go.astype(f32) * full[rows, :]
        parts = []
        for head in range(2):
            own = left if head == 0 else ~left
            q_h = jnp.where(own, query, jnp.zeros_like(query))
            g_h = jnp.where(own, go, jnp.zeros_like(go))
            log = logs[rows, head * 64 : head * 64 + 1]
            delta = jnp.sum(jnp.where(own, weighted, 0.0), axis=-1, keepdims=True)
            q_more = jnp.concatenate([q_h, columns(jnp.ones((Q_BLOCK, 1), f32), *three_terms(-log))], axis=1)
            g_more = jnp.concatenate([g_h, columns(*three_terms(-delta))], axis=1)
            probs = jnp.exp(nt(keys, q_more))
            grad_scores = (probs * nt(values, g_more)).astype(bf16)
            parts.append(nn(keys_t, grad_scores))
            dk[...] += nn(grad_scores, q_h)
            dv[...] += nn(probs.astype(bf16), g_h)
        grad_query = (jnp.where(top_rows, parts[0], parts[1]) * head_scale).T.astype(bf16)
        out[pl.ds(n * per, per), 0:64, :] = grad_query.reshape(per, 64, 128)
        return carry

    lax.fori_loop(0, 1024 // Q_BLOCK, step, 0)
    out[:, 64:128, :] = dk[...].astype(bf16).reshape(SEQ, 64, 128)
    out[:, 128:192, :] = dv[...].astype(bf16).reshape(SEQ, 64, 128)
    spill.flush()


def frames_kernel(rows_in, gain, shift, normed_out, high_out, low_out, feats, sem):
    copy = pltpu.make_async_copy(rows_in.at[:, :, :, D : D + C_IN], feats, sem.at[0])
    copy.start()
    copy.wait()
    xhat, _ = stats(feats[...].reshape(2048, C_IN).astype(f32))
    normed_out.put((xhat * vec(gain) + vec(shift)).astype(bf16))
    high = xhat.astype(bf16)
    high_out.put(high)
    low_out.put((xhat - high.astype(f32)).astype(bf16))


def head_grads_kernel(rows_in, grads_in, spill, hidden, sem):
    copy = pltpu.make_async_copy(rows_in.at[:, head_utterance(), :, 0:D], hidden, sem.at[0])
    copy.start()
    grads = grads_in()
    right = jnp.concatenate([grads[:, k * 64 : (k + 1) * 64, :].reshape(1024, 128) for k in range(3)], axis=1)
    dst, src = iota((1024, 1), 0), iota((1024, D), 1)
    row = jnp.where((dst & 7) < 6, (dst >> 3) * 6 + (dst & 7), -1)
    spread = (src == row).astype(f32).astype(bf16)
    copy.wait()
    res = tn(hidden[...].reshape(1024, D), right).astype(bf16)
    spill.put(nn(spread, res).astype(bf16))


def owner_order(core):
    src, dst = iota((D, D), 0), iota((1, D), 1)
    second = dst >= 384
    rest = dst - jnp.where(second, 384, 0)
    which = jnp.where(second, 1 - core, core)
    s = int_div(rest, 24)
    y = int_div(rest - 24 * s, 6)
    j = rest - 24 * s - 6 * y
    return (src == (2 * y + which) * 96 + s * 6 + j).astype(f32).astype(bf16)


S_MID, S_GI, S_INNER, S_GO, S_ATT, S_GA, S_END = 0, 384, 3456, 4992, 5760, 6144, 6912
O_MID, O_INNER, O_ATT, O_END = 0, 384, 1920, 2304


def middle_kernel(
    skip, recv, hidden, cot, out_w_in, out_b, mid_g_in, mid_s_in, inner_w_in, inner_b_in, outer_w_in, outer_b,
    fin_g_in, fin_s_in,
    act_out, grad_att_out, gmi_out, send_out, own_out, small_out,
    act, slope, out_w, inner_w, outer_w, sems,
):
    pairs = [(out_w_in, out_w)]
    for q in range(4):
        cols = slice(q * D, (q + 1) * D)
        pairs += [(inner_w_in.at[:, cols], inner_w.at[:, cols]), (outer_w_in.at[cols, :], outer_w.at[cols, :])]
    copies = fetch(sems, *pairs)
    core = core_index()
    keep = (1 - skip()[0]).astype(f32)
    mid_gain, fin_gain, inner_bias = vec(mid_g_in), vec(fin_g_in), vec(inner_b_in)
    att = jnp.concatenate(
        [jnp.concatenate([recv[u * PAIRS + p] for p in range(PAIRS)], axis=1) for u in range(2)], axis=0
    )
    copies[0].wait()
    middle_in = hidden()[...] + nn(att, out_w[...]) + vec(out_b)
    xm, rm = stats(middle_in)
    middle = xm * mid_gain + vec(mid_s_in)
    middle_b = middle.astype(bf16)
    order = owner_order(core)
    mid = nn(middle_b, order).astype(bf16)
    att_p = nn(att, order).astype(bf16)
    own, send = own_out, send_out

    own[:, O_MID : O_MID + 384] = mid[:, :384]
    own[:, O_ATT : O_ATT + 384] = att_p[:, :384]
    send[:, S_MID : S_MID + 384] = mid[:, 384:]
    send[:, S_ATT : S_ATT + 384] = att_p[:, 384:]
    outer = jnp.zeros((ROWS, D), f32)
    copies[1].wait()
    ahead = nn(middle_b, inner_w[:, 0:D])
    for q in range(4):
        cols = slice(q * D, (q + 1) * D)
        pre = ahead + inner_bias[:, cols]
        if q < 3:
            copies[3 + 2 * q].wait()
            ahead = nn(middle_b, inner_w[:, (q + 1) * D : (q + 2) * D])
        c, density = normal(pre)
        inner_b = (pre * c).astype(bf16)
        act[:, cols] = inner_b
        slope[:, cols] = c + pre * density
        copies[2 + 2 * q].wait()
        outer += nn(inner_b, outer_w[cols, :])
    first = core == 0
    for y in range(4):
        even = act[:, 2 * y * 384 : (2 * y + 1) * 384]
        odd = act[:, (2 * y + 1) * 384 : (2 * y + 2) * 384]
        own[:, O_INNER + y * 384 : O_INNER + (y + 1) * 384] = jnp.where(first, even, odd)
        send[:, S_INNER + y * 384 : S_INNER + (y + 1) * 384] = jnp.where(first, odd, even)
    final_in = middle + keep * (outer + vec(outer_b))
    xf, rf = stats(final_in)
    act_out.put((xf * fin_gain + vec(fin_s_in)).astype(bf16))
    gfi, fin_g, fin_s = norm_back(xf, rf, fin_gain, cot()[...].astype(f32))
    grad_outer = (keep * gfi).astype(bf16)
    send[:, S_GO : S_GO + D] = grad_outer
    grad_middle = gfi
    for q in range(4):
        cols = slice(q * D, (q + 1) * D)
        grad_inner = (slope[:, cols] * nt(grad_outer, outer_w[cols, :])).astype(bf16)
        send[:, S_GI + q * D : S_GI + (q + 1) * D] = grad_inner
        small_out.ref[3 + q : 4 + q, :] = col_sum(grad_inner)
        grad_middle += nt(grad_inner, inner_w[:, cols])
    gmi, mid_g, mid_s = norm_back(xm, rm, mid_gain, grad_middle)
    gmi_out.put(gmi)
    grad_attn = gmi.astype(bf16)
    send[:, S_GA : S_GA + D] = grad_attn
    grad_att = nt(grad_attn, out_w[...]).astype(bf16)
    for u in range(2):
        for p in range(PAIRS):
            grad_att_out.ref[u * PAIRS + p] = grad_att[u * 64 : (u + 1) * 64, p * 128 : (p + 1) * 128]
    grad_att_out.ref[2 * PAIRS :] = jnp.zeros((SEQ - 2 * PAIRS, 64, 128), bf16)
    grad_att_out.flush()
    for row, value in ((0, fin_g), (1, fin_s), (2, col_sum(grad_outer)), (7, mid_g), (8, mid_s), (9, col_sum(grad_attn))):
        small_out.ref[row : row + 1, :] = value
    small_out.ref[10:16, :] = jnp.zeros((6, D), f32)
    small_out.flush()


def dense_grads_kernel(own, sent, got, spill):
    out = spill.ref

    def right(start):
        return jnp.concatenate([sent[:, start : start + D], got[:, start : start + D]], axis=0)

    def left(start, theirs, width):
        return jnp.concatenate([own[:, start : start + width], got[:, theirs : theirs + width]], axis=0)

    mid = left(O_MID, S_MID, 384)
    mid_t = mid.T
    sixes = [nn(mid_t, right(S_GI + q * D)).astype(bf16) for q in range(4)]
    sixes.append(nn(left(O_ATT, S_ATT, 384).T, right(S_GA)).astype(bf16))
    outer = nn(left(O_INNER, S_INNER, 1536).T, right(S_GO))
    dst, src = iota((512, 480), 0), iota((1, 480), 1)
    q = int_div(src, 96)
    n = int_div(src - 96 * q, 6)
    j = src - 96 * q - 6 * n
    order = (dst == n * 32 + q * 6 + j).astype(f32).astype(bf16)
    for quarter in range(4):
        rows = slice(quarter * 96, quarter * 96 + 96)
        block = nn(order, jnp.concatenate([x[rows] for x in sixes], axis=0))
        for k in range(4):
            s = quarter * 4 + k
            for y in range(0, 4, 2):
                pieces = []
                for m in (y, y + 1):
                    pieces.append(block[(k * 4 + m) * 32 : (k * 4 + m) * 32 + 32])
                    pieces.append(outer[m * 384 + s * 24 : m * 384 + s * 24 + 24])
                out[s, y * CHUNK : (y + 2) * CHUNK, :] = jnp.concatenate(pieces, axis=0).astype(bf16)
        spill.flush(slice(quarter * 4, quarter * 4 + 4))


def qkv_back_kernel(
    recv, gmi, pre_in, masked, gain_in, weight, send_out, small_out, scratch
):
    pre = pre_in()[...]
    gain = vec(gain_in)
    xhat, r = stats(masked()[...] + gelu(pre))
    grad_hidden = gmi()[...]
    sums = []
    for slot in range(3):
        part = jnp.concatenate(
            [
                jnp.concatenate([recv[u * PAIRS + p, slot * 64 : (slot + 1) * 64, :] for p in range(PAIRS)], axis=1)
                for u in range(2)
            ],
            axis=0,
        )
        sums.append(col_sum(part))
        grad_hidden += nt(part, weight()[:, slot * D : (slot + 1) * D])
    grad_summed, enc_g, enc_s = norm_back(xhat, r, gain, grad_hidden)
    grad_conv = (gelu_slope(pre) * grad_summed).astype(bf16).astype(f32)
    for k, x in enumerate((grad_conv, grad_summed)):
        for g, rows in enumerate(rows_to_groups(x, scratch)):
            send_out[g, k * 16 : k * 16 + 16, :] = rows.astype(bf16)
    for row, value in enumerate((enc_g, enc_s, sums[0], sums[2], jnp.sum(grad_conv, axis=0, keepdims=True))):
        small_out.ref[row : row + 1, :] = value
    small_out.ref[5:8, :] = jnp.zeros((3, D), f32)
    small_out.flush()


def feats_back_kernel(grad, feats, gain_in, weight, feats_out, scratch):
    grad_proj = groups_to_rows(grad, scratch).astype(bf16)
    xhat, r = stats(feats()[...].astype(f32))
    feats_out[...] = norm_back(xhat, r, vec(gain_in), nt(grad_proj, weight()[...]))[0]


def tail_kernel(
    grad_in, small_a, small_b, weight, high, low, normed, qkv_rows, tail_out, frames, spread, by_four
):
    group = lax.axis_index("seq")
    lane = iota((1, 128), 1)
    ref = grad_in()
    grad = jnp.concatenate([ref[p].astype(f32) for p in range(SEQ)], axis=0)
    for f in range(SUPER):
        moved = pltpu.roll(grad, SW - f * GW, 1) if f else grad
        frames[pl.ds(f, 256, stride=SUPER), :] = jnp.where(lane < GW, moved[:, :128], 0.0)
    grads = frames[...].astype(bf16)
    grads_t = grads.T
    pick = (iota((128, D), 1) == iota((128, D), 0) + group * GW) & (iota((128, 1), 0) < GW)
    own_weight = nt(pick.astype(f32).astype(bf16), weight()[...])
    sums = jnp.sum(grads_t.astype(f32), axis=1, keepdims=True)
    in_g = jnp.sum(own_weight * (nn(grads_t, high()[...]) + nn(grads_t, low()[...])), axis=0, keepdims=True)
    in_s = jnp.sum(own_weight * sums, axis=0, keepdims=True)
    by_four[...] = nn(grads_t, normed()[...]).T
    bias = jnp.sum(grads.astype(f32), axis=0, keepdims=True)
    place = pick.astype(f32).astype(bf16)
    bias_high = bias.astype(bf16)
    bias_low = (bias - bias_high.astype(f32)).astype(bf16)
    proj_b = nn(jnp.concatenate([bias_high] * 8, axis=0), place) + nn(jnp.concatenate([bias_low] * 8, axis=0), place)
    a = lambda k: small_a()[k : k + 1, :]
    b = lambda k: small_b()[k : k + 1, :]
    vectors = [proj_b[:1], b(4), b(0), b(1), b(2), b(3), a(9), a(7), a(8), a(2), a(0), a(1)]
    lane6 = iota((1, D), 1)
    slot6 = lane6 - 6 * int_div(lane6, 6)
    sub = iota((8, D), 0)
    main = jnp.concatenate([jnp.where(slot6 == sub, v, 0.0) for v in vectors] + [jnp.zeros((32, D), f32)], axis=0)
    sub24 = iota((24, D), 0)
    slot24 = lane6 - 24 * int_div(lane6, 24)
    inner = [
        jnp.concatenate(
            [jnp.zeros((96, D), f32), jnp.where(slot24 == sub24, a(3 + k), 0.0), jnp.zeros((8, D), f32)], axis=0
        )
        for k in range(4)
    ]
    lane4, sub4 = iota((8, C_IN), 1) & 3, iota((8, C_IN), 0)
    last = jnp.concatenate(
        [
            jnp.zeros((120, C_IN), f32),
            jnp.where(lane4 == sub4, in_g, 0.0) + jnp.where(lane4 == sub4 - 4, in_s, 0.0),
        ],
        axis=0,
    )
    own = iota((128, D), 0)
    pick6 = (int_div(lane6, 6) == own).astype(f32).astype(bf16)
    pick24 = [(int_div(lane6, 24) + 32 * k == own).astype(f32).astype(bf16) for k in range(4)]
    pick4 = ((iota((1, C_IN), 1) >> 2) == iota((128, C_IN), 0)).astype(f32).astype(bf16)
    spread[...] = jnp.zeros_like(spread)
    both = jnp.zeros((128, 256), f32)
    for p, m in [(pick6, main)] + list(zip(pick24, inner)) + [(pick4, last)]:
        high_m = m.astype(bf16)
        low_m = (m - high_m.astype(f32)).astype(bf16)
        both += nt(p, jnp.concatenate([high_m, low_m], axis=0))
    for k in range(2):
        spread[pl.ds(k * 1024 + 6, 128, stride=8), :] = both[:, k * 128 : (k + 1) * 128]
    for k in range(2):
        first, second = [by_four[pl.ds(2 * k + n, 128, stride=4), :] for n in range(2)]
        spread[pl.ds(2048 + 6 + k, 128, stride=8), :] = first + pltpu.roll(second, GW, 1)
    rows = qkv_rows()
    for k in range(3):
        lanes = slice(k * 128, (k + 1) * 128)
        tail_out[:, lanes] = (rows[:, lanes].astype(f32) + spread[k * 1024 : (k + 1) * 1024, :]).astype(bf16)


def tail_sum_kernel(got, qkv_out, proj_out, *vector_outs):
    small = jnp.zeros((1, 128), f32)
    proj = [jnp.zeros((1, D), f32)] * 4
    sums = []
    for d in range(SEQ):
        total = got[d].astype(f32)
        for b in range(1, 8):
            total += got[b * SEQ + d].astype(f32)
        sums.append(total)
        small += total[6:7, :128] + total[6:7, 128:256]
        for k in range(4):
            piece = total[6 + k // 2 : 7 + k // 2, 256:]
            wide = jnp.concatenate([piece, jnp.zeros((1, D - 128), f32)], axis=1)
            shift = (d * GW - (k % 2) * GW) % D
            lane = iota((1, D), 1)
            start = (k % 2) * GW
            wide = jnp.where((lane >= start) & (lane < start + GW), wide, 0.0)
            proj[k] += pltpu.roll(wide, shift, 1) if shift else wide
    for p in range(PAIRS):
        pair = sums[p] + sums[PAIRS + p]
        for k in range(3):
            start = k * D + p * 128
            qkv_out[:, start : start + 128] = pair[:6, k * 128 : (k + 1) * 128]
    for k in range(4):
        proj_out[k : k + 1, :] = proj[k]
    starts = [120, 124] + [8 * k for k in range(7)] + [56, 64, 96, 72, 80, 88]
    for start, out in zip(starts, vector_outs):
        out[...] = small[0, start : start + out.shape[0]]


def to_peers(x, axis, groups=None):
    return lax.all_to_all(x, axis, 0, 0, tiled=True, axis_index_groups=groups)


Y_GROUPS = [[0, 2, 4, 6], [1, 3, 5, 7]]


def local(
    feats, lengths, skip_flag, cotangent, input_gain, input_shift, proj_weight, proj_bias, conv_weight, conv_bias,
    encoder_gain, encoder_shift, qkv_weight, query_bias, value_bias, output_weight, output_bias, middle_gain,
    middle_shift, inner_weight, inner_bias, outer_weight, outer_bias, final_gain, final_shift,
):
    seq = lax.axis_index("seq")
    rows_in = feats.reshape(ROWS, C_IN)
    cot = cotangent.reshape(ROWS, D)

    masked, conv_send = call(
        project_kernel,
        [Spill((ROWS, D), f32), shape((GROUPS, 16, SW), bf16)],
        Smem(lengths), Hbm(rows_in), Hbm(input_gain), Hbm(input_shift), Hbm(proj_weight), Hbm(proj_bias),
        flops=2 * ROWS * C_IN * D, name="project", scratch=[TRANSPOSE_SCRATCH],
    )
    conv_x = to_peers(conv_send, "seq")
    own_taps = lax.dynamic_slice_in_dim(conv_weight, seq * GW, GW, axis=0)
    taps = own_taps.transpose(0, 2, 1).reshape(GW, KW * GW)
    shifted = pltpu.VMEM((2, 144, SW), f32)
    conv_flops = 2 * 256 * SW * BAND
    conv_y, conv_x = call(
        conv_kernel, [shape((SEQ, 16, SW), bf16), Copy((SEQ, 16, SW), bf16, 0)], conv_x, Hbm(taps),
        scratch=[pltpu.VMEM((SW, BAND), bf16), shifted],
        flops=conv_flops, name="conv", mib=24,
    )
    conv_back = to_peers(conv_y, "seq")
    conv_pre, hidden, qkv_send, rows_send = call(
        qkv_kernel,
        [
            Spill((ROWS, D), f32), Spill((ROWS, D), f32), Spill((SEQ, 192, 128), bf16, parts=3),
            Spill((ROWS, D + C_IN), bf16),
        ],
        conv_back, Hbm(masked), Hbm(conv_bias), Hbm(encoder_gain), Hbm(encoder_shift), Hbm(qkv_weight), Hbm(query_bias),
        Hbm(value_bias), Hbm(rows_in), flops=2 * ROWS * D * 3 * D, name="qkv", scratch=[TRANSPOSE_SCRATCH],
    )
    qkv = to_peers(qkv_send, "seq")
    rows_all = lax.all_gather(rows_send, "seq", axis=0, tiled=True).reshape(SEQ, 2, 64, D + C_IN)
    attended, logs, attended_full, qkv_kept = call(
        attend_kernel,
        [shape((1024, 128), bf16), Spill((1024, 128), f32), Spill((1024, 128), f32), Copy((SEQ, 192, 128), bf16, 1)],
        Smem(lengths), qkv, flops=8 * 1024 * 1024 * 128, name="attend", mib=32,
    )
    att_recv = to_peers(attended.reshape(SEQ, 64, 128), "seq")
    activations, grad_att_send, gmi, pair_send, pair_own, small_a = call(
        middle_kernel,
        [
            Spill((ROWS, D), bf16), Spill((SEQ, 64, 128), bf16), Spill((ROWS, D), f32),
            shape((ROWS, S_END), bf16), shape((ROWS, O_END), bf16), Spill((16, D), f32),
        ],
        Smem(skip_flag), att_recv, Hbm(hidden), Hbm(cot), Raw(output_weight), Hbm(output_bias), Hbm(middle_gain),
        Hbm(middle_shift), Raw(inner_weight), Hbm(inner_bias), Raw(outer_weight), Hbm(outer_bias), Hbm(final_gain),
        Hbm(final_shift),
        scratch=[
            pltpu.VMEM((ROWS, FF), bf16), pltpu.VMEM((ROWS, FF), f32), pltpu.VMEM((D, D), bf16),
            pltpu.VMEM((D, FF), bf16), pltpu.VMEM((FF, D), bf16), pltpu.SemaphoreType.DMA((9,)),
        ],
        flops=2 * ROWS * (4 * D * FF + 2 * D * D), name="middle", mib=32,
    )
    swap = [(i, i ^ 1) for i in range(8)]
    pair_got = lax.ppermute(pair_send, "batch", swap)
    grad_att = to_peers(grad_att_send, "seq").reshape(1024, 128)
    (dense,) = call(
        dense_grads_kernel, [Spill((SEQ, 4 * CHUNK, D), bf16, parts=4)], pair_own, pair_send, pair_got,
        flops=2 * 256 * D * 3456, name="dense_grads", mib=24,
    )
    dense, grad_att = lax.optimization_barrier((dense, grad_att))
    dense_part = lax.psum_scatter(dense.reshape(SEQ * 4 * CHUNK, D), "seq", scatter_dimension=0, tiled=True)

    (grad_qkv_send,) = call(
        attend_back_kernel, [Spill((SEQ, 192, 128), bf16)], Smem(lengths), Hbm(qkv_kept), grad_att, Hbm(logs), Hbm(attended_full),
        scratch=[pltpu.VMEM((1024, 128), f32)] * 2, flops=20 * 1024 * 1024 * 128, name="attend_back",
    )
    grad_qkv = to_peers(grad_qkv_send, "seq")
    (qkv_rows,) = call(
        head_grads_kernel, [Spill((1024, 384), bf16)], Raw(rows_all), Hbm(grad_qkv_send),
        scratch=[pltpu.VMEM((SEQ, 64, D), bf16), pltpu.SemaphoreType.DMA((1,))], flops=4 * 1024 * D * 384,
        name="head_grads", mib=24,
    )
    frames_normed, frames_high, frames_low = call(
        frames_kernel, [Spill((2048, C_IN), bf16) for _ in range(3)], Raw(rows_all), Hbm(input_gain), Hbm(input_shift),
        scratch=[pltpu.VMEM((SEQ, 2, 64, C_IN), bf16), pltpu.SemaphoreType.DMA((1,))], name="frames", mib=32,
    )
    gmi, qkv_rows, frames_normed = lax.optimization_barrier((gmi, qkv_rows, frames_normed))
    back_send, small_b = call(
        qkv_back_kernel, [shape((SEQ, 32, SW), bf16), Spill((8, D), f32)],
        grad_qkv, Hbm(gmi), Hbm(conv_pre), Hbm(masked), Hbm(encoder_gain), Hbm(qkv_weight),
        scratch=[TRANSPOSE_SCRATCH], flops=2 * ROWS * D * 3 * D, name="qkv_back",
    )
    back_got = to_peers(back_send, "seq")
    back_other = lax.ppermute(back_got, "batch", swap)
    x_other = lax.ppermute(conv_x, "batch", swap)
    (grad_proj,) = call(
        conv_back_kernel, [shape((SEQ, 16, SW), bf16)], Smem(lengths), Hbm(back_got), Hbm(taps),
        scratch=[pltpu.VMEM((BAND, SW), bf16), shifted], flops=conv_flops, name="conv_back", mib=24,
    )
    grad_proj_got = to_peers(grad_proj, "seq")
    (tail,) = call(
        tail_kernel, [shape((1024, 384), bf16)], Hbm(grad_proj), Hbm(small_a), Hbm(small_b),
        Hbm(proj_weight), Hbm(frames_high), Hbm(frames_low), Hbm(frames_normed), Hbm(qkv_rows),
        scratch=[pltpu.VMEM((2048, 128), f32), pltpu.VMEM((3072, 128), f32), pltpu.VMEM((C_IN, 128), f32)],
        flops=6 * 2048 * C_IN * 128, name="tail", mib=32,
    )
    x_other, _ = lax.optimization_barrier((x_other, tail))
    tap_chunks = call(
        conv_weight_kernel, [Spill((GW, D), bf16) for _ in range(4)], Hbm(back_got), Hbm(back_other), Hbm(conv_x),
        Hbm(x_other),
        scratch=[
            pltpu.VMEM((192, BAND), f32), pltpu.VMEM((24, BAND), f32), pltpu.VMEM((192, 128), f32),
            pltpu.VMEM((4, GW, D), bf16), pltpu.VMEM((2, 2, 144, SW), f32),
        ],
        flops=conv_flops, name="conv_grads", mib=32,
    )
    tail, grad_proj_got, *tap_chunks = lax.optimization_barrier((tail, grad_proj_got, *tap_chunks))
    tap_got = []
    for k, piece in enumerate(tap_chunks):
        moves = [
            (b * 16 + g, (g // 2) * 16 + 8 * (g % 2) + 2 * ((b // 2 + k) % 4) + b % 2)
            for b in range(8)
            for g in range(GROUPS)
        ]
        tap_got.append(lax.ppermute(piece, ("batch", "seq"), moves))
    tail_got = to_peers(tail, ("batch", "seq"))
    (tap_own,) = call(conv_sum_kernel, [shape((GW, D), f32)], *[Hbm(x) for x in tap_got], name="conv_sum")
    grad_conv_weight = tap_own.reshape(6, KW, GW).transpose(0, 2, 1)
    dense_own = lax.psum_scatter(dense_part, "batch", scatter_dimension=0, tiled=True, axis_index_groups=Y_GROUPS)
    (grad_feats,) = call(
        feats_back_kernel, [shape((ROWS, C_IN), f32)], grad_proj_got, Hbm(rows_in), Hbm(input_gain), Hbm(proj_weight),
        scratch=[TRANSPOSE_SCRATCH], flops=2 * ROWS * C_IN * D, name="feats_back",
    )
    grad_inner_weight, grad_outer_weight, grad_output_weight = call(
        dense_sum_kernel, [shape((6, FF), f32), shape((24, D), f32), shape((6, D), f32)], Hbm(dense_own),
        name="dense_sum",
    )
    widths = [4, 4] + [6] * 9 + [24] + [6] * 3
    (
        grad_qkv_weight, grad_proj_weight, g_in_g, g_in_s, g_proj_b, g_conv_b, g_enc_g, g_enc_s, g_q_b, g_v_b, g_out_b, g_mid_g, g_mid_s,
        g_inner_b, g_outer_b, g_fin_g, g_fin_s,
    ) = call(
        tail_sum_kernel, [shape((6, 3 * D), f32), shape((4, D), f32)] + [shape((w,), f32) for w in widths],
        tail_got.reshape(128, 8, 384),
        name="tail_sum",
    )
    return (
        activations.reshape(2, 64, D), grad_feats.reshape(2, 64, C_IN), g_in_g, g_in_s, grad_proj_weight, g_proj_b,
        grad_conv_weight, g_conv_b, g_enc_g, g_enc_s, grad_qkv_weight, g_q_b, g_v_b, grad_output_weight, g_out_b,
        g_mid_g, g_mid_s, grad_inner_weight, g_inner_b, grad_outer_weight, g_outer_b, g_fin_g, g_fin_s,
    )


def solution(mesh):
    split = P("batch", "seq", None)
    both = ("batch", "seq")
    placed = (split, P("batch"), P("batch"), split) + (P(),) * 21
    row, matrix = P(both), P(both, None)
    return jax.shard_map(
        local,
        mesh=mesh,
        in_specs=placed,
        out_specs=(
            split, split, row, row, matrix, row, P(both, None, None), row, row, row, matrix, row, row, matrix, row,
            row, row, matrix, row, matrix, row, row, row,
        ),
        check_vma=False,
    )
```

```python
import functools

import jax
import jax.numpy as jnp
from jax import lax
from jax.experimental import pallas as pl
from jax.experimental.pallas import tpu as pltpu
from jax.sharding import PartitionSpec as P

f32 = jnp.float32
bf16 = jnp.bfloat16
i32 = jnp.int32

norm_eps = 1e-05
head_scale = 0.125
neg_fill = -1e30

D = 768
C_IN = 512
FF = 3072
GROUPS = 16
GW = 48
KW = 128
SUPER = 8
SW = SUPER * GW
TAP_BLOCKS = 17
BAND = TAP_BLOCKS * SW
ROWS = 128
SEQ = 16
PAIRS = 6
MIB = 1024 * 1024
TRANSPOSE_SCRATCH = pltpu.VMEM((D, 128), f32)

def nn(a, b):
    return lax.dot_general(a, b, (((1,), (0,)), ((), ())), preferred_element_type=f32)


def nt(a, b):
    return lax.dot_general(a, b, (((1,), (1,)), ((), ())), preferred_element_type=f32)


def tn(a, b):
    return lax.dot_general(a, b, (((0,), (0,)), ((), ())), preferred_element_type=f32)


def iota(shape, dim):
    return lax.broadcasted_iota(i32, shape, dim)


def int_div(x, c):
    return ((x.astype(f32) + 0.5) * (1.0 / c)).astype(i32)


def stats(x):
    c = x - jnp.mean(x, axis=-1, keepdims=True)
    r = lax.rsqrt(jnp.mean(c * c, axis=-1, keepdims=True) + norm_eps)
    return c * r, r


def norm_back(xhat, r, gain, g):
    e = g * gain
    dx = r * (e - jnp.mean(e, axis=-1, keepdims=True) - xhat * jnp.mean(e * xhat, axis=-1, keepdims=True))
    return dx, jnp.sum(g * xhat, axis=0, keepdims=True), jnp.sum(g, axis=0, keepdims=True)


def normal(x):
    bell = jnp.exp(-0.5 * x * x)
    t = 1.0 / (1.0 + (0.3275911 * 0.7071067811865476) * jnp.abs(x))
    poly = t * (0.127414796 + t * (-0.142248368 + t * (0.7107068705 + t * (-0.7265760135 + t * 0.5307027145))))
    tail = poly * bell
    return jnp.where(x < 0, tail, 1.0 - tail), 0.3989422804014327 * bell


def gelu(x):
    return x * normal(x)[0]


def gelu_slope(x):
    c, density = normal(x)
    return c + x * density


def col_sum(x):
    return jnp.sum(x.astype(f32), axis=0, keepdims=True)


def vec(lazy):
    ref = lazy()
    return ref[...].astype(f32).reshape(1, ref.shape[0])


def swap_blocks(xs):
    ys = [pltpu.roll(x, f * GW, 1) if f else x for f, x in enumerate(xs)]
    lane = iota((16, 128), 1)
    outs = []
    for g in range(SUPER):
        tiles = []
        for v in range(SW // 128):
            lo, hi = (128 * v) // GW, (128 * v + 127) // GW
            tile = ys[(lo - g) % SUPER][:, v * 128 : (v + 1) * 128]
            for q in range(lo + 1, hi + 1):
                tile = jnp.where(lane >= q * GW - 128 * v, ys[(q - g) % SUPER][:, v * 128 : (v + 1) * 128], tile)
            tiles.append(tile)
        w = jnp.concatenate(tiles, axis=1)
        outs.append(pltpu.roll(w, SW - g * GW, 1) if g else w)
    return outs


LANE_TILES = D // 128


def rows_to_groups(x, scratch):
    for v in range(LANE_TILES):
        scratch[v * ROWS : (v + 1) * ROWS, :] = x[:, v * 128 : (v + 1) * 128]
    outs = []
    for half in range(2):
        tiles = range(half * 3, half * 3 + 3)
        outs += swap_blocks(
            [
                jnp.concatenate([scratch[pl.ds(v * ROWS + f, 16, stride=SUPER), :] for v in tiles], axis=1)
                for f in range(SUPER)
            ]
        )
    return outs


def groups_to_rows(in_ref, scratch):
    for half in range(2):
        xs = [in_ref[half * 8 + g].astype(f32) for g in range(SUPER)]
        for f, x in enumerate(swap_blocks(xs)):
            for v in range(3):
                row = (half * 3 + v) * ROWS + f
                scratch[pl.ds(row, 16, stride=SUPER), :] = x[:, v * 128 : (v + 1) * 128]
    return jnp.concatenate([scratch[v * ROWS : (v + 1) * ROWS, :] for v in range(LANE_TILES)], axis=1)


class Hbm:
    def __init__(self, array):
        self.array = array


class Raw(Hbm):
    pass


class Smem(Hbm):
    pass


class Spill:
    def __init__(self, dims, dtype, parts=1):
        self.struct, self.parts = jax.ShapeDtypeStruct(dims, dtype), parts


class Copy:
    parts = 1

    def __init__(self, dims, dtype, operand):
        self.struct, self.operand = jax.ShapeDtypeStruct(dims, dtype), operand


class Flusher:
    def __init__(self, ref, target, sems, base, copies):
        self.ref, self.target, self.sems, self.next, self.copies = ref, target, sems, base, copies

    def put(self, value):
        self.ref[...] = value
        self.flush()

    def flush(self, *index):
        src, dst = (self.ref.at[index], self.target.at[index]) if index else (self.ref, self.target)
        copy = pltpu.make_async_copy(src, dst, self.sems.at[self.next])
        copy.start()
        self.next += 1
        self.copies.append(copy)


class Lazy:
    def __init__(self, copy, ref):
        self.copy, self.ref, self.waited = copy, ref, False

    def __call__(self):
        if not self.waited:
            self.copy.wait()
            self.waited = True
        return self.ref


def call(body, outs, *args, scratch=(), flops=0, name=None, mib=16):
    fetched = [k for k, a in enumerate(args) if type(a) in (Hbm, Smem)]
    spilled = [k for k, o in enumerate(outs) if isinstance(o, Spill)]
    copied = [k for k, o in enumerate(outs) if isinstance(o, Copy)]
    arrays = [
        pltpu.with_memory_space_constraint(a.array, pltpu.HBM) if isinstance(a, Hbm) and not isinstance(a, Smem) else getattr(a,'array',a) for a in args
    ]
    structs = [o.struct if isinstance(o, (Spill, Copy)) else o for o in outs]
    near = {Hbm: pltpu.VMEM, Smem: pltpu.SMEM}
    own = [near[type(args[k])](arrays[k].shape, arrays[k].dtype) for k in fetched]
    own += [pltpu.VMEM(structs[k].shape, structs[k].dtype) for k in spilled]
    sem_count = len(fetched) + sum(outs[k].parts for k in spilled) + len(copied)
    if sem_count:
        own.append(pltpu.SemaphoreType.DMA((sem_count,)))

    def wrapped(*refs):
        n_in, n_out = len(args), len(outs)
        ins, out_refs, rest = list(refs[:n_in]), list(refs[n_in : n_in + n_out]), list(refs[n_in + n_out :])
        extra, rest = rest[: len(own)], rest[len(own) :]
        lazies, flushed = [], []
        for slot, k in enumerate(fetched):
            copy = pltpu.make_async_copy(ins[k], extra[slot], extra[-1].at[slot])
            copy.start()
            ins[k] = Lazy(copy, extra[slot])
            lazies.append(ins[k])
        base = len(fetched)
        for slot, k in enumerate(spilled):
            out_refs[k] = Flusher(extra[len(fetched) + slot], out_refs[k], extra[-1], base, flushed)
            base += outs[k].parts
        for k in copied:
            out_refs[k] = Flusher(refs[outs[k].operand], out_refs[k], extra[-1], base, flushed)
            base += 1
        body(*ins, *out_refs, *rest)
        for lazy in lazies:
            lazy()
        for copy in flushed:
            copy.wait()

    bytes_accessed = sum(a.size * a.dtype.itemsize for a in arrays) + sum(o.size * o.dtype.itemsize for o in structs)
    return pl.pallas_call(
        wrapped,
        out_shape=[pltpu.HBM(o.struct.shape, o.struct.dtype) if isinstance(o, (Spill, Copy)) else o for o in outs],
        in_specs=[pl.BlockSpec(memory_space=pltpu.HBM if isinstance(a, Hbm) else pltpu.VMEM) for a in args],
        out_specs=[pl.BlockSpec(memory_space=pltpu.HBM if isinstance(o, (Spill, Copy)) else pltpu.VMEM) for o in outs],
        scratch_shapes=own + list(scratch),
        compiler_params=pltpu.CompilerParams(vmem_limit_bytes=mib * MIB),
        cost_estimate=pl.CostEstimate(flops=flops, bytes_accessed=bytes_accessed, transcendentals=0),
        name=name,
    )(*arrays)


def fetch(sems, *pairs):
    copies = [pltpu.make_async_copy(src, dst, sems.at[k]) for k, (src, dst) in enumerate(pairs)]
    for copy in copies:
        copy.start()
    return copies


def shape(dims, dtype):
    return jax.ShapeDtypeStruct(dims, dtype)


def live_rows(lengths):
    row = iota((ROWS, 1), 0)
    frame = (row & 63) + lax.axis_index("seq") * 64
    ref = lengths()
    length = jnp.where(row < 64, ref[0], ref[1])
    return (frame < length).astype(f32)


def head_utterance():
    return (lax.axis_index("seq") >= PAIRS).astype(i32)


def core_index():
    return lax.axis_index("batch") & 1


def project_kernel(lengths, feats, gain, shift, weight, bias, masked_out, send_out, scratch):
    xhat, _ = stats(feats()[...].astype(f32))
    normed = (xhat * vec(gain) + vec(shift)).astype(bf16)
    masked = (nn(normed, weight()[...]) + vec(bias)) * live_rows(lengths)
    masked_out.put(masked)
    for g, x in enumerate(rows_to_groups(masked, scratch)):
        send_out[g] = x.astype(bf16)


def band_rows(taps):
    flat = jnp.concatenate([taps[...].astype(f32), jnp.zeros((GW, SW), f32)], axis=1)
    return [(pltpu.roll(flat, f * GW, 1) if f else flat).astype(bf16) for f in range(SUPER)]


def padded(pieces, scratch):
    for u in range(2):
        scratch[u, 0:8, :] = jnp.zeros((8, SW), f32)
        scratch[u, 136:144, :] = jnp.zeros((8, SW), f32)
        for p, x in enumerate(pieces):
            scratch[u, 8 + p * 8 : 16 + p * 8, :] = x[u * 8 : u * 8 + 8]


def windows(scratch, starts):
    parts = [
        jnp.concatenate([scratch[u, start : start + 128, :] for u in range(2)], axis=0).astype(bf16) for start in starts
    ]
    return jnp.concatenate(parts, axis=1)


def by_seq(x, p):
    return jnp.concatenate([x[u * 128 + p * 8 : u * 128 + p * 8 + 8] for u in range(2)], axis=0)


def conv_kernel(x, taps, out, x_out, w, scratch):
    x_out.flush()
    for f, rows in enumerate(band_rows(taps())):
        w[f * GW : (f + 1) * GW, :] = rows
    padded([x[p].astype(f32) for p in range(SEQ)], scratch)
    res = nt(windows(scratch, range(TAP_BLOCKS)), w[...])
    for p in range(SEQ):
        out[p] = by_seq(res, p).astype(bf16)


CHUNK = 56


def conv_back_kernel(lengths, got_in, taps, out, w, scratch):
    for f, rows in enumerate(band_rows(taps())):
        for i in range(TAP_BLOCKS):
            w[i * SW + f * GW : i * SW + (f + 1) * GW, :] = rows[:, i * SW : (i + 1) * SW]
    got = got_in()
    padded([got[p, :16, :].astype(f32) for p in range(SEQ)], scratch)
    res = nn(windows(scratch, range(16, -1, -1)), w[...])
    row, f = iota((16, SW), 0), int_div(iota((1, SW), 1), GW)
    ref = lengths()
    length = jnp.where(row < 8, ref[0], ref[1])
    for p in range(SEQ):
        total = by_seq(res, p) + got[p, 16:, :].astype(f32)
        live = p * 64 + (row & 7) * SUPER + f < length
        out[p] = jnp.where(live, total, 0.0).astype(bf16)


def conv_weight_kernel(got_in, other_in, x_in, x_other, *rest):
    tap_outs, (wide, acc, spread, chunks, scratch) = rest[:4], rest[4:]
    core = core_index()
    src, dst = iota((SW, 192), 0), iota((1, 192), 1)
    f = int_div(dst, 24)
    y = int_div(dst - 24 * f, 6)
    own_taps = (src == f * GW + (2 * y + core) * 6 + (dst - 24 * f - 6 * y)).astype(f32).astype(bf16)
    grads, parts = [], []
    for k, (got, x) in enumerate(((got_in(), x_in()), (other_in(), x_other()))):
        grad = jnp.concatenate([got[p, :16, :] for p in range(SEQ)], axis=0)
        grad = nn(grad, own_taps)
        grads.append(jnp.concatenate([grad[p * 16 + u * 8 : p * 16 + u * 8 + 8] for u in range(2) for p in range(SEQ)], axis=0))
        padded([x[p].astype(f32) for p in range(SEQ)], scratch.at[k])
        parts.append(windows(scratch.at[k], range(TAP_BLOCKS)))
    wide[...] = nn(jnp.concatenate(grads, axis=0).astype(bf16).T, jnp.concatenate(parts, axis=0))
    acc[...] = wide[7 * 24 :, :]
    for f in range(6, -1, -1):
        acc[...] = pltpu.roll(acc[...], BAND - GW, 1) + wide[f * 24 : f * 24 + 24, :]
    for v in range(LANE_TILES):
        lanes = slice(v * 128, (v + 1) * 128)
        for i in range(8):
            spread[pl.ds(i, 24, stride=8), :] = acc[:, i * D + v * 128 : i * D + (v + 1) * 128]
        for y in range(4):
            chunks[y, :, lanes] = spread[y * GW : (y + 1) * GW, :].astype(bf16)
    own_y = lax.axis_index("batch") >> 1
    for k, tap_out in enumerate(tap_outs):
        tap_out.put(chunks[(own_y + k) & 3])


def conv_sum_kernel(*refs):
    total = refs[0]()[...].astype(f32)
    for ref in refs[1:-1]:
        total += ref()[...].astype(f32)
    refs[-1][...] = total


def dense_sum_kernel(total_in, inner_out, outer_out, output_out):
    total = total_in()[...].astype(f32)
    for q in range(4):
        inner_out[:, q * D : (q + 1) * D] = total[q * 6 : q * 6 + 6]
    output_out[...] = total[24:30]
    outer_out[...] = total[32:]


def qkv_kernel(
    conv, masked, conv_bias, gain, shift, weight, query_bias, value_bias, feats,
    pre_out, hidden_out, send_out, rows_out, scratch,
):
    pre = groups_to_rows(conv, scratch) + vec(conv_bias)
    pre_out.put(pre)
    xhat, _ = stats(masked()[...] + gelu(pre))
    hidden = xhat * vec(gain) + vec(shift)
    hidden_out.put(hidden)
    hidden_b = hidden.astype(bf16)
    rows_out.ref[:, :D] = hidden_b
    rows_out.ref[:, D:] = feats()[...]
    rows_out.flush()
    zero = jnp.zeros((1, D), f32)
    send = send_out.ref
    for slot, (block, bias) in enumerate(((1, zero), (2, vec(value_bias)), (0, vec(query_bias)))):
        part = (nn(hidden_b, weight()[:, block * D : (block + 1) * D]) + bias).astype(bf16)
        for u in range(2):
            for pair in range(PAIRS):
                send[u * PAIRS + pair, slot * 64 : (slot + 1) * 64, :] = part[
                    u * 64 : (u + 1) * 64, pair * 128 : (pair + 1) * 128
                ]
        part_rows = slice(slot * 64, (slot + 1) * 64)
        send[2 * PAIRS :, part_rows, :] = jnp.zeros((SEQ - 2 * PAIRS, 64, 128), bf16)
        send_out.flush(slice(None), part_rows)


Q_BLOCK = 512


def columns(*values):
    rows = max(v.shape[0] for v in values)
    lane = iota((rows, 128), 1)
    out = jnp.zeros((rows, 128), f32)
    for k, v in enumerate(values):
        out = jnp.where(lane == k, v, out)
    return out.astype(bf16)


def three_terms(x):
    high = x.astype(bf16).astype(f32)
    mid = (x - high).astype(bf16).astype(f32)
    return high, mid, x - high - mid


def key_bias(lengths):
    ref = lengths()
    length = jnp.where(head_utterance() == 0, ref[0], ref[1])
    return jnp.where(iota((1024, 1), 0) < length, 0.0, neg_fill)


def attend_kernel(lengths, qkv, out, log_spill, out_spill, copy_spill):
    log_out, full_out = log_spill.ref, out_spill.ref
    copy_spill.flush()
    keys = jnp.concatenate([qkv[:, 0:64, :].reshape(1024, 128), columns(key_bias(lengths))], axis=1)
    values = jnp.concatenate([qkv[:, 64:128, :].reshape(1024, 128), columns(jnp.ones((1024, 1), f32))], axis=1)
    left = iota((1024, 128), 1) < 64
    query = qkv[:, 128:192, :].reshape(1024, 128) * head_scale
    parts, logs = [], []
    for head in range(2):
        own = left if head == 0 else ~left
        q_h = jnp.concatenate([jnp.where(own, query, jnp.zeros_like(query)), columns(jnp.ones((1024, 1), f32))], axis=1)
        scores = nt(q_h, keys)
        top = jnp.max(scores, axis=-1, keepdims=True)
        e = jnp.exp(scores - top).astype(bf16)
        sums = nn(e, values)
        total = sums[:, 128:129]
        parts.append(sums[:, :128] * (1.0 / total))
        logs.append(top + jnp.log(total))
    both = jnp.where(left, parts[0], parts[1])
    out[...] = both.astype(bf16)
    full_out[...] = both
    log_out[...] = jnp.where(left, logs[0], logs[1])
    log_spill.flush()
    out_spill.flush()


def attend_back_kernel(lengths, qkv_in, grad, logs_in, full_in, spill, dk, dv, dq):
    qkv, logs, full, out = qkv_in(), logs_in(), full_in(), spill.ref
    one = jnp.ones((1024, 1), f32)
    keys_only = qkv[:, 0:64, :].reshape(1024, 128)
    keys = jnp.concatenate([keys_only, columns(key_bias(lengths), one, one, one)], axis=1)
    values = jnp.concatenate([qkv[:, 64:128, :].reshape(1024, 128), columns(one, one, one)], axis=1)
    keys_t = keys_only.T
    left = iota((Q_BLOCK, 128), 1) < 64
    top_rows = iota((128, Q_BLOCK), 0) < 64
    per = Q_BLOCK // 64
    dk[...] = jnp.zeros_like(dk)
    dv[...] = jnp.zeros_like(dv)
    dq[...] = jnp.zeros_like(dq)

    def step(n, carry):
        query = qkv[pl.ds(n * per, per), 128:192, :].reshape(Q_BLOCK, 128) * head_scale
        rows = pl.ds(pl.multiple_of(n * Q_BLOCK, Q_BLOCK), Q_BLOCK)
        go = grad[rows, :]
        weighted = go.astype(f32) * full[rows, :]
        def one_head(head, carry):
            own = (left & (head == 0)) | (~left & (head == 1))
            q_h = jnp.where(own, query, jnp.zeros_like(query))
            g_h = jnp.where(own, go, jnp.zeros_like(go))
            log = jnp.where(head == 0, logs[rows, 0:1], logs[rows, 64:65])
            delta = jnp.sum(jnp.where(own, weighted, 0.0), axis=-1, keepdims=True)
            q_more = jnp.concatenate([q_h, columns(jnp.ones((Q_BLOCK, 1), f32), *three_terms(-log))], axis=1)
            g_more = jnp.concatenate([g_h, columns(*three_terms(-delta))], axis=1)
            probs = jnp.exp(nt(keys, q_more))
            grad_scores = (probs * nt(values, g_more)).astype(bf16)
            head_rows = (top_rows & (head == 0)) | (~top_rows & (head == 1))
            dq[...] = jnp.where(head_rows, nn(keys_t, grad_scores), dq[...])
            dk[...] += nn(grad_scores, q_h)
            dv[...] += nn(probs.astype(bf16), g_h)
            return carry

        lax.fori_loop(0, 2, one_head, 0)
        grad_query = (dq[...] * head_scale).T.astype(bf16)
        out[pl.ds(n * per, per), 0:64, :] = grad_query.reshape(per, 64, 128)
        return carry

    lax.fori_loop(0, 1024 // Q_BLOCK, step, 0)
    out[:, 64:128, :] = dk[...].astype(bf16).reshape(SEQ, 64, 128)
    out[:, 128:192, :] = dv[...].astype(bf16).reshape(SEQ, 64, 128)
    spill.flush()


def frames_kernel(rows_in, gain, shift, normed_out, high_out, low_out, feats, sem):
    copy = pltpu.make_async_copy(rows_in.at[:, :, :, D : D + C_IN], feats, sem.at[0])
    copy.start()
    gain_row, shift_row = vec(gain), vec(shift)
    copy.wait()

    def step(p, carry):
        rows = pl.ds(pl.multiple_of(p * 128, 128), 128)
        xhat, _ = stats(feats[p].reshape(128, C_IN).astype(f32))
        normed_out.ref[rows, :] = (xhat * gain_row + shift_row).astype(bf16)
        high = xhat.astype(bf16)
        high_out.ref[rows, :] = high
        low_out.ref[rows, :] = (xhat - high.astype(f32)).astype(bf16)
        return carry

    lax.fori_loop(0, SEQ, step, 0)
    for spill in (normed_out, high_out, low_out):
        spill.flush()


def head_grads_kernel(rows_in, grads_in, spill, hidden, sem):
    copy = pltpu.make_async_copy(rows_in.at[:, head_utterance(), :, 0:D], hidden, sem.at[0])
    copy.start()
    grads = grads_in()
    right = jnp.concatenate([grads[:, k * 64 : (k + 1) * 64, :].reshape(1024, 128) for k in range(3)], axis=1)
    copy.wait()
    res = tn(hidden[...].reshape(1024, D), right).astype(bf16)

    def step(k, carry):
        rows = pl.ds(pl.multiple_of(k * 256, 256), 256)
        dst, src = iota((256, 1), 0) + k * 256, iota((256, D), 1)
        row = jnp.where((dst & 7) < 6, (dst >> 3) * 6 + (dst & 7), -1)
        spill.ref[rows, :] = nn((src == row).astype(f32).astype(bf16), res).astype(bf16)
        return carry

    lax.fori_loop(0, 4, step, 0)
    spill.flush()


def owner_order(core):
    src, dst = iota((D, D), 0), iota((1, D), 1)
    second = dst >= 384
    rest = dst - jnp.where(second, 384, 0)
    which = jnp.where(second, 1 - core, core)
    s = int_div(rest, 24)
    y = int_div(rest - 24 * s, 6)
    j = rest - 24 * s - 6 * y
    return (src == (2 * y + which) * 96 + s * 6 + j).astype(f32).astype(bf16)


S_MID, S_GI, S_INNER, S_GO, S_ATT, S_GA, S_END = 0, 384, 3456, 4992, 5760, 6144, 6912
O_MID, O_INNER, O_ATT, O_END = 0, 384, 1920, 2304


def middle_kernel(
    skip, recv, hidden, cot, out_w_in, out_b, mid_g_in, mid_s_in, inner_w_in, inner_b_in, outer_w_in, outer_b,
    fin_g_in, fin_s_in,
    act_out, grad_att_out, gmi_out, send_out, own_out, small_out,
    act, slope, out_w, inner_w, outer_w, bias, total, sems,
):
    pairs = [(out_w_in, out_w)]
    for q in range(4):
        cols = slice(q * D, (q + 1) * D)
        pairs += [(inner_w_in.at[:, cols], inner_w.at[:, cols]), (outer_w_in.at[cols, :], outer_w.at[cols, :])]
    copies = fetch(sems, *pairs)
    core = core_index()
    keep = (1 - skip()[0]).astype(f32)
    mid_gain, fin_gain, inner_bias = vec(mid_g_in), vec(fin_g_in), vec(inner_b_in)
    att = jnp.concatenate(
        [jnp.concatenate([recv[u * PAIRS + p] for p in range(PAIRS)], axis=1) for u in range(2)], axis=0
    )
    copies[0].wait()
    middle_in = hidden()[...] + nn(att, out_w[...]) + vec(out_b)
    xm, rm = stats(middle_in)
    middle = xm * mid_gain + vec(mid_s_in)
    middle_b = middle.astype(bf16)
    order = owner_order(core)
    mid = nn(middle_b, order).astype(bf16)
    att_p = nn(att, order).astype(bf16)
    own, send = own_out, send_out

    own[:, O_MID : O_MID + 384] = mid[:, :384]
    own[:, O_ATT : O_ATT + 384] = att_p[:, :384]
    send[:, S_MID : S_MID + 384] = mid[:, 384:]
    send[:, S_ATT : S_ATT + 384] = att_p[:, 384:]
    bias[0:1, :] = inner_bias
    total[...] = jnp.zeros_like(total)

    def block(q):
        return pl.ds(pl.multiple_of(q * D, D), D)

    def forward(q, carry):
        cols = block(q)
        pltpu.make_async_copy(inner_w_in.at[:, cols], inner_w.at[:, cols], sems.at[1 + 2 * q]).wait()
        pre = nn(middle_b, inner_w[:, cols]) + bias[0:1, cols]
        c, density = normal(pre)
        inner_b = (pre * c).astype(bf16)
        act[:, cols] = inner_b
        slope[:, cols] = c + pre * density
        pltpu.make_async_copy(outer_w_in.at[cols, :], outer_w.at[cols, :], sems.at[2 + 2 * q]).wait()
        total[...] += nn(inner_b, outer_w[cols, :])
        return carry

    lax.fori_loop(0, 4, forward, 0)
    outer = total[...]
    first = core == 0
    for y in range(4):
        even = act[:, 2 * y * 384 : (2 * y + 1) * 384]
        odd = act[:, (2 * y + 1) * 384 : (2 * y + 2) * 384]
        own[:, O_INNER + y * 384 : O_INNER + (y + 1) * 384] = jnp.where(first, even, odd)
        send[:, S_INNER + y * 384 : S_INNER + (y + 1) * 384] = jnp.where(first, odd, even)
    final_in = middle + keep * (outer + vec(outer_b))
    xf, rf = stats(final_in)
    act_out.put((xf * fin_gain + vec(fin_s_in)).astype(bf16))
    gfi, fin_g, fin_s = norm_back(xf, rf, fin_gain, cot()[...].astype(f32))
    grad_outer = (keep * gfi).astype(bf16)
    send[:, S_GO : S_GO + D] = grad_outer
    total[...] = gfi

    def backward(q, carry):
        cols = block(q)
        grad_inner = (slope[:, cols] * nt(grad_outer, outer_w[cols, :])).astype(bf16)
        send[:, pl.ds(pl.multiple_of(S_GI + q * D, 128), D)] = grad_inner
        small_out.ref[pl.ds(3 + q, 1), :] = col_sum(grad_inner)
        total[...] += nt(grad_inner, inner_w[:, cols])
        return carry

    lax.fori_loop(0, 4, backward, 0)
    grad_middle = total[...]
    gmi, mid_g, mid_s = norm_back(xm, rm, mid_gain, grad_middle)
    gmi_out.put(gmi)
    grad_attn = gmi.astype(bf16)
    send[:, S_GA : S_GA + D] = grad_attn
    grad_att = nt(grad_attn, out_w[...]).astype(bf16)
    for u in range(2):
        for p in range(PAIRS):
            grad_att_out.ref[u * PAIRS + p] = grad_att[u * 64 : (u + 1) * 64, p * 128 : (p + 1) * 128]
    grad_att_out.ref[2 * PAIRS :] = jnp.zeros((SEQ - 2 * PAIRS, 64, 128), bf16)
    grad_att_out.flush()
    for row, value in ((0, fin_g), (1, fin_s), (2, col_sum(grad_outer)), (7, mid_g), (8, mid_s), (9, col_sum(grad_attn))):
        small_out.ref[row : row + 1, :] = value
    small_out.ref[10:16, :] = jnp.zeros((6, D), f32)
    small_out.flush()


def dense_grads_kernel(own, sent, got, spill):
    out = spill.ref

    def right(start):
        return jnp.concatenate([sent[:, start : start + D], got[:, start : start + D]], axis=0)

    def left(start, theirs, width):
        return jnp.concatenate([own[:, start : start + width], got[:, theirs : theirs + width]], axis=0)

    mid = left(O_MID, S_MID, 384)
    mid_t = mid.T
    sixes = [nn(mid_t, right(S_GI + q * D)).astype(bf16) for q in range(4)]
    sixes.append(nn(left(O_ATT, S_ATT, 384).T, right(S_GA)).astype(bf16))
    outer = nn(left(O_INNER, S_INNER, 1536).T, right(S_GO))
    dst, src = iota((512, 480), 0), iota((1, 480), 1)
    q = int_div(src, 96)
    n = int_div(src - 96 * q, 6)
    j = src - 96 * q - 6 * n
    order = (dst == n * 32 + q * 6 + j).astype(f32).astype(bf16)
    for quarter in range(4):
        rows = slice(quarter * 96, quarter * 96 + 96)
        block = nn(order, jnp.concatenate([x[rows] for x in sixes], axis=0))
        for k in range(4):
            s = quarter * 4 + k
            for y in range(0, 4, 2):
                pieces = []
                for m in (y, y + 1):
                    pieces.append(block[(k * 4 + m) * 32 : (k * 4 + m) * 32 + 32])
                    pieces.append(outer[m * 384 + s * 24 : m * 384 + s * 24 + 24])
                out[s, y * CHUNK : (y + 2) * CHUNK, :] = jnp.concatenate(pieces, axis=0).astype(bf16)
        spill.flush(slice(quarter * 4, quarter * 4 + 4))


def qkv_back_kernel(
    recv, gmi, pre_in, masked, gain_in, weight, send_out, small_out, scratch
):
    pre = pre_in()[...]
    gain = vec(gain_in)
    xhat, r = stats(masked()[...] + gelu(pre))
    grad_hidden = gmi()[...]
    sums = []
    for slot in range(3):
        part = jnp.concatenate(
            [
                jnp.concatenate([recv[u * PAIRS + p, slot * 64 : (slot + 1) * 64, :] for p in range(PAIRS)], axis=1)
                for u in range(2)
            ],
            axis=0,
        )
        sums.append(col_sum(part))
        grad_hidden += nt(part, weight()[:, slot * D : (slot + 1) * D])
    grad_summed, enc_g, enc_s = norm_back(xhat, r, gain, grad_hidden)
    grad_conv = (gelu_slope(pre) * grad_summed).astype(bf16).astype(f32)
    for k, x in enumerate((grad_conv, grad_summed)):
        for g, rows in enumerate(rows_to_groups(x, scratch)):
            send_out[g, k * 16 : k * 16 + 16, :] = rows.astype(bf16)
    for row, value in enumerate((enc_g, enc_s, sums[0], sums[2], jnp.sum(grad_conv, axis=0, keepdims=True))):
        small_out.ref[row : row + 1, :] = value
    small_out.ref[5:8, :] = jnp.zeros((3, D), f32)
    small_out.flush()


def feats_back_kernel(grad, feats, gain_in, weight, feats_out, scratch):
    grad_proj = groups_to_rows(grad, scratch).astype(bf16)
    xhat, r = stats(feats()[...].astype(f32))
    feats_out[...] = norm_back(xhat, r, vec(gain_in), nt(grad_proj, weight()[...]))[0]


def tail_kernel(
    grad_in, small_a, small_b, weight, high, low, normed, qkv_rows, tail_out, frames, spread, by_four
):
    group = lax.axis_index("seq")
    lane = iota((1, 128), 1)
    ref = grad_in()
    grad = jnp.concatenate([ref[p].astype(f32) for p in range(SEQ)], axis=0)
    for f in range(SUPER):
        moved = pltpu.roll(grad, SW - f * GW, 1) if f else grad
        frames[pl.ds(f, 256, stride=SUPER), :] = jnp.where(lane < GW, moved[:, :128], 0.0)
    grads = frames[...].astype(bf16)
    grads_t = grads.T
    pick = (iota((128, D), 1) == iota((128, D), 0) + group * GW) & (iota((128, 1), 0) < GW)
    own_weight = nt(pick.astype(f32).astype(bf16), weight()[...])
    sums = jnp.sum(grads_t.astype(f32), axis=1, keepdims=True)
    in_g = jnp.sum(own_weight * (nn(grads_t, high()[...]) + nn(grads_t, low()[...])), axis=0, keepdims=True)
    in_s = jnp.sum(own_weight * sums, axis=0, keepdims=True)
    by_four[...] = nn(grads_t, normed()[...]).T
    bias = jnp.sum(grads.astype(f32), axis=0, keepdims=True)
    place = pick.astype(f32).astype(bf16)
    bias_high = bias.astype(bf16)
    bias_low = (bias - bias_high.astype(f32)).astype(bf16)
    proj_b = nn(jnp.concatenate([bias_high] * 8, axis=0), place) + nn(jnp.concatenate([bias_low] * 8, axis=0), place)
    a = lambda k: small_a()[k : k + 1, :]
    b = lambda k: small_b()[k : k + 1, :]
    vectors = [proj_b[:1], b(4), b(0), b(1), b(2), b(3), a(9), a(7), a(8), a(2), a(0), a(1)]
    lane6 = iota((1, D), 1)
    slot6 = lane6 - 6 * int_div(lane6, 6)
    sub = iota((8, D), 0)
    main = jnp.concatenate([jnp.where(slot6 == sub, v, 0.0) for v in vectors] + [jnp.zeros((32, D), f32)], axis=0)
    sub24 = iota((24, D), 0)
    slot24 = lane6 - 24 * int_div(lane6, 24)
    inner = [
        jnp.concatenate(
            [jnp.zeros((96, D), f32), jnp.where(slot24 == sub24, a(3 + k), 0.0), jnp.zeros((8, D), f32)], axis=0
        )
        for k in range(4)
    ]
    lane4, sub4 = iota((8, C_IN), 1) & 3, iota((8, C_IN), 0)
    last = jnp.concatenate(
        [
            jnp.zeros((120, C_IN), f32),
            jnp.where(lane4 == sub4, in_g, 0.0) + jnp.where(lane4 == sub4 - 4, in_s, 0.0),
        ],
        axis=0,
    )
    own = iota((128, D), 0)
    pick6 = (int_div(lane6, 6) == own).astype(f32).astype(bf16)
    pick24 = [(int_div(lane6, 24) + 32 * k == own).astype(f32).astype(bf16) for k in range(4)]
    pick4 = ((iota((1, C_IN), 1) >> 2) == iota((128, C_IN), 0)).astype(f32).astype(bf16)
    spread[...] = jnp.zeros_like(spread)
    both = jnp.zeros((128, 256), f32)
    for p, m in [(pick6, main)] + list(zip(pick24, inner)) + [(pick4, last)]:
        high_m = m.astype(bf16)
        low_m = (m - high_m.astype(f32)).astype(bf16)
        both += nt(p, jnp.concatenate([high_m, low_m], axis=0))
    for k in range(2):
        spread[pl.ds(k * 1024 + 6, 128, stride=8), :] = both[:, k * 128 : (k + 1) * 128]
    for k in range(2):
        first, second = [by_four[pl.ds(2 * k + n, 128, stride=4), :] for n in range(2)]
        spread[pl.ds(2048 + 6 + k, 128, stride=8), :] = first + pltpu.roll(second, GW, 1)
    rows = qkv_rows()
    for k in range(3):
        lanes = slice(k * 128, (k + 1) * 128)
        tail_out[:, lanes] = (rows[:, lanes].astype(f32) + spread[k * 1024 : (k + 1) * 1024, :]).astype(bf16)


def tail_sum_kernel(got, qkv_out, proj_out, *vector_outs):
    small = jnp.zeros((1, 128), f32)
    proj = [jnp.zeros((1, D), f32)] * 4
    sums = []
    for d in range(SEQ):
        total = got[d].astype(f32)
        for b in range(1, 8):
            total += got[b * SEQ + d].astype(f32)
        sums.append(total)
        small += total[6:7, :128] + total[6:7, 128:256]
        for k in range(4):
            piece = total[6 + k // 2 : 7 + k // 2, 256:]
            wide = jnp.concatenate([piece, jnp.zeros((1, D - 128), f32)], axis=1)
            shift = (d * GW - (k % 2) * GW) % D
            lane = iota((1, D), 1)
            start = (k % 2) * GW
            wide = jnp.where((lane >= start) & (lane < start + GW), wide, 0.0)
            proj[k] += pltpu.roll(wide, shift, 1) if shift else wide
    for p in range(PAIRS):
        pair = sums[p] + sums[PAIRS + p]
        for k in range(3):
            start = k * D + p * 128
            qkv_out[:, start : start + 128] = pair[:6, k * 128 : (k + 1) * 128]
    for k in range(4):
        proj_out[k : k + 1, :] = proj[k]
    starts = [120, 124] + [8 * k for k in range(7)] + [56, 64, 96, 72, 80, 88]
    for start, out in zip(starts, vector_outs):
        out[...] = small[0, start : start + out.shape[0]]


def to_peers(x, axis, groups=None):
    return lax.all_to_all(x, axis, 0, 0, tiled=True, axis_index_groups=groups)


Y_GROUPS = [[0, 2, 4, 6], [1, 3, 5, 7]]


def local(
    feats, lengths, skip_flag, cotangent, input_gain, input_shift, proj_weight, proj_bias, conv_weight, conv_bias,
    encoder_gain, encoder_shift, qkv_weight, query_bias, value_bias, output_weight, output_bias, middle_gain,
    middle_shift, inner_weight, inner_bias, outer_weight, outer_bias, final_gain, final_shift,
):
    seq = lax.axis_index("seq")
    rows_in = feats.reshape(ROWS, C_IN)
    cot = cotangent.reshape(ROWS, D)

    masked, conv_send = call(
        project_kernel,
        [Spill((ROWS, D), f32), shape((GROUPS, 16, SW), bf16)],
        Smem(lengths), Hbm(rows_in), Hbm(input_gain), Hbm(input_shift), Hbm(proj_weight), Hbm(proj_bias),
        flops=2 * ROWS * C_IN * D, name="project", scratch=[TRANSPOSE_SCRATCH],
    )
    conv_x = to_peers(conv_send, "seq")
    own_taps = lax.dynamic_slice_in_dim(conv_weight, seq * GW, GW, axis=0)
    taps = own_taps.transpose(0, 2, 1).reshape(GW, KW * GW)
    shifted = pltpu.VMEM((2, 144, SW), f32)
    conv_flops = 2 * 256 * SW * BAND
    conv_y, conv_x = call(
        conv_kernel, [shape((SEQ, 16, SW), bf16), Copy((SEQ, 16, SW), bf16, 0)], conv_x, Hbm(taps),
        scratch=[pltpu.VMEM((SW, BAND), bf16), shifted],
        flops=conv_flops, name="conv", mib=24,
    )
    conv_back = to_peers(conv_y, "seq")
    conv_pre, hidden, qkv_send, rows_send = call(
        qkv_kernel,
        [
            Spill((ROWS, D), f32), Spill((ROWS, D), f32), Spill((SEQ, 192, 128), bf16, parts=3),
            Spill((ROWS, D + C_IN), bf16),
        ],
        conv_back, Hbm(masked), Hbm(conv_bias), Hbm(encoder_gain), Hbm(encoder_shift), Hbm(qkv_weight), Hbm(query_bias),
        Hbm(value_bias), Hbm(rows_in), flops=2 * ROWS * D * 3 * D, name="qkv", scratch=[TRANSPOSE_SCRATCH],
    )
    qkv = to_peers(qkv_send, "seq")
    rows_all = lax.all_gather(rows_send, "seq", axis=0, tiled=True).reshape(SEQ, 2, 64, D + C_IN)
    attended, logs, attended_full, qkv_kept = call(
        attend_kernel,
        [shape((1024, 128), bf16), Spill((1024, 128), f32), Spill((1024, 128), f32), Copy((SEQ, 192, 128), bf16, 1)],
        Smem(lengths), qkv, flops=8 * 1024 * 1024 * 128, name="attend", mib=32,
    )
    att_recv = to_peers(attended.reshape(SEQ, 64, 128), "seq")
    activations, grad_att_send, gmi, pair_send, pair_own, small_a = call(
        middle_kernel,
        [
            Spill((ROWS, D), bf16), Spill((SEQ, 64, 128), bf16), Spill((ROWS, D), f32),
            shape((ROWS, S_END), bf16), shape((ROWS, O_END), bf16), Spill((16, D), f32),
        ],
        Smem(skip_flag), att_recv, Hbm(hidden), Hbm(cot), Raw(output_weight), Hbm(output_bias), Hbm(middle_gain),
        Hbm(middle_shift), Raw(inner_weight), Hbm(inner_bias), Raw(outer_weight), Hbm(outer_bias), Hbm(final_gain),
        Hbm(final_shift),
        scratch=[
            pltpu.VMEM((ROWS, FF), bf16), pltpu.VMEM((ROWS, FF), f32), pltpu.VMEM((D, D), bf16),
            pltpu.VMEM((D, FF), bf16), pltpu.VMEM((FF, D), bf16), pltpu.VMEM((8, FF), f32), pltpu.VMEM((ROWS, D), f32),
            pltpu.SemaphoreType.DMA((9,)),
        ],
        flops=2 * ROWS * (4 * D * FF + 2 * D * D), name="middle", mib=32,
    )
    swap = [(i, i ^ 1) for i in range(8)]
    pair_got = lax.ppermute(pair_send, "batch", swap)
    grad_att = to_peers(grad_att_send, "seq").reshape(1024, 128)
    (dense,) = call(
        dense_grads_kernel, [Spill((SEQ, 4 * CHUNK, D), bf16, parts=4)], pair_own, pair_send, pair_got,
        flops=2 * 256 * D * 3456, name="dense_grads", mib=24,
    )
    dense, grad_att = lax.optimization_barrier((dense, grad_att))
    dense_part = lax.psum_scatter(dense.reshape(SEQ * 4 * CHUNK, D), "seq", scatter_dimension=0, tiled=True)

    (grad_qkv_send,) = call(
        attend_back_kernel, [Spill((SEQ, 192, 128), bf16)], Smem(lengths), Hbm(qkv_kept), grad_att, Hbm(logs), Hbm(attended_full),
        scratch=[pltpu.VMEM((1024, 128), f32)] * 2 + [pltpu.VMEM((128, Q_BLOCK), f32)], flops=20 * 1024 * 1024 * 128,
        name="attend_back",
    )
    grad_qkv = to_peers(grad_qkv_send, "seq")
    (qkv_rows,) = call(
        head_grads_kernel, [Spill((1024, 384), bf16)], Raw(rows_all), Hbm(grad_qkv_send),
        scratch=[pltpu.VMEM((SEQ, 64, D), bf16), pltpu.SemaphoreType.DMA((1,))], flops=4 * 1024 * D * 384,
        name="head_grads", mib=24,
    )
    frames_normed, frames_high, frames_low = call(
        frames_kernel, [Spill((2048, C_IN), bf16) for _ in range(3)], Raw(rows_all), Hbm(input_gain), Hbm(input_shift),
        scratch=[pltpu.VMEM((SEQ, 2, 64, C_IN), bf16), pltpu.SemaphoreType.DMA((1,))], name="frames", mib=32,
    )
    gmi, qkv_rows, frames_normed = lax.optimization_barrier((gmi, qkv_rows, frames_normed))
    back_send, small_b = call(
        qkv_back_kernel, [shape((SEQ, 32, SW), bf16), Spill((8, D), f32)],
        grad_qkv, Hbm(gmi), Hbm(conv_pre), Hbm(masked), Hbm(encoder_gain), Hbm(qkv_weight),
        scratch=[TRANSPOSE_SCRATCH], flops=2 * ROWS * D * 3 * D, name="qkv_back",
    )
    back_got = to_peers(back_send, "seq")
    back_other = lax.ppermute(back_got, "batch", swap)
    x_other = lax.ppermute(conv_x, "batch", swap)
    (grad_proj,) = call(
        conv_back_kernel, [shape((SEQ, 16, SW), bf16)], Smem(lengths), Hbm(back_got), Hbm(taps),
        scratch=[pltpu.VMEM((BAND, SW), bf16), shifted], flops=conv_flops, name="conv_back", mib=24,
    )
    grad_proj_got = to_peers(grad_proj, "seq")
    (tail,) = call(
        tail_kernel, [shape((1024, 384), bf16)], Hbm(grad_proj), Hbm(small_a), Hbm(small_b),
        Hbm(proj_weight), Hbm(frames_high), Hbm(frames_low), Hbm(frames_normed), Hbm(qkv_rows),
        scratch=[pltpu.VMEM((2048, 128), f32), pltpu.VMEM((3072, 128), f32), pltpu.VMEM((C_IN, 128), f32)],
        flops=6 * 2048 * C_IN * 128, name="tail", mib=32,
    )
    x_other, _ = lax.optimization_barrier((x_other, tail))
    tap_chunks = call(
        conv_weight_kernel, [Spill((GW, D), bf16) for _ in range(4)], Hbm(back_got), Hbm(back_other), Hbm(conv_x),
        Hbm(x_other),
        scratch=[
            pltpu.VMEM((192, BAND), f32), pltpu.VMEM((24, BAND), f32), pltpu.VMEM((192, 128), f32),
            pltpu.VMEM((4, GW, D), bf16), pltpu.VMEM((2, 2, 144, SW), f32),
        ],
        flops=conv_flops, name="conv_grads", mib=32,
    )
    tail, grad_proj_got, *tap_chunks = lax.optimization_barrier((tail, grad_proj_got, *tap_chunks))
    tap_got = []
    for k, piece in enumerate(tap_chunks):
        moves = [
            (b * 16 + g, (g // 2) * 16 + 8 * (g % 2) + 2 * ((b // 2 + k) % 4) + b % 2)
            for b in range(8)
            for g in range(GROUPS)
        ]
        tap_got.append(lax.ppermute(piece, ("batch", "seq"), moves))
    tail_got = to_peers(tail, ("batch", "seq"))
    (tap_own,) = call(conv_sum_kernel, [shape((GW, D), f32)], *[Hbm(x) for x in tap_got], name="conv_sum")
    grad_conv_weight = tap_own.reshape(6, KW, GW).transpose(0, 2, 1)
    dense_own = lax.psum_scatter(dense_part, "batch", scatter_dimension=0, tiled=True, axis_index_groups=Y_GROUPS)
    (grad_feats,) = call(
        feats_back_kernel, [shape((ROWS, C_IN), f32)], grad_proj_got, Hbm(rows_in), Hbm(input_gain), Hbm(proj_weight),
        scratch=[TRANSPOSE_SCRATCH], flops=2 * ROWS * C_IN * D, name="feats_back",
    )
    grad_inner_weight, grad_outer_weight, grad_output_weight = call(
        dense_sum_kernel, [shape((6, FF), f32), shape((24, D), f32), shape((6, D), f32)], Hbm(dense_own),
        name="dense_sum",
    )
    widths = [4, 4] + [6] * 9 + [24] + [6] * 3
    (
        grad_qkv_weight, grad_proj_weight, g_in_g, g_in_s, g_proj_b, g_conv_b, g_enc_g, g_enc_s, g_q_b, g_v_b, g_out_b, g_mid_g, g_mid_s,
        g_inner_b, g_outer_b, g_fin_g, g_fin_s,
    ) = call(
        tail_sum_kernel, [shape((6, 3 * D), f32), shape((4, D), f32)] + [shape((w,), f32) for w in widths],
        tail_got.reshape(128, 8, 384),
        name="tail_sum",
    )
    return (
        activations.reshape(2, 64, D), grad_feats.reshape(2, 64, C_IN), g_in_g, g_in_s, grad_proj_weight, g_proj_b,
        grad_conv_weight, g_conv_b, g_enc_g, g_enc_s, grad_qkv_weight, g_q_b, g_v_b, grad_output_weight, g_out_b,
        g_mid_g, g_mid_s, grad_inner_weight, g_inner_b, grad_outer_weight, g_outer_b, g_fin_g, g_fin_s,
    )


def solution(mesh):
    split = P("batch", "seq", None)
    both = ("batch", "seq")
    placed = (split, P("batch"), P("batch"), split) + (P(),) * 21
    row, matrix = P(both), P(both, None)
    return jax.shard_map(
        local,
        mesh=mesh,
        in_specs=placed,
        out_specs=(
            split, split, row, row, matrix, row, P(both, None, None), row, row, row, matrix, row, row, matrix, row,
            row, row, matrix, row, matrix, row, row, row,
        ),
        check_vma=False,
    )
```

```python
import functools

import jax
import jax.numpy as jnp
from jax import lax
from jax.experimental import pallas as pl
from jax.experimental.pallas import tpu as pltpu
from jax.sharding import PartitionSpec as P

f32 = jnp.float32
bf16 = jnp.bfloat16
i32 = jnp.int32

norm_eps = 1e-05
head_scale = 0.125
neg_fill = -1e30

D = 768
C_IN = 512
FF = 3072
GROUPS = 16
GW = 48
KW = 128
SUPER = 8
SW = SUPER * GW
TAP_BLOCKS = 17
BAND = TAP_BLOCKS * SW
ROWS = 128
SEQ = 16
PAIRS = 6
MIB = 1024 * 1024
TRANSPOSE_SCRATCH = pltpu.VMEM((D, 128), f32)

def nn(a, b):
    return lax.dot_general(a, b, (((1,), (0,)), ((), ())), preferred_element_type=f32)


def nt(a, b):
    return lax.dot_general(a, b, (((1,), (1,)), ((), ())), preferred_element_type=f32)


def tn(a, b):
    return lax.dot_general(a, b, (((0,), (0,)), ((), ())), preferred_element_type=f32)


def iota(shape, dim):
    return lax.broadcasted_iota(i32, shape, dim)


def int_div(x, c):
    return ((x.astype(f32) + 0.5) * (1.0 / c)).astype(i32)


def stats(x):
    c = x - jnp.mean(x, axis=-1, keepdims=True)
    r = lax.rsqrt(jnp.mean(c * c, axis=-1, keepdims=True) + norm_eps)
    return c * r, r


def norm_back(xhat, r, gain, g):
    e = g * gain
    dx = r * (e - jnp.mean(e, axis=-1, keepdims=True) - xhat * jnp.mean(e * xhat, axis=-1, keepdims=True))
    return dx, jnp.sum(g * xhat, axis=0, keepdims=True), jnp.sum(g, axis=0, keepdims=True)


def normal(x):
    bell = jnp.exp(-0.5 * x * x)
    t = 1.0 / (1.0 + (0.3275911 * 0.7071067811865476) * jnp.abs(x))
    poly = t * (0.127414796 + t * (-0.142248368 + t * (0.7107068705 + t * (-0.7265760135 + t * 0.5307027145))))
    tail = poly * bell
    return jnp.where(x < 0, tail, 1.0 - tail), 0.3989422804014327 * bell


def gelu(x):
    return x * normal(x)[0]


def gelu_slope(x):
    c, density = normal(x)
    return c + x * density


def col_sum(x):
    return jnp.sum(x.astype(f32), axis=0, keepdims=True)


def vec(lazy):
    ref = lazy()
    return ref[...].astype(f32).reshape(1, ref.shape[0])


def swap_blocks(xs):
    ys = [pltpu.roll(x, f * GW, 1) if f else x for f, x in enumerate(xs)]
    lane = iota((16, 128), 1)
    outs = []
    for g in range(SUPER):
        tiles = []
        for v in range(SW // 128):
            lo, hi = (128 * v) // GW, (128 * v + 127) // GW
            tile = ys[(lo - g) % SUPER][:, v * 128 : (v + 1) * 128]
            for q in range(lo + 1, hi + 1):
                tile = jnp.where(lane >= q * GW - 128 * v, ys[(q - g) % SUPER][:, v * 128 : (v + 1) * 128], tile)
            tiles.append(tile)
        w = jnp.concatenate(tiles, axis=1)
        outs.append(pltpu.roll(w, SW - g * GW, 1) if g else w)
    return outs


LANE_TILES = D // 128


def rows_to_groups(x, scratch):
    for v in range(LANE_TILES):
        scratch[v * ROWS : (v + 1) * ROWS, :] = x[:, v * 128 : (v + 1) * 128]
    outs = []
    for half in range(2):
        tiles = range(half * 3, half * 3 + 3)
        outs += swap_blocks(
            [
                jnp.concatenate([scratch[pl.ds(v * ROWS + f, 16, stride=SUPER), :] for v in tiles], axis=1)
                for f in range(SUPER)
            ]
        )
    return outs


def groups_to_rows(in_ref, scratch):
    for half in range(2):
        xs = [in_ref[half * 8 + g].astype(f32) for g in range(SUPER)]
        for f, x in enumerate(swap_blocks(xs)):
            for v in range(3):
                row = (half * 3 + v) * ROWS + f
                scratch[pl.ds(row, 16, stride=SUPER), :] = x[:, v * 128 : (v + 1) * 128]
    return jnp.concatenate([scratch[v * ROWS : (v + 1) * ROWS, :] for v in range(LANE_TILES)], axis=1)


class Hbm:
    def __init__(self, array):
        self.array = array


class Raw(Hbm):
    pass


class Smem(Hbm):
    pass


class Spill:
    def __init__(self, dims, dtype, parts=1):
        self.struct, self.parts = jax.ShapeDtypeStruct(dims, dtype), parts


class Copy:
    parts = 1

    def __init__(self, dims, dtype, operand):
        self.struct, self.operand = jax.ShapeDtypeStruct(dims, dtype), operand


class Flusher:
    def __init__(self, ref, target, sems, base, copies):
        self.ref, self.target, self.sems, self.next, self.copies = ref, target, sems, base, copies

    def put(self, value):
        self.ref[...] = value
        self.flush()

    def flush(self, *index):
        src, dst = (self.ref.at[index], self.target.at[index]) if index else (self.ref, self.target)
        copy = pltpu.make_async_copy(src, dst, self.sems.at[self.next])
        copy.start()
        self.next += 1
        self.copies.append(copy)


class Lazy:
    def __init__(self, copy, ref):
        self.copy, self.ref, self.waited = copy, ref, False

    def __call__(self):
        if not self.waited:
            self.copy.wait()
            self.waited = True
        return self.ref


def call(body, outs, *args, scratch=(), flops=0, name=None, mib=16):
    fetched = [k for k, a in enumerate(args) if type(a) in (Hbm, Smem)]
    spilled = [k for k, o in enumerate(outs) if isinstance(o, Spill)]
    copied = [k for k, o in enumerate(outs) if isinstance(o, Copy)]
    arrays = [
        pltpu.with_memory_space_constraint(a.array, pltpu.HBM) if isinstance(a, Hbm) and not isinstance(a, Smem) else getattr(a,'array',a) for a in args
    ]
    structs = [o.struct if isinstance(o, (Spill, Copy)) else o for o in outs]
    near = {Hbm: pltpu.VMEM, Smem: pltpu.SMEM}
    own = [near[type(args[k])](arrays[k].shape, arrays[k].dtype) for k in fetched]
    own += [pltpu.VMEM(structs[k].shape, structs[k].dtype) for k in spilled]
    sem_count = len(fetched) + sum(outs[k].parts for k in spilled) + len(copied)
    if sem_count:
        own.append(pltpu.SemaphoreType.DMA((sem_count,)))

    def wrapped(*refs):
        n_in, n_out = len(args), len(outs)
        ins, out_refs, rest = list(refs[:n_in]), list(refs[n_in : n_in + n_out]), list(refs[n_in + n_out :])
        extra, rest = rest[: len(own)], rest[len(own) :]
        lazies, flushed = [], []
        for slot, k in enumerate(fetched):
            copy = pltpu.make_async_copy(ins[k], extra[slot], extra[-1].at[slot])
            copy.start()
            ins[k] = Lazy(copy, extra[slot])
            lazies.append(ins[k])
        base = len(fetched)
        for slot, k in enumerate(spilled):
            out_refs[k] = Flusher(extra[len(fetched) + slot], out_refs[k], extra[-1], base, flushed)
            base += outs[k].parts
        for k in copied:
            out_refs[k] = Flusher(refs[outs[k].operand], out_refs[k], extra[-1], base, flushed)
            base += 1
        body(*ins, *out_refs, *rest)
        for lazy in lazies:
            lazy()
        for copy in flushed:
            copy.wait()

    bytes_accessed = sum(a.size * a.dtype.itemsize for a in arrays) + sum(o.size * o.dtype.itemsize for o in structs)
    return pl.pallas_call(
        wrapped,
        out_shape=[pltpu.HBM(o.struct.shape, o.struct.dtype) if isinstance(o, (Spill, Copy)) else o for o in outs],
        in_specs=[pl.BlockSpec(memory_space=pltpu.HBM if isinstance(a, Hbm) else pltpu.VMEM) for a in args],
        out_specs=[pl.BlockSpec(memory_space=pltpu.HBM if isinstance(o, (Spill, Copy)) else pltpu.VMEM) for o in outs],
        scratch_shapes=own + list(scratch),
        compiler_params=pltpu.CompilerParams(vmem_limit_bytes=mib * MIB),
        cost_estimate=pl.CostEstimate(flops=flops, bytes_accessed=bytes_accessed, transcendentals=0),
        name=name,
    )(*arrays)


def fetch(sems, *pairs):
    copies = [pltpu.make_async_copy(src, dst, sems.at[k]) for k, (src, dst) in enumerate(pairs)]
    for copy in copies:
        copy.start()
    return copies


def shape(dims, dtype):
    return jax.ShapeDtypeStruct(dims, dtype)


def live_rows(lengths):
    row = iota((ROWS, 1), 0)
    frame = (row & 63) + lax.axis_index("seq") * 64
    ref = lengths()
    length = jnp.where(row < 64, ref[0], ref[1])
    return (frame < length).astype(f32)


def head_utterance():
    return (lax.axis_index("seq") >= PAIRS).astype(i32)


def core_index():
    return lax.axis_index("batch") & 1


def project_kernel(feats, gain, shift, weight, bias, projected_out, send_out, scratch):
    xhat, _ = stats(feats()[...].astype(f32))
    normed = (xhat * vec(gain) + vec(shift)).astype(bf16)
    projected = nn(normed, weight()[...]) + vec(bias)
    projected_out.put(projected)
    for g, x in enumerate(rows_to_groups(projected, scratch)):
        send_out[g] = x.astype(bf16)


def band_rows(taps):
    flat = jnp.concatenate([taps[...].astype(f32), jnp.zeros((GW, SW), f32)], axis=1)
    return [(pltpu.roll(flat, f * GW, 1) if f else flat).astype(bf16) for f in range(SUPER)]


def padded(pieces, scratch):
    for u in range(2):
        scratch[u, 0:8, :] = jnp.zeros((8, SW), f32)
        scratch[u, 136:144, :] = jnp.zeros((8, SW), f32)
        for p, x in enumerate(pieces):
            scratch[u, 8 + p * 8 : 16 + p * 8, :] = x[u * 8 : u * 8 + 8]


def windows(scratch, starts):
    parts = [
        jnp.concatenate([scratch[u, start : start + 128, :] for u in range(2)], axis=0).astype(bf16) for start in starts
    ]
    return jnp.concatenate(parts, axis=1)


def by_seq(x, p):
    return jnp.concatenate([x[u * 128 + p * 8 : u * 128 + p * 8 + 8] for u in range(2)], axis=0)


def group_live(ref, p):
    row, f = iota((16, SW), 0), int_div(iota((1, SW), 1), GW)
    return p * 64 + (row & 7) * SUPER + f < jnp.where(row < 8, ref[0], ref[1])


def conv_kernel(lengths, x, taps, out, x_out, w, scratch):
    ref = lengths()
    masked = [jnp.where(group_live(ref, p), x[p].astype(f32), 0.0) for p in range(SEQ)]
    for p in range(SEQ):
        x_out.ref[p] = masked[p].astype(bf16)
    x_out.flush()
    padded(masked, scratch)
    for f, rows in enumerate(band_rows(taps())):
        w[f * GW : (f + 1) * GW, :] = rows
    res = nt(windows(scratch, range(TAP_BLOCKS)), w[...])
    for p in range(SEQ):
        out[p] = by_seq(res, p).astype(bf16)


CHUNK = 56


def conv_back_kernel(lengths, got_in, taps, out, w, scratch):
    for f, rows in enumerate(band_rows(taps())):
        for i in range(TAP_BLOCKS):
            w[i * SW + f * GW : i * SW + (f + 1) * GW, :] = rows[:, i * SW : (i + 1) * SW]
    got = got_in()
    padded([got[p, :16, :].astype(f32) for p in range(SEQ)], scratch)
    res = nn(windows(scratch, range(16, -1, -1)), w[...])
    ref = lengths()
    for p in range(SEQ):
        total = by_seq(res, p) + got[p, 16:, :].astype(f32)
        out[p] = jnp.where(group_live(ref, p), total, 0.0).astype(bf16)


def conv_weight_kernel(got_in, other_in, x_in, x_other, *rest):
    tap_outs, (wide, acc, spread, chunks, scratch) = rest[:4], rest[4:]
    core = core_index()
    src, dst = iota((SW, 192), 0), iota((1, 192), 1)
    f = int_div(dst, 24)
    y = int_div(dst - 24 * f, 6)
    own_taps = (src == f * GW + (2 * y + core) * 6 + (dst - 24 * f - 6 * y)).astype(f32).astype(bf16)
    grads, parts = [], []
    for k, (got, x) in enumerate(((got_in(), x_in()), (other_in(), x_other()))):
        grad = jnp.concatenate([got[p, :16, :] for p in range(SEQ)], axis=0)
        grad = nn(grad, own_taps)
        grads.append(jnp.concatenate([grad[p * 16 + u * 8 : p * 16 + u * 8 + 8] for u in range(2) for p in range(SEQ)], axis=0))
        padded([x[p].astype(f32) for p in range(SEQ)], scratch.at[k])
        parts.append(windows(scratch.at[k], range(TAP_BLOCKS)))
    wide[...] = nn(jnp.concatenate(grads, axis=0).astype(bf16).T, jnp.concatenate(parts, axis=0))
    acc[...] = wide[7 * 24 :, :]
    for f in range(6, -1, -1):
        acc[...] = pltpu.roll(acc[...], BAND - GW, 1) + wide[f * 24 : f * 24 + 24, :]
    for v in range(LANE_TILES):
        lanes = slice(v * 128, (v + 1) * 128)
        for i in range(8):
            spread[pl.ds(i, 24, stride=8), :] = acc[:, i * D + v * 128 : i * D + (v + 1) * 128]
        for y in range(4):
            chunks[y, :, lanes] = spread[y * GW : (y + 1) * GW, :].astype(bf16)
    own_y = lax.axis_index("batch") >> 1
    for k, tap_out in enumerate(tap_outs):
        tap_out.put(chunks[(own_y + k) & 3])


def conv_sum_kernel(*refs):
    total = refs[0]()[...].astype(f32)
    for ref in refs[1:-1]:
        total += ref()[...].astype(f32)
    refs[-1][...] = total


def dense_sum_kernel(total_in, inner_out, outer_out, output_out):
    total = total_in()[...].astype(f32)
    for q in range(4):
        inner_out[:, q * D : (q + 1) * D] = total[q * 6 : q * 6 + 6]
    output_out[...] = total[24:30]
    outer_out[...] = total[32:]


def qkv_kernel(
    lengths, conv, projected, conv_bias, gain, shift, weight_in, query_bias, value_bias, feats,
    pre_out, hidden_out, send_out, rows_out, scratch, weight, sems,
):
    cols = [slice(block * D, (block + 1) * D) for block in (1, 2, 0)]
    copies = fetch(sems, *[(weight_in.at[:, c], weight.at[:, c]) for c in cols])
    pre = groups_to_rows(conv, scratch) + vec(conv_bias)
    pre_out.put(pre)
    xhat, _ = stats(projected()[...] * live_rows(lengths) + gelu(pre))
    hidden = xhat * vec(gain) + vec(shift)
    hidden_out.put(hidden)
    hidden_b = hidden.astype(bf16)
    rows_out.ref[:, :D] = hidden_b
    rows_out.ref[:, D:] = feats()[...]
    rows_out.flush()
    zero = jnp.zeros((1, D), f32)
    send = send_out.ref
    for slot, bias in enumerate((zero, vec(value_bias), vec(query_bias))):
        copies[slot].wait()
        part = (nn(hidden_b, weight[:, cols[slot]]) + bias).astype(bf16)
        for u in range(2):
            for pair in range(PAIRS):
                send[u * PAIRS + pair, slot * 64 : (slot + 1) * 64, :] = part[
                    u * 64 : (u + 1) * 64, pair * 128 : (pair + 1) * 128
                ]
        part_rows = slice(slot * 64, (slot + 1) * 64)
        send[2 * PAIRS :, part_rows, :] = jnp.zeros((SEQ - 2 * PAIRS, 64, 128), bf16)
        send_out.flush(slice(None), part_rows)


Q_BLOCK = 512


def columns(*values):
    rows = max(v.shape[0] for v in values)
    lane = iota((rows, 128), 1)
    out = jnp.zeros((rows, 128), f32)
    for k, v in enumerate(values):
        out = jnp.where(lane == k, v, out)
    return out.astype(bf16)


def three_terms(x):
    high = x.astype(bf16).astype(f32)
    mid = (x - high).astype(bf16).astype(f32)
    return high, mid, x - high - mid


def key_bias(lengths):
    ref = lengths()
    length = jnp.where(head_utterance() == 0, ref[0], ref[1])
    return jnp.where(iota((1024, 1), 0) < length, 0.0, neg_fill)


def attend_kernel(lengths, qkv, out, log_spill, out_spill, copy_spill):
    log_out, full_out = log_spill.ref, out_spill.ref
    copy_spill.flush()
    keys = jnp.concatenate([qkv[:, 0:64, :].reshape(1024, 128), columns(key_bias(lengths))], axis=1)
    values = jnp.concatenate([qkv[:, 64:128, :].reshape(1024, 128), columns(jnp.ones((1024, 1), f32))], axis=1)
    left = iota((1024, 128), 1) < 64
    query = qkv[:, 128:192, :].reshape(1024, 128) * head_scale
    parts, logs = [], []
    for head in range(2):
        own = left if head == 0 else ~left
        q_h = jnp.concatenate([jnp.where(own, query, jnp.zeros_like(query)), columns(jnp.ones((1024, 1), f32))], axis=1)
        scores = nt(q_h, keys)
        top = jnp.max(scores, axis=-1, keepdims=True)
        e = jnp.exp(scores - top).astype(bf16)
        sums = nn(e, values)
        total = sums[:, 128:129]
        parts.append(sums[:, :128] * (1.0 / total))
        logs.append(top + jnp.log(total))
    both = jnp.where(left, parts[0], parts[1])
    out[...] = both.astype(bf16)
    full_out[...] = both
    log_out[...] = jnp.where(left, logs[0], logs[1])
    log_spill.flush()
    out_spill.flush()


def attend_back_kernel(lengths, qkv_in, grad, logs_in, full_in, spill, dk, dv, dq):
    qkv, logs, full, out = qkv_in(), logs_in(), full_in(), spill.ref
    one = jnp.ones((1024, 1), f32)
    keys_only = qkv[:, 0:64, :].reshape(1024, 128)
    keys = jnp.concatenate([keys_only, columns(key_bias(lengths), one, one, one)], axis=1)
    values = jnp.concatenate([qkv[:, 64:128, :].reshape(1024, 128), columns(one, one, one)], axis=1)
    keys_t = keys_only.T
    left = iota((Q_BLOCK, 128), 1) < 64
    top_rows = iota((128, Q_BLOCK), 0) < 64
    per = Q_BLOCK // 64
    dk[...] = jnp.zeros_like(dk)
    dv[...] = jnp.zeros_like(dv)
    dq[...] = jnp.zeros_like(dq)

    def step(n, carry):
        query = qkv[pl.ds(n * per, per), 128:192, :].reshape(Q_BLOCK, 128) * head_scale
        rows = pl.ds(pl.multiple_of(n * Q_BLOCK, Q_BLOCK), Q_BLOCK)
        go = grad[rows, :]
        weighted = go.astype(f32) * full[rows, :]
        def one_head(head, carry):
            own = (left & (head == 0)) | (~left & (head == 1))
            q_h = jnp.where(own, query, jnp.zeros_like(query))
            g_h = jnp.where(own, go, jnp.zeros_like(go))
            log = jnp.where(head == 0, logs[rows, 0:1], logs[rows, 64:65])
            delta = jnp.sum(jnp.where(own, weighted, 0.0), axis=-1, keepdims=True)
            q_more = jnp.concatenate([q_h, columns(jnp.ones((Q_BLOCK, 1), f32), *three_terms(-log))], axis=1)
            g_more = jnp.concatenate([g_h, columns(*three_terms(-delta))], axis=1)
            probs = jnp.exp(nt(keys, q_more))
            grad_scores = (probs * nt(values, g_more)).astype(bf16)
            head_rows = (top_rows & (head == 0)) | (~top_rows & (head == 1))
            dq[...] = jnp.where(head_rows, nn(keys_t, grad_scores), dq[...])
            dk[...] += nn(grad_scores, q_h)
            dv[...] += nn(probs.astype(bf16), g_h)
            return carry

        lax.fori_loop(0, 2, one_head, 0)
        grad_query = (dq[...] * head_scale).T.astype(bf16)
        out[pl.ds(n * per, per), 0:64, :] = grad_query.reshape(per, 64, 128)
        return carry

    lax.fori_loop(0, 1024 // Q_BLOCK, step, 0)
    out[:, 64:128, :] = dk[...].astype(bf16).reshape(SEQ, 64, 128)
    out[:, 128:192, :] = dv[...].astype(bf16).reshape(SEQ, 64, 128)
    spill.flush()


def frames_kernel(rows_in, gain, shift, normed_out, high_out, low_out, feats, sem):
    copy = pltpu.make_async_copy(rows_in.at[:, :, :, D : D + C_IN], feats, sem.at[0])
    copy.start()
    gain_row, shift_row = vec(gain), vec(shift)
    copy.wait()

    def step(p, carry):
        rows = pl.ds(pl.multiple_of(p * 128, 128), 128)
        xhat, _ = stats(feats[p].reshape(128, C_IN).astype(f32))
        normed_out.ref[rows, :] = (xhat * gain_row + shift_row).astype(bf16)
        high = xhat.astype(bf16)
        high_out.ref[rows, :] = high
        low_out.ref[rows, :] = (xhat - high.astype(f32)).astype(bf16)
        return carry

    lax.fori_loop(0, SEQ, step, 0)
    for spill in (normed_out, high_out, low_out):
        spill.flush()


def head_grads_kernel(rows_in, grads_in, spill, hidden, sem):
    copy = pltpu.make_async_copy(rows_in.at[:, head_utterance(), :, 0:D], hidden, sem.at[0])
    copy.start()
    grads = grads_in()
    right = jnp.concatenate([grads[:, k * 64 : (k + 1) * 64, :].reshape(1024, 128) for k in range(3)], axis=1)
    copy.wait()
    res = tn(hidden[...].reshape(1024, D), right).astype(bf16)

    def step(k, carry):
        rows = pl.ds(pl.multiple_of(k * 256, 256), 256)
        dst, src = iota((256, 1), 0) + k * 256, iota((256, D), 1)
        row = jnp.where((dst & 7) < 6, (dst >> 3) * 6 + (dst & 7), -1)
        spill.ref[rows, :] = nn((src == row).astype(f32).astype(bf16), res).astype(bf16)
        return carry

    lax.fori_loop(0, 4, step, 0)
    spill.flush()


def owner_order(core):
    src, dst = iota((D, D), 0), iota((1, D), 1)
    second = dst >= 384
    rest = dst - jnp.where(second, 384, 0)
    which = jnp.where(second, 1 - core, core)
    s = int_div(rest, 24)
    y = int_div(rest - 24 * s, 6)
    j = rest - 24 * s - 6 * y
    return (src == (2 * y + which) * 96 + s * 6 + j).astype(f32).astype(bf16)


S_MID, S_GI, S_INNER, S_GO, S_ATT, S_GA, S_END = 0, 384, 3456, 4992, 5760, 6144, 6912
O_MID, O_INNER, O_ATT, O_END = 0, 384, 1920, 2304


def middle_kernel(
    skip, recv, hidden, cot, out_w_in, out_b, mid_g_in, mid_s_in, inner_w_in, inner_b_in, outer_w_in, outer_b,
    fin_g_in, fin_s_in,
    act_out, grad_att_out, gmi_out, send_out, own_out, small_out,
    act, slope, out_w, inner_w, outer_w, bias, total, sems,
):
    pairs = [(out_w_in, out_w)]
    for q in range(4):
        cols = slice(q * D, (q + 1) * D)
        pairs += [(inner_w_in.at[:, cols], inner_w.at[:, cols]), (outer_w_in.at[cols, :], outer_w.at[cols, :])]
    copies = fetch(sems, *pairs)
    core = core_index()
    keep = (1 - skip()[0]).astype(f32)
    mid_gain, fin_gain, inner_bias = vec(mid_g_in), vec(fin_g_in), vec(inner_b_in)
    att = jnp.concatenate(
        [jnp.concatenate([recv[u * PAIRS + p] for p in range(PAIRS)], axis=1) for u in range(2)], axis=0
    )
    copies[0].wait()
    middle_in = hidden()[...] + nn(att, out_w[...]) + vec(out_b)
    xm, rm = stats(middle_in)
    middle = xm * mid_gain + vec(mid_s_in)
    middle_b = middle.astype(bf16)
    order = owner_order(core)
    mid = nn(middle_b, order).astype(bf16)
    att_p = nn(att, order).astype(bf16)
    own, send = own_out, send_out

    own[:, O_MID : O_MID + 384] = mid[:, :384]
    own[:, O_ATT : O_ATT + 384] = att_p[:, :384]
    send[:, S_MID : S_MID + 384] = mid[:, 384:]
    send[:, S_ATT : S_ATT + 384] = att_p[:, 384:]
    bias[0:1, :] = inner_bias
    total[...] = jnp.zeros_like(total)

    def block(q):
        return pl.ds(pl.multiple_of(q * D, D), D)

    def forward(q, carry):
        cols = block(q)
        pltpu.make_async_copy(inner_w_in.at[:, cols], inner_w.at[:, cols], sems.at[1 + 2 * q]).wait()
        pre = nn(middle_b, inner_w[:, cols]) + bias[0:1, cols]
        c, density = normal(pre)
        inner_b = (pre * c).astype(bf16)
        act[:, cols] = inner_b
        slope[:, cols] = c + pre * density
        pltpu.make_async_copy(outer_w_in.at[cols, :], outer_w.at[cols, :], sems.at[2 + 2 * q]).wait()
        total[...] += nn(inner_b, outer_w[cols, :])
        return carry

    lax.fori_loop(0, 4, forward, 0)
    outer = total[...]
    first = core == 0
    for y in range(4):
        even = act[:, 2 * y * 384 : (2 * y + 1) * 384]
        odd = act[:, (2 * y + 1) * 384 : (2 * y + 2) * 384]
        own[:, O_INNER + y * 384 : O_INNER + (y + 1) * 384] = jnp.where(first, even, odd)
        send[:, S_INNER + y * 384 : S_INNER + (y + 1) * 384] = jnp.where(first, odd, even)
    final_in = middle + keep * (outer + vec(outer_b))
    xf, rf = stats(final_in)
    act_out.put((xf * fin_gain + vec(fin_s_in)).astype(bf16))
    gfi, fin_g, fin_s = norm_back(xf, rf, fin_gain, cot()[...].astype(f32))
    grad_outer = (keep * gfi).astype(bf16)
    send[:, S_GO : S_GO + D] = grad_outer
    total[...] = gfi

    def backward(q, carry):
        cols = block(q)
        grad_inner = (slope[:, cols] * nt(grad_outer, outer_w[cols, :])).astype(bf16)
        send[:, pl.ds(pl.multiple_of(S_GI + q * D, 128), D)] = grad_inner
        small_out.ref[pl.ds(3 + q, 1), :] = col_sum(grad_inner)
        total[...] += nt(grad_inner, inner_w[:, cols])
        return carry

    lax.fori_loop(0, 4, backward, 0)
    grad_middle = total[...]
    gmi, mid_g, mid_s = norm_back(xm, rm, mid_gain, grad_middle)
    gmi_out.put(gmi)
    grad_attn = gmi.astype(bf16)
    send[:, S_GA : S_GA + D] = grad_attn
    grad_att = nt(grad_attn, out_w[...]).astype(bf16)
    for u in range(2):
        for p in range(PAIRS):
            grad_att_out.ref[u * PAIRS + p] = grad_att[u * 64 : (u + 1) * 64, p * 128 : (p + 1) * 128]
    grad_att_out.ref[2 * PAIRS :] = jnp.zeros((SEQ - 2 * PAIRS, 64, 128), bf16)
    grad_att_out.flush()
    for row, value in ((0, fin_g), (1, fin_s), (2, col_sum(grad_outer)), (7, mid_g), (8, mid_s), (9, col_sum(grad_attn))):
        small_out.ref[row : row + 1, :] = value
    small_out.ref[10:16, :] = jnp.zeros((6, D), f32)
    small_out.flush()


def dense_grads_kernel(own, sent, got, spill):
    out = spill.ref

    def right(start):
        return jnp.concatenate([sent[:, start : start + D], got[:, start : start + D]], axis=0)

    def left(start, theirs, width):
        return jnp.concatenate([own[:, start : start + width], got[:, theirs : theirs + width]], axis=0)

    mid = left(O_MID, S_MID, 384)
    mid_t = mid.T
    sixes = [nn(mid_t, right(S_GI + q * D)).astype(bf16) for q in range(4)]
    sixes.append(nn(left(O_ATT, S_ATT, 384).T, right(S_GA)).astype(bf16))
    outer = nn(left(O_INNER, S_INNER, 1536).T, right(S_GO))
    dst, src = iota((512, 480), 0), iota((1, 480), 1)
    q = int_div(src, 96)
    n = int_div(src - 96 * q, 6)
    j = src - 96 * q - 6 * n
    order = (dst == n * 32 + q * 6 + j).astype(f32).astype(bf16)
    for quarter in range(4):
        rows = slice(quarter * 96, quarter * 96 + 96)
        block = nn(order, jnp.concatenate([x[rows] for x in sixes], axis=0))
        for k in range(4):
            s = quarter * 4 + k
            for y in range(0, 4, 2):
                pieces = []
                for m in (y, y + 1):
                    pieces.append(block[(k * 4 + m) * 32 : (k * 4 + m) * 32 + 32])
                    pieces.append(outer[m * 384 + s * 24 : m * 384 + s * 24 + 24])
                out[s, y * CHUNK : (y + 2) * CHUNK, :] = jnp.concatenate(pieces, axis=0).astype(bf16)
        spill.flush(slice(quarter * 4, quarter * 4 + 4))


def qkv_back_kernel(
    lengths, recv, gmi, pre_in, projected, gain_in, weight, send_out, small_out, scratch
):
    pre = pre_in()[...]
    gain = vec(gain_in)
    xhat, r = stats(projected()[...] * live_rows(lengths) + gelu(pre))
    grad_hidden = gmi()[...]
    sums = []
    for slot in range(3):
        part = jnp.concatenate(
            [
                jnp.concatenate([recv[u * PAIRS + p, slot * 64 : (slot + 1) * 64, :] for p in range(PAIRS)], axis=1)
                for u in range(2)
            ],
            axis=0,
        )
        sums.append(col_sum(part))
        grad_hidden += nt(part, weight()[:, slot * D : (slot + 1) * D])
    grad_summed, enc_g, enc_s = norm_back(xhat, r, gain, grad_hidden)
    grad_conv = (gelu_slope(pre) * grad_summed).astype(bf16).astype(f32)
    for k, x in enumerate((grad_conv, grad_summed)):
        for g, rows in enumerate(rows_to_groups(x, scratch)):
            send_out[g, k * 16 : k * 16 + 16, :] = rows.astype(bf16)
    for row, value in enumerate((enc_g, enc_s, sums[0], sums[2], jnp.sum(grad_conv, axis=0, keepdims=True))):
        small_out.ref[row : row + 1, :] = value
    small_out.ref[5:8, :] = jnp.zeros((3, D), f32)
    small_out.flush()


def feats_back_kernel(grad, feats, gain_in, weight, feats_out, scratch):
    grad_proj = groups_to_rows(grad, scratch).astype(bf16)
    xhat, r = stats(feats()[...].astype(f32))
    feats_out[...] = norm_back(xhat, r, vec(gain_in), nt(grad_proj, weight()[...]))[0]


def tail_kernel(
    grad_in, small_a, small_b, weight, high, low, normed, qkv_rows, tail_out, frames, spread, by_four
):
    group = lax.axis_index("seq")
    lane = iota((1, 128), 1)
    ref = grad_in()
    grad = jnp.concatenate([ref[p].astype(f32) for p in range(SEQ)], axis=0)
    for f in range(SUPER):
        moved = pltpu.roll(grad, SW - f * GW, 1) if f else grad
        frames[pl.ds(f, 256, stride=SUPER), :] = jnp.where(lane < GW, moved[:, :128], 0.0)
    grads = frames[...].astype(bf16)
    grads_t = grads.T
    pick = (iota((128, D), 1) == iota((128, D), 0) + group * GW) & (iota((128, 1), 0) < GW)
    own_weight = nt(pick.astype(f32).astype(bf16), weight()[...])
    sums = jnp.sum(grads_t.astype(f32), axis=1, keepdims=True)
    in_g = jnp.sum(own_weight * (nn(grads_t, high()[...]) + nn(grads_t, low()[...])), axis=0, keepdims=True)
    in_s = jnp.sum(own_weight * sums, axis=0, keepdims=True)
    by_four[...] = nn(grads_t, normed()[...]).T
    bias = jnp.sum(grads.astype(f32), axis=0, keepdims=True)
    place = pick.astype(f32).astype(bf16)
    bias_high = bias.astype(bf16)
    bias_low = (bias - bias_high.astype(f32)).astype(bf16)
    proj_b = nn(jnp.concatenate([bias_high] * 8, axis=0), place) + nn(jnp.concatenate([bias_low] * 8, axis=0), place)
    a = lambda k: small_a()[k : k + 1, :]
    b = lambda k: small_b()[k : k + 1, :]
    vectors = [proj_b[:1], b(4), b(0), b(1), b(2), b(3), a(9), a(7), a(8), a(2), a(0), a(1)]
    lane6 = iota((1, D), 1)
    slot6 = lane6 - 6 * int_div(lane6, 6)
    sub = iota((8, D), 0)
    main = jnp.concatenate([jnp.where(slot6 == sub, v, 0.0) for v in vectors] + [jnp.zeros((32, D), f32)], axis=0)
    sub24 = iota((24, D), 0)
    slot24 = lane6 - 24 * int_div(lane6, 24)
    inner = [
        jnp.concatenate(
            [jnp.zeros((96, D), f32), jnp.where(slot24 == sub24, a(3 + k), 0.0), jnp.zeros((8, D), f32)], axis=0
        )
        for k in range(4)
    ]
    lane4, sub4 = iota((8, C_IN), 1) & 3, iota((8, C_IN), 0)
    last = jnp.concatenate(
        [
            jnp.zeros((120, C_IN), f32),
            jnp.where(lane4 == sub4, in_g, 0.0) + jnp.where(lane4 == sub4 - 4, in_s, 0.0),
        ],
        axis=0,
    )
    own = iota((128, D), 0)
    pick6 = (int_div(lane6, 6) == own).astype(f32).astype(bf16)
    pick24 = [(int_div(lane6, 24) + 32 * k == own).astype(f32).astype(bf16) for k in range(4)]
    pick4 = ((iota((1, C_IN), 1) >> 2) == iota((128, C_IN), 0)).astype(f32).astype(bf16)
    spread[...] = jnp.zeros_like(spread)
    both = jnp.zeros((128, 256), f32)
    for p, m in [(pick6, main)] + list(zip(pick24, inner)) + [(pick4, last)]:
        high_m = m.astype(bf16)
        low_m = (m - high_m.astype(f32)).astype(bf16)
        both += nt(p, jnp.concatenate([high_m, low_m], axis=0))
    for k in range(2):
        spread[pl.ds(k * 1024 + 6, 128, stride=8), :] = both[:, k * 128 : (k + 1) * 128]
    for k in range(2):
        first, second = [by_four[pl.ds(2 * k + n, 128, stride=4), :] for n in range(2)]
        spread[pl.ds(2048 + 6 + k, 128, stride=8), :] = first + pltpu.roll(second, GW, 1)
    rows = qkv_rows()
    for k in range(3):
        lanes = slice(k * 128, (k + 1) * 128)
        tail_out[:, lanes] = (rows[:, lanes].astype(f32) + spread[k * 1024 : (k + 1) * 1024, :]).astype(bf16)


def tail_sum_kernel(got, qkv_out, proj_out, *vector_outs):
    small = jnp.zeros((1, 128), f32)
    proj = [jnp.zeros((1, D), f32)] * 4
    sums = []
    for d in range(SEQ):
        total = got[d].astype(f32)
        for b in range(1, 8):
            total += got[b * SEQ + d].astype(f32)
        sums.append(total)
        small += total[6:7, :128] + total[6:7, 128:256]
        for k in range(4):
            piece = total[6 + k // 2 : 7 + k // 2, 256:]
            wide = jnp.concatenate([piece, jnp.zeros((1, D - 128), f32)], axis=1)
            shift = (d * GW - (k % 2) * GW) % D
            lane = iota((1, D), 1)
            start = (k % 2) * GW
            wide = jnp.where((lane >= start) & (lane < start + GW), wide, 0.0)
            proj[k] += pltpu.roll(wide, shift, 1) if shift else wide
    for p in range(PAIRS):
        pair = sums[p] + sums[PAIRS + p]
        for k in range(3):
            start = k * D + p * 128
            qkv_out[:, start : start + 128] = pair[:6, k * 128 : (k + 1) * 128]
    for k in range(4):
        proj_out[k : k + 1, :] = proj[k]
    starts = [120, 124] + [8 * k for k in range(7)] + [56, 64, 96, 72, 80, 88]
    for start, out in zip(starts, vector_outs):
        out[...] = small[0, start : start + out.shape[0]]


def to_peers(x, axis, groups=None):
    return lax.all_to_all(x, axis, 0, 0, tiled=True, axis_index_groups=groups)


Y_GROUPS = [[0, 2, 4, 6], [1, 3, 5, 7]]


def local(
    feats, lengths, skip_flag, cotangent, input_gain, input_shift, proj_weight, proj_bias, conv_weight, conv_bias,
    encoder_gain, encoder_shift, qkv_weight, query_bias, value_bias, output_weight, output_bias, middle_gain,
    middle_shift, inner_weight, inner_bias, outer_weight, outer_bias, final_gain, final_shift,
):
    seq = lax.axis_index("seq")
    rows_in = feats.reshape(ROWS, C_IN)
    cot = cotangent.reshape(ROWS, D)

    projected, conv_send = call(
        project_kernel,
        [Spill((ROWS, D), f32), shape((GROUPS, 16, SW), bf16)],
        Hbm(rows_in), Hbm(input_gain), Hbm(input_shift), Hbm(proj_weight), Hbm(proj_bias),
        flops=2 * ROWS * C_IN * D, name="project", scratch=[TRANSPOSE_SCRATCH],
    )
    conv_x = to_peers(conv_send, "seq")
    own_taps = lax.dynamic_slice_in_dim(conv_weight, seq * GW, GW, axis=0)
    taps = own_taps.transpose(0, 2, 1).reshape(GW, KW * GW)
    shifted = pltpu.VMEM((2, 144, SW), f32)
    conv_flops = 2 * 256 * SW * BAND
    conv_y, conv_x = call(
        conv_kernel, [shape((SEQ, 16, SW), bf16), Spill((SEQ, 16, SW), bf16)], Smem(lengths), conv_x, Hbm(taps),
        scratch=[pltpu.VMEM((SW, BAND), bf16), shifted],
        flops=conv_flops, name="conv", mib=24,
    )
    conv_back = to_peers(conv_y, "seq")
    conv_pre, hidden, qkv_send, rows_send = call(
        qkv_kernel,
        [
            Spill((ROWS, D), f32), Spill((ROWS, D), f32), Spill((SEQ, 192, 128), bf16, parts=3),
            Spill((ROWS, D + C_IN), bf16),
        ],
        Smem(lengths), conv_back, Hbm(projected), Hbm(conv_bias), Hbm(encoder_gain), Hbm(encoder_shift), Raw(qkv_weight),
        Hbm(query_bias),
        Hbm(value_bias), Hbm(rows_in), flops=2 * ROWS * D * 3 * D, name="qkv",
        scratch=[TRANSPOSE_SCRATCH, pltpu.VMEM((D, 3 * D), bf16), pltpu.SemaphoreType.DMA((3,))],
    )
    qkv = to_peers(qkv_send, "seq")
    rows_all = lax.all_gather(rows_send, "seq", axis=0, tiled=True).reshape(SEQ, 2, 64, D + C_IN)
    attended, logs, attended_full, qkv_kept = call(
        attend_kernel,
        [shape((1024, 128), bf16), Spill((1024, 128), f32), Spill((1024, 128), f32), Copy((SEQ, 192, 128), bf16, 1)],
        Smem(lengths), qkv, flops=8 * 1024 * 1024 * 128, name="attend", mib=32,
    )
    att_recv = to_peers(attended.reshape(SEQ, 64, 128), "seq")
    activations, grad_att_send, gmi, pair_send, pair_own, small_a = call(
        middle_kernel,
        [
            Spill((ROWS, D), bf16), Spill((SEQ, 64, 128), bf16), Spill((ROWS, D), f32),
            shape((ROWS, S_END), bf16), shape((ROWS, O_END), bf16), Spill((16, D), f32),
        ],
        Smem(skip_flag), att_recv, Hbm(hidden), Hbm(cot), Raw(output_weight), Hbm(output_bias), Hbm(middle_gain),
        Hbm(middle_shift), Raw(inner_weight), Hbm(inner_bias), Raw(outer_weight), Hbm(outer_bias), Hbm(final_gain),
        Hbm(final_shift),
        scratch=[
            pltpu.VMEM((ROWS, FF), bf16), pltpu.VMEM((ROWS, FF), f32), pltpu.VMEM((D, D), bf16),
            pltpu.VMEM((D, FF), bf16), pltpu.VMEM((FF, D), bf16), pltpu.VMEM((8, FF), f32), pltpu.VMEM((ROWS, D), f32),
            pltpu.SemaphoreType.DMA((9,)),
        ],
        flops=2 * ROWS * (4 * D * FF + 2 * D * D), name="middle", mib=32,
    )
    swap = [(i, i ^ 1) for i in range(8)]
    pair_got = lax.ppermute(pair_send, "batch", swap)
    grad_att = to_peers(grad_att_send, "seq").reshape(1024, 128)
    (dense,) = call(
        dense_grads_kernel, [Spill((SEQ, 4 * CHUNK, D), bf16, parts=4)], pair_own, pair_send, pair_got,
        flops=2 * 256 * D * 3456, name="dense_grads", mib=24,
    )
    dense, grad_att = lax.optimization_barrier((dense, grad_att))
    dense_part = lax.psum_scatter(dense.reshape(SEQ * 4 * CHUNK, D), "seq", scatter_dimension=0, tiled=True)

    (grad_qkv_send,) = call(
        attend_back_kernel, [Spill((SEQ, 192, 128), bf16)], Smem(lengths), Hbm(qkv_kept), grad_att, Hbm(logs), Hbm(attended_full),
        scratch=[pltpu.VMEM((1024, 128), f32)] * 2 + [pltpu.VMEM((128, Q_BLOCK), f32)], flops=20 * 1024 * 1024 * 128,
        name="attend_back",
    )
    grad_qkv = to_peers(grad_qkv_send, "seq")
    (qkv_rows,) = call(
        head_grads_kernel, [Spill((1024, 384), bf16)], Raw(rows_all), Hbm(grad_qkv_send),
        scratch=[pltpu.VMEM((SEQ, 64, D), bf16), pltpu.SemaphoreType.DMA((1,))], flops=4 * 1024 * D * 384,
        name="head_grads", mib=24,
    )
    frames_normed, frames_high, frames_low = call(
        frames_kernel, [Spill((2048, C_IN), bf16) for _ in range(3)], Raw(rows_all), Hbm(input_gain), Hbm(input_shift),
        scratch=[pltpu.VMEM((SEQ, 2, 64, C_IN), bf16), pltpu.SemaphoreType.DMA((1,))], name="frames", mib=32,
    )
    gmi, qkv_rows, frames_normed = lax.optimization_barrier((gmi, qkv_rows, frames_normed))
    back_send, small_b = call(
        qkv_back_kernel, [shape((SEQ, 32, SW), bf16), Spill((8, D), f32)],
        Smem(lengths), grad_qkv, Hbm(gmi), Hbm(conv_pre), Hbm(projected), Hbm(encoder_gain), Hbm(qkv_weight),
        scratch=[TRANSPOSE_SCRATCH], flops=2 * ROWS * D * 3 * D, name="qkv_back",
    )
    back_got = to_peers(back_send, "seq")
    back_other = lax.ppermute(back_got, "batch", swap)
    x_other = lax.ppermute(conv_x, "batch", swap)
    (grad_proj,) = call(
        conv_back_kernel, [shape((SEQ, 16, SW), bf16)], Smem(lengths), Hbm(back_got), Hbm(taps),
        scratch=[pltpu.VMEM((BAND, SW), bf16), shifted], flops=conv_flops, name="conv_back", mib=24,
    )
    grad_proj_got = to_peers(grad_proj, "seq")
    (tail,) = call(
        tail_kernel, [shape((1024, 384), bf16)], Hbm(grad_proj), Hbm(small_a), Hbm(small_b),
        Hbm(proj_weight), Hbm(frames_high), Hbm(frames_low), Hbm(frames_normed), Hbm(qkv_rows),
        scratch=[pltpu.VMEM((2048, 128), f32), pltpu.VMEM((3072, 128), f32), pltpu.VMEM((C_IN, 128), f32)],
        flops=6 * 2048 * C_IN * 128, name="tail", mib=32,
    )
    x_other, _ = lax.optimization_barrier((x_other, tail))
    tap_chunks = call(
        conv_weight_kernel, [Spill((GW, D), bf16) for _ in range(4)], Hbm(back_got), Hbm(back_other), Hbm(conv_x),
        Hbm(x_other),
        scratch=[
            pltpu.VMEM((192, BAND), f32), pltpu.VMEM((24, BAND), f32), pltpu.VMEM((192, 128), f32),
            pltpu.VMEM((4, GW, D), bf16), pltpu.VMEM((2, 2, 144, SW), f32),
        ],
        flops=conv_flops, name="conv_grads", mib=32,
    )
    tail, grad_proj_got, *tap_chunks = lax.optimization_barrier((tail, grad_proj_got, *tap_chunks))
    tap_got = []
    for k, piece in enumerate(tap_chunks):
        moves = [
            (b * 16 + g, (g // 2) * 16 + 8 * (g % 2) + 2 * ((b // 2 + k) % 4) + b % 2)
            for b in range(8)
            for g in range(GROUPS)
        ]
        tap_got.append(lax.ppermute(piece, ("batch", "seq"), moves))
    tail_got = to_peers(tail, ("batch", "seq"))
    (tap_own,) = call(conv_sum_kernel, [shape((GW, D), f32)], *[Hbm(x) for x in tap_got], name="conv_sum")
    grad_conv_weight = tap_own.reshape(6, KW, GW).transpose(0, 2, 1)
    dense_own = lax.psum_scatter(dense_part, "batch", scatter_dimension=0, tiled=True, axis_index_groups=Y_GROUPS)
    (grad_feats,) = call(
        feats_back_kernel, [shape((ROWS, C_IN), f32)], grad_proj_got, Hbm(rows_in), Hbm(input_gain), Hbm(proj_weight),
        scratch=[TRANSPOSE_SCRATCH], flops=2 * ROWS * C_IN * D, name="feats_back",
    )
    grad_inner_weight, grad_outer_weight, grad_output_weight = call(
        dense_sum_kernel, [shape((6, FF), f32), shape((24, D), f32), shape((6, D), f32)], Hbm(dense_own),
        name="dense_sum",
    )
    widths = [4, 4] + [6] * 9 + [24] + [6] * 3
    (
        grad_qkv_weight, grad_proj_weight, g_in_g, g_in_s, g_proj_b, g_conv_b, g_enc_g, g_enc_s, g_q_b, g_v_b, g_out_b, g_mid_g, g_mid_s,
        g_inner_b, g_outer_b, g_fin_g, g_fin_s,
    ) = call(
        tail_sum_kernel, [shape((6, 3 * D), f32), shape((4, D), f32)] + [shape((w,), f32) for w in widths],
        tail_got.reshape(128, 8, 384),
        name="tail_sum",
    )
    return (
        activations.reshape(2, 64, D), grad_feats.reshape(2, 64, C_IN), g_in_g, g_in_s, grad_proj_weight, g_proj_b,
        grad_conv_weight, g_conv_b, g_enc_g, g_enc_s, grad_qkv_weight, g_q_b, g_v_b, grad_output_weight, g_out_b,
        g_mid_g, g_mid_s, grad_inner_weight, g_inner_b, grad_outer_weight, g_outer_b, g_fin_g, g_fin_s,
    )


def solution(mesh):
    split = P("batch", "seq", None)
    both = ("batch", "seq")
    placed = (split, P("batch"), P("batch"), split) + (P(),) * 21
    row, matrix = P(both), P(both, None)
    return jax.shard_map(
        local,
        mesh=mesh,
        in_specs=placed,
        out_specs=(
            split, split, row, row, matrix, row, P(both, None, None), row, row, row, matrix, row, row, matrix, row,
            row, row, matrix, row, matrix, row, row, row,
        ),
        check_vma=False,
    )
```
